32 devices in a mesh: dp: 8 (over z, core), seq: 4 (over y, x).
Axes of the slice: x: 2, y: 2, z: 4, core: 2. Of those that a mesh axis runs over, the one named last changes fastest.
Arguments:
- q_pre: bfloat16 [8, 512, 16, 128], P('dp', 'seq'), may hold values from -6 to 6
- k_pre: bfloat16 [8, 512, 8, 128], P('dp', 'seq'), may hold values from -6 to 6
- values: bfloat16 [8, 512, 8, 128], P('dp', 'seq'), may hold values from -6 to 6
- grad_out: bfloat16 [8, 512, 16, 128], P('dp', 'seq'), may hold values from -6 to 6
- segment_ids: int32 [8, 512], P('dp', 'seq'), may hold values from 0 to 7, never falling along the last dimension, each value on 1 to 256 neighbouring positions
- q_gain: float32 [128], replicated, may hold values from 0.1 to 1.9
- k_gain: float32 [128], replicated, may hold values from 0.1 to 1.9
Outputs:
- grad_q: bfloat16 [8, 512, 16, 128], P('dp', 'seq')
- grad_k: bfloat16 [8, 512, 8, 128], P('dp', 'seq')
- grad_v: bfloat16 [8, 512, 8, 128], P('dp', 'seq')
- grad_q_gain: float32 [128], replicated
- grad_k_gain: float32 [128], replicated
The draws below stay inside these ranges and needn't reach their ends.
Inputs may be any that keep to these rules, and one draw needn't show every extreme that they name: `segment_ids`: along a span the ids never fall, and each id from 0 to 7 names one run of consecutive tokens.
All inputs are finite; a program needn't handle non-finite values.
Results may differ from the reference program's by a relative error of at most 0.017.
Values may be sent and summed in bfloat16 or wider, within the bound.
No kernel may reach another device: no remote copies, remote signals or barrier semaphores. Data moves between devices by JAX's collectives and lax.ppermute only.
A program may use at most 64 MiB of HBM per device.

```python
import math
import jax
import jax.numpy as jnp
import numpy as np
from jax import lax

QH = 16
KVH = 8
HD = 128
PRESCALE = 168
DOCS = 8
SPANS = 8
SEQLEN = 512


def shard_levels(key, extent, shards, smallest, high):
    def one(axis_at, blocks):
        steps = jax.random.uniform(jax.random.fold_in(jax.random.fold_in(key, 6), axis_at), (blocks,), jnp.float32, smallest / len(shards), high / len(shards))
        return jnp.repeat(jnp.exp(steps), extent[axis_at] // blocks).reshape((-1,) + (1,) * (len(extent) - axis_at - 1))

    loudness = one(*shards[0])
    for cut in shards[1:]:
        loudness = loudness * one(*cut)
    return loudness


def split_up(count, total, limit, slope):
    portions = [(1 << 20) // math.isqrt(grade ** slope) + 1 for grade in range(2, count + 1)]
    spare, holding = total - limit - (count - 1), [1] * (count - 1)
    while spare > 0:
        candidates = [i for i in range(count - 1) if holding[i] < limit]
        pool, left = sum([portions[i] for i in candidates]), spare
        for i in candidates:
            addition = min(limit - holding[i], max(1, left * portions[i] // pool), spare)
            holding[i] = holding[i] + addition
            spare = spare - addition
    return np.array([limit] + holding)


def ragged(own_key, number_of, total, reach, skew):
    if number_of == 2:
        one = jax.random.randint(own_key, (), max(1, total - reach), min(reach, total - 1) + 1)
        return jnp.stack([one, total - one])
    lengths = jnp.asarray(split_up(number_of, total, reach, skew), jnp.int32)
    couples = (number_of - 1) // 2
    source_of, sink = lengths[1:1 + 2 * couples:2], lengths[2:2 + 2 * couples:2]
    room = jnp.minimum(source_of - 1, reach - sink)
    shifted = jax.random.randint(jax.random.fold_in(own_key, 1), (couples,), 0, 1 << 20) % (room + 1)
    lengths = lengths.at[1:1 + 2 * couples:2].set(source_of - shifted).at[2:2 + 2 * couples:2].set(sink + shifted)
    return lengths[jax.random.permutation(jax.random.fold_in(own_key, 2), number_of)]


def gaussian(key, shape, scale, bound, cuts=(), kind=jnp.bfloat16):
    array = scale * jax.random.normal(key, shape, jnp.float32)
    if cuts:
        array = array * shard_levels(key, shape, cuts, -0.22, 0.18)
    return jnp.clip(array, -bound, bound).astype(kind)


def setup_inputs(seed: int = 0) -> dict:
    key_list = jax.random.split(jax.random.key(seed), 8)
    return {
        "q_pre": gaussian(key_list[0], (SPANS, SEQLEN, QH, HD), 1.0, 6.0, ((0, 8), (1, 4))),
        "k_pre": gaussian(key_list[1], (SPANS, SEQLEN, KVH, HD), 1.0, 6.0, ((0, 8), (1, 4))),
        "values": gaussian(key_list[2], (SPANS, SEQLEN, KVH, HD), 1.0, 6.0, ((0, 8), (1, 4))),
        "grad_out": gaussian(key_list[3], (SPANS, SEQLEN, QH, HD), 1.0, 6.0, ((0, 8), (1, 4))),
        "segment_ids": jax.vmap(lambda own: jnp.searchsorted(jnp.cumsum(ragged(own, DOCS, SEQLEN, SEQLEN // 2, 2)), jnp.arange(SEQLEN), side="right"))(jax.random.split(key_list[4], SPANS)).reshape((SPANS, SEQLEN)).astype(jnp.int32),
        "q_gain": jnp.clip(1.0 + 0.18 * jax.random.normal(key_list[5], (HD,), jnp.float32), 0.1, 1.9),
        "k_gain": jnp.clip(1.0 + 0.18 * jax.random.normal(key_list[6], (HD,), jnp.float32), 0.1, 1.9),
    }


norm_epsilon = 1e-06
rope_base = 1000000.0
rope_factor = 8.0

def document_positions(segments, docs):
    labels = jnp.arange(docs, dtype=jnp.int32)
    member = (segments[:, None] == labels[None, :]).astype(jnp.int32)
    counts = lax.optimization_barrier(jnp.sum(member, axis=0)).astype(jnp.int32)
    starts = (jnp.cumsum(counts) - counts).astype(jnp.int32)
    first = lax.optimization_barrier(jnp.sum(member * starts[None, :], axis=1)).astype(jnp.int32)
    return (jnp.arange(segments.shape[0], dtype=jnp.int32) - first, first)

def embed(rows, gain, positions):
    width = rows.shape[-1]
    half = width // 2
    scale = lax.rsqrt(lax.optimization_barrier(jnp.mean(rows * rows, axis=-1, keepdims=True)) + norm_epsilon)
    normed = rows * scale * gain
    freqs = rope_base ** (-(jnp.arange(half, dtype=jnp.float32) * 2.0 / width))
    angles = (positions.astype(jnp.float32) / rope_factor)[:, None] * freqs[None, :]
    cosine = jnp.cos(angles)[:, None, :]
    sine = jnp.sin(angles)[:, None, :]
    first_half = normed[..., :half]
    second_half = normed[..., half:]
    return jnp.concatenate([first_half * cosine - second_half * sine, second_half * cosine + first_half * sine], axis=-1)

def attend(queries, keys, vals, upstream, visible, score_scale):
    group_queries = jnp.transpose(queries, (1, 0, 2)).astype(jnp.float32)
    key_rows = keys.astype(jnp.float32)
    value_rows = vals.astype(jnp.float32)
    scores = score_scale * jnp.einsum('gid,jd->gij', group_queries, key_rows)
    raw = jnp.where(visible[None], jnp.exp(scores), 0.0)
    totals = lax.optimization_barrier(jnp.sum(raw, axis=-1))
    expo = lax.optimization_barrier(raw.astype(jnp.bfloat16)).astype(jnp.float32)
    outputs = jnp.einsum('gij,jd->gid', expo, value_rows) / totals[..., None]
    grads = jnp.transpose(upstream, (1, 0, 2)).astype(jnp.float32)
    delta = lax.optimization_barrier(jnp.sum(grads * outputs, axis=-1))
    logsum = jnp.log(totals)
    probs = jnp.where(visible[None], jnp.exp(scores - logsum[..., None]), 0.0)
    probs = lax.optimization_barrier(probs.astype(jnp.bfloat16)).astype(jnp.float32)
    value_grad = jnp.einsum('gij,gid->jd', probs, grads)
    prob_grads = jnp.einsum('gid,jd->gij', grads, value_rows)
    score_grads = (probs * (prob_grads - delta[..., None]) * score_scale).astype(jnp.bfloat16)
    score_grads = lax.optimization_barrier(score_grads).astype(jnp.float32)
    query_grad = jnp.einsum('gij,jd->gid', score_grads, key_rows)
    key_grad = jnp.einsum('gij,gid->jd', score_grads, group_queries)
    return (jnp.transpose(query_grad, (1, 0, 2)), key_grad, value_grad)

def reference(q_pre, k_pre, values, grad_out, segment_ids, q_gain, k_gain):
    total = q_pre.shape[1]
    heads = q_pre.shape[2]
    kv_heads = k_pre.shape[2]
    width = q_pre.shape[3]
    group = heads // kv_heads
    score_scale = float(PRESCALE) ** (-0.5)

    def one_span(inputs):
        queries, keys, vals, upstream, segments = inputs
        positions, first = document_positions(segments, DOCS)
        index = jnp.arange(total, dtype=jnp.int32)
        visible = (segments[:, None] == segments[None, :]) & (index[:, None] >= index[None, :])

        def embed_rows(rows, gain):
            return embed(rows, gain, positions)
        query_rot, query_back = jax.vjp(embed_rows, queries.astype(jnp.float32), q_gain)
        key_rot, key_back = jax.vjp(embed_rows, keys.astype(jnp.float32), k_gain)
        query_heads = query_rot.astype(jnp.bfloat16).reshape(total, kv_heads, group, width).transpose(1, 0, 2, 3)
        key_heads = key_rot.astype(jnp.bfloat16).transpose(1, 0, 2)
        value_heads = vals.transpose(1, 0, 2)
        upstream_heads = upstream.reshape(total, kv_heads, group, width).transpose(1, 0, 2, 3)

        def one_head(items):
            return attend(items[0], items[1], items[2], items[3], visible, score_scale)
        query_grad, key_grad, value_grad = lax.map(one_head, (query_heads, key_heads, value_heads, upstream_heads))
        query_grad = query_grad.transpose(1, 0, 2, 3).reshape(total, heads, width)
        key_grad = key_grad.transpose(1, 0, 2)
        query_input, query_gain_grad = query_back(query_grad)
        key_input, key_gain_grad = key_back(key_grad)
        return (query_input.astype(jnp.bfloat16), key_input.astype(jnp.bfloat16), value_grad.transpose(1, 0, 2).astype(jnp.bfloat16), query_gain_grad, key_gain_grad)
    grad_q, grad_k, grad_v, query_gains, key_gains = lax.map(one_span, (q_pre, k_pre, values, grad_out, segment_ids))
    return (grad_q, grad_k, grad_v, lax.optimization_barrier(jnp.sum(query_gains, axis=0)), lax.optimization_barrier(jnp.sum(key_gains, axis=0)))
```

```python
import functools

import jax
import jax.numpy as jnp
import numpy as np
from jax import lax
from jax.experimental import pallas as pl
from jax.experimental.pallas import tpu as pltpu
from jax.sharding import PartitionSpec as P

PRESCALE = 168
EPS = 1e-06
ROPE_BASE = 1000000.0
ROPE_FACTOR = 8.0
GROUPS = 2
NEG = -1e30
SCALE = float(PRESCALE) ** (-0.5)
LOG2E = 1.4426950408889634
VMEM_LIMIT = 48 * 1024 * 1024
NT = (((1,), (1,)), ((), ()))
TN = (((0,), (0,)), ((), ()))


def rope_tables(block, width, blocks):
    half = width // 2
    freqs = ROPE_BASE ** (-(np.arange(half, dtype=np.float64) * 2.0 / width))
    freqs = np.concatenate([freqs, freqs])
    inner = (np.arange(block) / ROPE_FACTOR)[:, None] * freqs[None, :]
    outer = (np.asarray(blocks) * block / ROPE_FACTOR)[:, None] * freqs[None, :]
    f32 = lambda x: jnp.asarray(x.astype(np.float32))
    return f32(np.stack([np.cos(inner), np.sin(inner)])), f32(np.stack([np.cos(outer), np.sin(outer)], axis=1))


def rope_of(inner_ref, outer_ref, row):
    both = outer_ref[row]
    cb, sb = both[0:1, :], both[1:2, :]
    ct, st = inner_ref[0], inner_ref[1]
    cos = ct * cb - st * sb
    sin = st * cb + ct * sb
    lane = lax.broadcasted_iota(jnp.int32, sin.shape, 1)
    return cos, jnp.where(lane < sin.shape[1] // 2, -sin, sin)


def swap_halves(x):
    return pltpu.roll(x, x.shape[1] // 2, 1)


def unrotate(y, cos, sin):
    return y * cos + swap_halves(y * sin)


def pack_kernel(kv_heads, back, axis, k_ref, v_ref, seg_ref, gain_ref, inner_ref, outer_ref, *rest):
    outs, scratch = rest[:-1], rest[-1]
    block = seg_ref.shape[1]
    per = kv_heads // len(outs)
    cos, sin = rope_of(inner_ref, outer_ref, lax.axis_index(axis) + back)
    gain = gain_ref[...]
    scratch[...] = k_ref[...].astype(jnp.float32)
    for h in range(kv_heads):
        x = scratch[pl.ds(h, block, stride=kv_heads), :]
        r = x * lax.rsqrt(jnp.mean(x * x, axis=1, keepdims=True) + EPS) * gain
        y = r * cos + swap_halves(r) * sin
        outs[h // per][pl.ds((h % per) * block, block), :] = y.astype(jnp.bfloat16)
    scratch[...] = v_ref[...].astype(jnp.float32)
    seg = jnp.broadcast_to(seg_ref[...].astype(jnp.float32) + 1.0, (16, block)).astype(jnp.bfloat16)
    for h in range(kv_heads):
        x = scratch[pl.ds(h, block, stride=kv_heads), :]
        outs[h // per][pl.ds((per + h % per) * block, block), :] = x.astype(jnp.bfloat16)
    for out in outs:
        out[pl.ds(2 * per * block, 16), :] = seg


def query_kernel(heads, back, axis, q_ref, g_ref, gain_ref, inner_ref, outer_ref, qo_ref, go_ref, scratch):
    block = q_ref.shape[0] // heads
    cos, sin = rope_of(inner_ref, outer_ref, lax.axis_index(axis) + back)
    gain = gain_ref[...]
    scratch[...] = q_ref[...].astype(jnp.float32)
    for h in range(heads):
        x = scratch[pl.ds(h, block, stride=heads), :]
        r = x * lax.rsqrt(jnp.mean(x * x, axis=1, keepdims=True) + EPS) * gain
        y = r * cos + swap_halves(r) * sin
        qo_ref[pl.ds(h * block, block), :] = y.astype(jnp.bfloat16)
    scratch[...] = g_ref[...].astype(jnp.float32)
    for h in range(heads):
        go_ref[pl.ds(h * block, block), :] = scratch[pl.ds(h, block, stride=heads), :].astype(jnp.bfloat16)


def attend_kernel(per, group, back, q_ref, g_ref, *rest):
    blocks = rest[: back + 1]
    dq_ref, own_ref = rest[back + 1 : back + 3]
    part_refs = rest[back + 3 : 2 * back + 3]
    bias_ref = rest[-1]
    block = own_ref.shape[0] // (2 * per)
    rows = group * block
    ids = blocks[0][pl.ds(2 * per * block, 16), :].astype(jnp.float32)[0:1, :]
    ids = jnp.concatenate([ids] * group, axis=1)
    for d in range(back + 1):
        key_row = blocks[d][pl.ds(2 * per * block, 16), :].astype(jnp.float32)[0:1, :]
        key_ids = jnp.broadcast_to(key_row, (block, block)).T
        key_ids = jnp.concatenate([key_ids] * group, axis=1)
        seen = key_ids == ids
        if d == 0:
            key_at = lax.broadcasted_iota(jnp.int32, (block, rows), 0)
            query_at = lax.broadcasted_iota(jnp.int32, (block, rows), 1) & (block - 1)
            seen = seen & (key_at <= query_at)
        bias_ref[pl.ds(d * block, block), :] = jnp.where(seen, 0.0, NEG)
    for h in range(per):
        q = q_ref[pl.ds(h * rows, rows), :]
        g = g_ref[pl.ds(h * rows, rows), :]
        k = jnp.concatenate([b[pl.ds(h * block, block), :] for b in blocks], axis=0)
        v = jnp.concatenate([b[pl.ds((per + h) * block, block), :] for b in blocks], axis=0)
        scores = lax.dot_general(k, q, NT, preferred_element_type=jnp.float32)
        expo = jnp.exp2(scores * (SCALE * LOG2E) + bias_ref[...])
        prob_grads = lax.dot_general(v, g, NT, preferred_element_type=jnp.float32)
        inverse = 1.0 / jnp.sum(expo, axis=0, keepdims=True)
        delta = jnp.sum(expo * prob_grads, axis=0, keepdims=True) * inverse
        probs = expo * inverse
        score_grads = (probs * (prob_grads - delta)).astype(jnp.bfloat16)
        dv = jnp.dot(probs.astype(jnp.bfloat16), g, preferred_element_type=jnp.float32)
        dk = jnp.dot(score_grads, q, preferred_element_type=jnp.float32) * SCALE
        dq = lax.dot_general(score_grads, k, TN, preferred_element_type=jnp.float32) * SCALE
        dq_ref[pl.ds(h * rows, rows), :] = dq
        own_ref[pl.ds(h * block, block), :] = dk[:block]
        own_ref[pl.ds((per + h) * block, block), :] = dv[:block]
        for d in range(1, back + 1):
            part = part_refs[d - 1]
            part[pl.ds(h * block, block), :] = dk[d * block : (d + 1) * block].astype(jnp.bfloat16)
            part[pl.ds((per + h) * block, block), :] = dv[d * block : (d + 1) * block].astype(jnp.bfloat16)


def query_back_kernel(heads, kv_heads, groups, back, axis, *rest):
    q_ref, qgain_ref, kgain_ref, inner_ref, outer_ref = rest[:5]
    rest = rest[5:]
    dq_refs, own_refs = rest[:groups], rest[groups : 2 * groups]
    msg_refs = rest[2 * groups : (3 + back) * groups]
    part_refs = rest[(3 + back) * groups : (3 + 2 * back) * groups]
    gq_ref, gains_ref, scratch = rest[-3:]
    block = q_ref.shape[0] // heads
    width = q_ref.shape[1]
    per = kv_heads // groups
    here = lax.axis_index(axis) + back
    total = jnp.zeros((block, width), jnp.float32)
    for d in range(back + 1):
        cos, sin = rope_of(inner_ref, outer_ref, here - d)
        for g in range(groups):
            for h in range(per):
                at = pl.ds(h * block, block)
                dk = own_refs[g][at, :] if d == 0 else part_refs[g * back + d - 1][at, :].astype(jnp.float32)
                k = msg_refs[g * (back + 1) + d][at, :].astype(jnp.float32)
                total = total + unrotate(dk, cos, sin) * unrotate(k, cos, sin)
    kgain = jnp.sum(total, axis=0, keepdims=True) / kgain_ref[...]
    cos, sin = rope_of(inner_ref, outer_ref, here)
    scratch[...] = q_ref[...].astype(jnp.float32)
    gain = qgain_ref[...]
    total = jnp.zeros((block, width), jnp.float32)
    each = heads // groups
    for h in range(heads):
        x = scratch[pl.ds(h, block, stride=heads), :]
        scale = lax.rsqrt(jnp.mean(x * x, axis=1, keepdims=True) + EPS)
        normed = x * scale
        dr = unrotate(dq_refs[h // each][pl.ds((h % each) * block, block), :], cos, sin)
        total = total + dr * normed
        dn = dr * gain
        dx = scale * (dn - normed * jnp.mean(dn * normed, axis=1, keepdims=True))
        scratch[pl.ds(h, block, stride=heads), :] = dx
    gq_ref[...] = scratch[...].astype(jnp.bfloat16)
    qgain = jnp.sum(total, axis=0, keepdims=True)
    gains_ref[...] = jnp.concatenate([qgain, kgain, jnp.zeros((6, width), jnp.float32)], axis=0)


def key_back_kernel(kv_heads, groups, back, axis, *rest):
    k_ref, gain_ref, inner_ref, outer_ref = rest[:4]
    own_refs = rest[4 : 4 + groups]
    got_refs = rest[4 + groups : 4 + (1 + back) * groups]
    gk_ref, gv_ref, scratch = rest[-3:]
    block = k_ref.shape[0] // kv_heads
    per = kv_heads // groups
    cos, sin = rope_of(inner_ref, outer_ref, lax.axis_index(axis) + back)
    gain = gain_ref[...]

    def total(g, row):
        at = pl.ds(row * block, block)
        value = own_refs[g][at, :]
        for d in range(back):
            value = value + got_refs[g * back + d][at, :].astype(jnp.float32)
        return value

    scratch[...] = k_ref[...].astype(jnp.float32)
    for h in range(kv_heads):
        x = scratch[pl.ds(h, block, stride=kv_heads), :]
        scale = lax.rsqrt(jnp.mean(x * x, axis=1, keepdims=True) + EPS)
        normed = x * scale
        dn = unrotate(total(h // per, h % per), cos, sin) * gain
        dx = scale * (dn - normed * jnp.mean(dn * normed, axis=1, keepdims=True))
        scratch[pl.ds(h, block, stride=kv_heads), :] = dx
    gk_ref[...] = scratch[...].astype(jnp.bfloat16)
    for h in range(kv_heads):
        scratch[pl.ds(h, block, stride=kv_heads), :] = total(h // per, per + h % per)
    gv_ref[...] = scratch[...].astype(jnp.bfloat16)


def call(kernel, outs, scratch, cost, *args):
    vmem = pl.BlockSpec(memory_space=pltpu.VMEM)
    return pl.pallas_call(
        kernel,
        out_shape=[jax.ShapeDtypeStruct(s, t) for s, t in outs],
        in_specs=[vmem] * len(args),
        out_specs=[vmem] * len(outs),
        scratch_shapes=[pltpu.VMEM(s, jnp.float32) for s in scratch],
        compiler_params=pltpu.CompilerParams(vmem_limit_bytes=VMEM_LIMIT),
        cost_estimate=pl.CostEstimate(flops=cost, bytes_accessed=1 << 20, transcendentals=0),
    )(*args)


def sum_over(x, axis, size):
    if size & (size - 1):
        return lax.psum(x, axis)
    step = 1
    while step < size:
        x = x + lax.ppermute(x, axis, [(i, i ^ step) for i in range(size)])
        step *= 2
    return x


def body(spans, parts, q_pre, k_pre, values, grad_out, segment_ids, q_gain, k_gain):
    block, heads, width = q_pre.shape[1:]
    kv_heads = k_pre.shape[2]
    group = heads // kv_heads
    groups = GROUPS
    per = kv_heads // groups
    longest = parts * block // 2
    back = min(parts - 1, (longest - 2) // block + 1)
    bf16, f32 = jnp.bfloat16, jnp.float32
    inner, outer = rope_tables(block, width, range(-back, parts))
    q2, g2 = (x.reshape(block * heads, width) for x in (q_pre, grad_out))
    k2, v2 = (x.reshape(block * kv_heads, width) for x in (k_pre, values))
    qg, kg = q_gain.reshape(1, width), k_gain.reshape(1, width)

    message = (2 * per * block + 16, width)
    own = call(
        functools.partial(pack_kernel, kv_heads, back, "seq"),
        [(message, bf16)] * groups, [(block * kv_heads, width)], 1 << 28,
        k2, v2, segment_ids, kg, inner, outer,
    )
    window = [
        [own[g]] + [lax.ppermute(own[g], "seq", [(i, i + d) for i in range(parts - d)]) for d in range(1, back + 1)]
        for g in range(groups)
    ]
    q_rot, g_rot = call(
        functools.partial(query_kernel, heads, back, "seq"),
        [((heads * block, width), bf16)] * 2, [(heads * block, width)], 1 << 29,
        q2, g2, qg, inner, outer,
    )
    dqs, owns, shares, returned = [], [], [], []
    rows = group * block * per
    for g in range(groups):
        dq, kept, *share = call(
            functools.partial(attend_kernel, per, group, back),
            [((rows, width), f32), ((2 * per * block, width), f32)] + [((2 * per * block, width), bf16)] * back,
            [((back + 1) * block, group * block)], 1 << 30,
            lax.slice_in_dim(q_rot, g * rows, (g + 1) * rows), lax.slice_in_dim(g_rot, g * rows, (g + 1) * rows),
            *window[g],
        )
        dqs.append(dq)
        owns.append(kept)
        shares += share
        returned += [
            lax.ppermute(share[d - 1], "seq", [(i + d, i) for i in range(parts - d)]) for d in range(1, back + 1)
        ]
    grad_q, gains = call(
        functools.partial(query_back_kernel, heads, kv_heads, groups, back, "seq"),
        [((heads * block, width), bf16), ((8, width), f32)], [(heads * block, width)], 1 << 29,
        q2, qg, kg, inner, outer, *dqs, *owns, *[m for w in window for m in w], *shares,
    )
    gains = sum_over(sum_over(gains, "seq", parts), "dp", spans)
    grad_k, grad_v = call(
        functools.partial(key_back_kernel, kv_heads, groups, back, "seq"),
        [((kv_heads * block, width), bf16)] * 2, [(kv_heads * block, width)], 1 << 28,
        k2, kg, inner, outer, *owns, *returned,
    )
    return (
        grad_q.reshape(q_pre.shape),
        grad_k.reshape(k_pre.shape),
        grad_v.reshape(values.shape),
        gains[0],
        gains[1],
    )


def solution(mesh):
    tokens = P("dp", "seq", None, None)
    return jax.shard_map(
        functools.partial(body, mesh.shape["dp"], mesh.shape["seq"]),
        mesh=mesh,
        in_specs=(tokens, tokens, tokens, tokens, P("dp", "seq"), P(), P()),
        out_specs=(tokens, tokens, tokens, P(), P()),
        check_vma=False,
    )
```

```python
import functools

import jax
import jax.numpy as jnp
import numpy as np
from jax import lax
from jax.experimental import pallas as pl
from jax.experimental.pallas import tpu as pltpu
from jax.sharding import PartitionSpec as P

PRESCALE = 168
EPS = 1e-06
ROPE_BASE = 1000000.0
ROPE_FACTOR = 8.0
GROUPS = 2
NEG = -1e30
SCALE = float(PRESCALE) ** (-0.5)
LOG2E = 1.4426950408889634
VMEM_LIMIT = 48 * 1024 * 1024
NT = (((1,), (1,)), ((), ()))
TN = (((0,), (0,)), ((), ()))


def rope_tables(block, width, blocks):
    half = width // 2
    freqs = ROPE_BASE ** (-(np.arange(half, dtype=np.float64) * 2.0 / width))
    freqs = np.concatenate([freqs, freqs])
    inner = (np.arange(block) / ROPE_FACTOR)[:, None] * freqs[None, :]
    outer = (np.asarray(blocks) * block / ROPE_FACTOR)[:, None] * freqs[None, :]
    f32 = lambda x: jnp.asarray(x.astype(np.float32))
    return f32(np.stack([np.cos(inner), np.sin(inner)])), f32(np.stack([np.cos(outer), np.sin(outer)], axis=1))


def rope_of(inner_ref, outer_ref, row):
    both = outer_ref[row]
    cb, sb = both[0:1, :], both[1:2, :]
    ct, st = inner_ref[0], inner_ref[1]
    cos = ct * cb - st * sb
    sin = st * cb + ct * sb
    lane = lax.broadcasted_iota(jnp.int32, sin.shape, 1)
    return cos, jnp.where(lane < sin.shape[1] // 2, -sin, sin)


def swap_halves(x):
    return pltpu.roll(x, x.shape[1] // 2, 1)


def unrotate(y, cos, sin):
    return y * cos + swap_halves(y * sin)


def pack_kernel(kv_heads, back, axis, k_ref, v_ref, seg_ref, gain_ref, inner_ref, outer_ref, *rest):
    outs, scratch = rest[:-1], rest[-1]
    block = seg_ref.shape[1]
    per = kv_heads // len(outs)
    cos, sin = rope_of(inner_ref, outer_ref, lax.axis_index(axis) + back)
    gain = gain_ref[...]
    scratch[...] = k_ref[...].astype(jnp.float32)
    for h in range(kv_heads):
        x = scratch[pl.ds(h, block, stride=kv_heads), :]
        r = x * lax.rsqrt(jnp.mean(x * x, axis=1, keepdims=True) + EPS) * gain
        y = r * cos + swap_halves(r) * sin
        outs[h // per][pl.ds((h % per) * block, block), :] = y.astype(jnp.bfloat16)
    scratch[...] = v_ref[...].astype(jnp.float32)
    seg = jnp.broadcast_to(seg_ref[...].astype(jnp.float32) + 1.0, (16, block)).astype(jnp.bfloat16)
    for h in range(kv_heads):
        x = scratch[pl.ds(h, block, stride=kv_heads), :]
        outs[h // per][pl.ds((per + h % per) * block, block), :] = x.astype(jnp.bfloat16)
    for out in outs:
        out[pl.ds(2 * per * block, 16), :] = seg


def query_kernel(heads, back, axis, q_ref, g_ref, gain_ref, inner_ref, outer_ref, qo_ref, go_ref, scratch):
    block = q_ref.shape[0] // heads
    cos, sin = rope_of(inner_ref, outer_ref, lax.axis_index(axis) + back)
    gain = gain_ref[...]
    scratch[...] = q_ref[...].astype(jnp.float32)
    for h in range(heads):
        x = scratch[pl.ds(h, block, stride=heads), :]
        r = x * lax.rsqrt(jnp.mean(x * x, axis=1, keepdims=True) + EPS) * gain
        y = r * cos + swap_halves(r) * sin
        qo_ref[pl.ds(h * block, block), :] = y.astype(jnp.bfloat16)
    scratch[...] = g_ref[...].astype(jnp.float32)
    for h in range(heads):
        go_ref[pl.ds(h * block, block), :] = scratch[pl.ds(h, block, stride=heads), :].astype(jnp.bfloat16)


def attend_kernel(per, group, back, q_ref, g_ref, *rest):
    blocks = rest[: back + 1]
    dq_ref, own_ref = rest[back + 1 : back + 3]
    part_refs = rest[back + 3 : 2 * back + 3]
    bias_ref = rest[-1]
    block = own_ref.shape[0] // (2 * per)
    rows = group * block
    ids = blocks[0][pl.ds(2 * per * block, 16), :].astype(jnp.float32)[0:1, :]
    ids = jnp.concatenate([ids] * group, axis=1)
    for d in range(back + 1):
        key_row = blocks[d][pl.ds(2 * per * block, 16), :].astype(jnp.float32)[0:1, :]
        key_ids = jnp.broadcast_to(key_row, (block, block)).T
        key_ids = jnp.concatenate([key_ids] * group, axis=1)
        seen = key_ids == ids
        if d == 0:
            key_at = lax.broadcasted_iota(jnp.int32, (block, rows), 0)
            query_at = lax.broadcasted_iota(jnp.int32, (block, rows), 1) & (block - 1)
            seen = seen & (key_at <= query_at)
        bias_ref[pl.ds(d * block, block), :] = jnp.where(seen, 0.0, NEG)
    for h in range(per):
        q = q_ref[pl.ds(h * rows, rows), :]
        g = g_ref[pl.ds(h * rows, rows), :]
        k = jnp.concatenate([b[pl.ds(h * block, block), :] for b in blocks], axis=0)
        v = jnp.concatenate([b[pl.ds((per + h) * block, block), :] for b in blocks], axis=0)
        scores = lax.dot_general(k, q, NT, preferred_element_type=jnp.float32)
        expo = jnp.exp2(scores * (SCALE * LOG2E) + bias_ref[...])
        prob_grads = lax.dot_general(v, g, NT, preferred_element_type=jnp.float32)
        inverse = 1.0 / jnp.sum(expo, axis=0, keepdims=True)
        delta = jnp.sum(expo * prob_grads, axis=0, keepdims=True) * inverse
        probs = expo * inverse
        score_grads = (probs * (prob_grads - delta)).astype(jnp.bfloat16)
        dv = jnp.dot(probs.astype(jnp.bfloat16), g, preferred_element_type=jnp.float32)
        dk = jnp.dot(score_grads, q, preferred_element_type=jnp.float32) * SCALE
        dq = lax.dot_general(score_grads, k, TN, preferred_element_type=jnp.float32) * SCALE
        dq_ref[pl.ds(h * rows, rows), :] = dq
        own_ref[pl.ds(h * block, block), :] = dk[:block]
        own_ref[pl.ds((per + h) * block, block), :] = dv[:block]
        for d in range(1, back + 1):
            part = part_refs[d - 1]
            part[pl.ds(h * block, block), :] = dk[d * block : (d + 1) * block].astype(jnp.bfloat16)
            part[pl.ds((per + h) * block, block), :] = dv[d * block : (d + 1) * block].astype(jnp.bfloat16)


def query_back_kernel(heads, kv_heads, groups, back, axis, *rest):
    q_ref, qgain_ref, kgain_ref, inner_ref, outer_ref = rest[:5]
    rest = rest[5:]
    dq_refs, own_refs = rest[:groups], rest[groups : 2 * groups]
    msg_refs = rest[2 * groups : (3 + back) * groups]
    part_refs = rest[(3 + back) * groups : (3 + 2 * back) * groups]
    gq_ref, gains_ref, scratch = rest[-3:]
    block = q_ref.shape[0] // heads
    width = q_ref.shape[1]
    per = kv_heads // groups
    here = lax.axis_index(axis) + back
    total = jnp.zeros((block, width), jnp.float32)
    for d in range(back + 1):
        cos, sin = rope_of(inner_ref, outer_ref, here - d)
        for g in range(groups):
            for h in range(per):
                at = pl.ds(h * block, block)
                dk = own_refs[g][at, :] if d == 0 else part_refs[g * back + d - 1][at, :].astype(jnp.float32)
                k = msg_refs[g * (back + 1) + d][at, :].astype(jnp.float32)
                total = total + unrotate(dk, cos, sin) * unrotate(k, cos, sin)
    kgain = jnp.sum(total, axis=0, keepdims=True) / kgain_ref[...]
    cos, sin = rope_of(inner_ref, outer_ref, here)
    scratch[...] = q_ref[...].astype(jnp.float32)
    gain = qgain_ref[...]
    total = jnp.zeros((block, width), jnp.float32)
    each = heads // groups
    for h in range(heads):
        x = scratch[pl.ds(h, block, stride=heads), :]
        scale = lax.rsqrt(jnp.mean(x * x, axis=1, keepdims=True) + EPS)
        normed = x * scale
        dr = unrotate(dq_refs[h // each][pl.ds((h % each) * block, block), :], cos, sin)
        total = total + dr * normed
        dn = dr * gain
        dx = scale * (dn - normed * jnp.mean(dn * normed, axis=1, keepdims=True))
        scratch[pl.ds(h, block, stride=heads), :] = dx
    gq_ref[...] = scratch[...].astype(jnp.bfloat16)
    qgain = jnp.sum(total, axis=0, keepdims=True)
    gains_ref[...] = jnp.concatenate([qgain, kgain, jnp.zeros((6, width), jnp.float32)], axis=0)


def key_back_kernel(kv_heads, groups, back, axis, *rest):
    k_ref, gain_ref, inner_ref, outer_ref = rest[:4]
    own_refs = rest[4 : 4 + groups]
    got_refs = rest[4 + groups : 4 + (1 + back) * groups]
    gk_ref, gv_ref, scratch = rest[-3:]
    block = k_ref.shape[0] // kv_heads
    per = kv_heads // groups
    cos, sin = rope_of(inner_ref, outer_ref, lax.axis_index(axis) + back)
    gain = gain_ref[...]

    def total(g, row):
        at = pl.ds(row * block, block)
        value = own_refs[g][at, :]
        for d in range(back):
            value = value + got_refs[g * back + d][at, :].astype(jnp.float32)
        return value

    scratch[...] = k_ref[...].astype(jnp.float32)
    for h in range(kv_heads):
        x = scratch[pl.ds(h, block, stride=kv_heads), :]
        scale = lax.rsqrt(jnp.mean(x * x, axis=1, keepdims=True) + EPS)
        normed = x * scale
        dn = unrotate(total(h // per, h % per), cos, sin) * gain
        dx = scale * (dn - normed * jnp.mean(dn * normed, axis=1, keepdims=True))
        scratch[pl.ds(h, block, stride=kv_heads), :] = dx
    gk_ref[...] = scratch[...].astype(jnp.bfloat16)
    for h in range(kv_heads):
        scratch[pl.ds(h, block, stride=kv_heads), :] = total(h // per, per + h % per)
    gv_ref[...] = scratch[...].astype(jnp.bfloat16)


def call(kernel, outs, scratch, cost, *args):
    vmem = pl.BlockSpec(memory_space=pltpu.VMEM)
    return pl.pallas_call(
        kernel,
        out_shape=[jax.ShapeDtypeStruct(s, t) for s, t in outs],
        in_specs=[vmem] * len(args),
        out_specs=[vmem] * len(outs),
        scratch_shapes=[pltpu.VMEM(s, jnp.float32) for s in scratch],
        compiler_params=pltpu.CompilerParams(vmem_limit_bytes=VMEM_LIMIT),
        cost_estimate=pl.CostEstimate(flops=cost, bytes_accessed=1 << 20, transcendentals=0),
    )(*args)


def sum_over(x, axis, size):
    if size & (size - 1):
        return lax.psum(x, axis)
    step = 1
    while step < size:
        x = x + lax.ppermute(x, axis, [(i, i ^ step) for i in range(size)])
        step *= 2
    return x


def by_tokens(spans, parts, q_pre, k_pre, values, grad_out, segment_ids, q_gain, k_gain):
    block, heads, width = q_pre.shape[1:]
    kv_heads = k_pre.shape[2]
    group = heads // kv_heads
    groups = GROUPS
    per = kv_heads // groups
    longest = parts * block // 2
    back = min(parts - 1, (longest - 2) // block + 1)
    bf16, f32 = jnp.bfloat16, jnp.float32
    inner, outer = rope_tables(block, width, range(-back, parts))
    q2, g2 = (x.reshape(block * heads, width) for x in (q_pre, grad_out))
    k2, v2 = (x.reshape(block * kv_heads, width) for x in (k_pre, values))
    qg, kg = q_gain.reshape(1, width), k_gain.reshape(1, width)

    message = (2 * per * block + 16, width)
    own = call(
        functools.partial(pack_kernel, kv_heads, back, "seq"),
        [(message, bf16)] * groups, [(block * kv_heads, width)], 1 << 28,
        k2, v2, segment_ids, kg, inner, outer,
    )
    window = [
        [own[g]] + [lax.ppermute(own[g], "seq", [(i, i + d) for i in range(parts - d)]) for d in range(1, back + 1)]
        for g in range(groups)
    ]
    q_rot, g_rot = call(
        functools.partial(query_kernel, heads, back, "seq"),
        [((heads * block, width), bf16)] * 2, [(heads * block, width)], 1 << 29,
        q2, g2, qg, inner, outer,
    )
    dqs, owns, shares, returned = [], [], [], []
    rows = group * block * per
    for g in range(groups):
        dq, kept, *share = call(
            functools.partial(attend_kernel, per, group, back),
            [((rows, width), f32), ((2 * per * block, width), f32)] + [((2 * per * block, width), bf16)] * back,
            [((back + 1) * block, group * block)], 1 << 30,
            lax.slice_in_dim(q_rot, g * rows, (g + 1) * rows), lax.slice_in_dim(g_rot, g * rows, (g + 1) * rows),
            *window[g],
        )
        dqs.append(dq)
        owns.append(kept)
        shares += share
        returned += [
            lax.ppermute(share[d - 1], "seq", [(i + d, i) for i in range(parts - d)]) for d in range(1, back + 1)
        ]
    grad_q, gains = call(
        functools.partial(query_back_kernel, heads, kv_heads, groups, back, "seq"),
        [((heads * block, width), bf16), ((8, width), f32)], [(heads * block, width)], 1 << 29,
        q2, qg, kg, inner, outer, *dqs, *owns, *[m for w in window for m in w], *shares,
    )
    gains = sum_over(sum_over(gains, "seq", parts), "dp", spans)
    grad_k, grad_v = call(
        functools.partial(key_back_kernel, kv_heads, groups, back, "seq"),
        [((kv_heads * block, width), bf16)] * 2, [(kv_heads * block, width)], 1 << 28,
        k2, kg, inner, outer, *owns, *returned,
    )
    return (
        grad_q.reshape(q_pre.shape),
        grad_k.reshape(k_pre.shape),
        grad_v.reshape(values.shape),
        gains[0],
        gains[1],
    )


def dma_all(pairs, sems):
    copies = [pltpu.make_async_copy(src, dst, sems.at[i]) for i, (src, dst) in enumerate(pairs)]
    for copy in copies:
        copy.start()
    return copies


def spread_kernel(axis, parts, groups, heads, kv_heads, q_hbm, g_hbm, k_hbm, v_hbm, seg_hbm, *rest):
    outs = rest[: parts * groups]
    q_in, g_in, k_in, v_in, seg_in, q_f32, g_f32, k_f32, v_f32, msg, in_sems, out_sems = rest[parts * groups :]
    block = seg_in.shape[1]
    group = heads // kv_heads
    per = kv_heads // parts // groups
    me = lax.axis_index(axis)
    loads = dma_all(
        [(k_hbm, k_in), (v_hbm, v_in), (q_hbm, q_in), (g_hbm, g_in), (seg_hbm, seg_in)], in_sems
    )
    for copy, src, dst in zip(loads, (k_in, v_in, q_in, g_in), (k_f32, v_f32, q_f32, g_f32)):
        copy.wait()
        dst[...] = src[...].astype(jnp.float32)
    loads[4].wait()
    ids = jnp.broadcast_to(seg_in[...].astype(jnp.float32), (16, block)).astype(jnp.bfloat16)
    stores = []
    for grp in range(groups):
        for part in range(parts):
            slot = grp * parts + part
            at = 0
            for p in range(per):
                kv = (part * groups + grp) * per + p
                pieces = [(q_f32, kv * group + i, heads) for i in range(group)]
                pieces += [(g_f32, kv * group + i, heads) for i in range(group)]
                pieces += [(k_f32, kv, kv_heads), (v_f32, kv, kv_heads)]
                for src, head, stride in pieces:
                    rows = src[pl.ds(head, block, stride=stride), :]
                    msg[slot, pl.ds(at, block), :] = rows.astype(jnp.bfloat16)
                    at += block
            msg[slot, pl.ds(at, 16), :] = ids
        for m in range(parts):
            i = grp * parts + m
            copy = pltpu.make_async_copy(msg.at[grp * parts + (me ^ m)], outs[i], out_sems.at[i])
            copy.start()
            stores.append(copy)
    for copy in stores:
        copy.wait()


def heads_kernel(axis, parts, per, group, back, inner_hbm, outer_hbm, gains_hbm, *rest):
    msgs, outs = rest[:parts], rest[parts : 2 * parts]
    share_ref, inner_ref, outer_ref, gains_ref, buf, res, in_sems, out_sems = rest[2 * parts :]
    block, width = inner_ref.shape[1:]
    rows = group * block
    me = lax.axis_index(axis)
    loads = dma_all(
        [(inner_hbm, inner_ref), (outer_hbm, outer_ref), (gains_hbm, gains_ref)]
        + [(msgs[m], buf.at[me ^ m]) for m in range(parts)],
        in_sems,
    )
    for copy in loads:
        copy.wait()
    q_gain, k_gain = gains_ref[0:1, :], gains_ref[1:2, :]
    f32, bf16 = jnp.float32, jnp.bfloat16
    ropes = [rope_of(inner_ref, outer_ref, b) for b in range(parts)]
    last = per * (2 * group + 2) * block
    id_rows = [buf[b, pl.ds(last, 16), :].astype(f32)[0:1, :] for b in range(parts)]
    id_columns = [jnp.broadcast_to(row, (block, block)).T for row in id_rows]
    key_at = lax.broadcasted_iota(jnp.int32, (block, block), 0)
    query_at = lax.broadcasted_iota(jnp.int32, (block, block), 1)
    causal = key_at <= query_at

    def seen(key_block, query_block):
        same = id_columns[key_block] == id_rows[query_block]
        if key_block == query_block:
            same = same & causal
        return jnp.concatenate([same.astype(f32)] * group, axis=1) > 0.5

    def embed(x, gain, rope):
        scale = lax.rsqrt(jnp.mean(x * x, axis=1, keepdims=True) + EPS)
        normed = x * scale
        r = normed * gain
        return (r * rope[0] + swap_halves(r) * rope[1]).astype(bf16), normed, scale

    def embed_back(dy, gain, rope, normed, scale):
        dr = unrotate(dy, *rope)
        dn = dr * gain
        dx = scale * (dn - normed * jnp.mean(dn * normed, axis=1, keepdims=True))
        return dx.astype(bf16), dr * normed

    q_total = jnp.zeros((block, width), f32)
    k_total = jnp.zeros((block, width), f32)
    for p in range(per):
        base = p * (2 * group + 2) * block
        out_base = p * (group + 2) * block

        def piece(b, i):
            return buf[b, pl.ds(base + i * block, block), :]

        keys = [embed(piece(b, 2 * group).astype(f32), k_gain, ropes[b]) for b in range(parts)]
        dk = [jnp.zeros((block, width), f32)] * parts
        dv = [jnp.zeros((block, width), f32)] * parts
        for b in range(parts):
            first = max(0, b - back)
            queries = [embed(piece(b, i).astype(f32), q_gain, ropes[b]) for i in range(group)]
            q = jnp.concatenate([x[0] for x in queries], axis=0)
            g = buf[b, pl.ds(base + rows, rows), :]
            k = jnp.concatenate([keys[j][0] for j in range(first, b + 1)], axis=0)
            v = jnp.concatenate([piece(j, 2 * group + 1) for j in range(first, b + 1)], axis=0)
            mask = jnp.concatenate([seen(j, b) for j in range(first, b + 1)], axis=0)
            scores = lax.dot_general(k, q, NT, preferred_element_type=f32)
            expo = jnp.where(mask, jnp.exp2(scores * (SCALE * LOG2E)), 0.0)
            prob_grads = lax.dot_general(v, g, NT, preferred_element_type=f32)
            inverse = 1.0 / jnp.sum(expo, axis=0, keepdims=True)
            delta = jnp.sum(expo * prob_grads, axis=0, keepdims=True) * inverse
            probs = expo * inverse
            score_grads = (probs * (prob_grads - delta)).astype(bf16)
            dvs = jnp.dot(probs.astype(bf16), g, preferred_element_type=f32)
            dks = jnp.dot(score_grads, q, preferred_element_type=f32)
            dq = lax.dot_general(score_grads, k, TN, preferred_element_type=f32) * SCALE
            for i in range(group):
                dx, share = embed_back(dq[i * block : (i + 1) * block], q_gain, ropes[b], *queries[i][1:])
                res[b, pl.ds(out_base + i * block, block), :] = dx
                q_total = q_total + share
            for j in range(first, b + 1):
                at = slice((j - first) * block, (j - first + 1) * block)
                dk[j] = dk[j] + dks[at]
                dv[j] = dv[j] + dvs[at]
        for b in range(parts):
            dx, share = embed_back(dk[b] * SCALE, k_gain, ropes[b], *keys[b][1:])
            res[b, pl.ds(out_base + rows, block), :] = dx
            res[b, pl.ds(out_base + rows + block, block), :] = dv[b].astype(bf16)
            k_total = k_total + share
    stores = [pltpu.make_async_copy(res.at[me ^ m], outs[m], out_sems.at[m]) for m in range(parts)]
    for copy in stores:
        copy.start()
    share_ref[...] = jnp.concatenate(
        [
            jnp.sum(q_total, axis=0, keepdims=True),
            jnp.sum(k_total, axis=0, keepdims=True),
            jnp.zeros((6, width), f32),
        ],
        axis=0,
    )
    for copy in stores:
        copy.wait()


def collect_kernel(axis, parts, groups, heads, kv_heads, *rest):
    msgs = rest[: parts * groups]
    gq_hbm, gk_hbm, gv_hbm, buf, q_f32, k_f32, v_f32, q_out, k_out, v_out, in_sems, out_sems = rest[parts * groups :]
    group = heads // kv_heads
    per = kv_heads // parts // groups
    block = q_out.shape[0] // heads
    me = lax.axis_index(axis)
    loads = dma_all(
        [
            (msgs[grp * parts + m], buf.at[grp * parts + (me ^ m)])
            for grp in range(groups)
            for m in range(parts)
        ],
        in_sems,
    )
    for copy in loads:
        copy.wait()
    for grp in range(groups):
        for part in range(parts):
            at = 0
            for p in range(per):
                kv = (part * groups + grp) * per + p
                pieces = [(q_f32, kv * group + i, heads) for i in range(group)]
                pieces += [(k_f32, kv, kv_heads), (v_f32, kv, kv_heads)]
                for dst, head, stride in pieces:
                    rows = buf[grp * parts + part, pl.ds(at, block), :].astype(jnp.float32)
                    dst[pl.ds(head, block, stride=stride), :] = rows
                    at += block
    stores = []
    for i, (src, out, dst) in enumerate(((q_f32, q_out, gq_hbm), (k_f32, k_out, gk_hbm), (v_f32, v_out, gv_hbm))):
        out[...] = src[...].astype(jnp.bfloat16)
        copy = pltpu.make_async_copy(out, dst, out_sems.at[i])
        copy.start()
        stores.append(copy)
    for copy in stores:
        copy.wait()


def call_any(kernel, outs, scratch, cost, *args):
    return pl.pallas_call(
        kernel,
        out_shape=[jax.ShapeDtypeStruct(s, t) for s, t, _ in outs],
        in_specs=[pl.BlockSpec(memory_space=pl.ANY)] * len(args),
        out_specs=[pl.BlockSpec(memory_space=m) for _, _, m in outs],
        scratch_shapes=scratch,
        compiler_params=pltpu.CompilerParams(vmem_limit_bytes=VMEM_LIMIT),
        cost_estimate=pl.CostEstimate(flops=cost, bytes_accessed=1 << 20, transcendentals=0),
    )(*args)


def exchange_sum(x, axis, size, *partners):
    got = [lax.ppermute(x, axis, [(i, i ^ m) for i in range(size)]) for m in partners]
    return x + got[0] if len(got) == 1 else (x + got[0]) + (got[1] + got[2])


def by_heads(spans, parts, q_pre, k_pre, values, grad_out, segment_ids, q_gain, k_gain):
    block, heads, width = q_pre.shape[1:]
    kv_heads = k_pre.shape[2]
    group = heads // kv_heads
    groups = min(GROUPS, kv_heads // parts)
    per = kv_heads // parts // groups
    longest = parts * block // 2
    back = min(parts - 1, (longest - 2) // block + 1)
    bf16, f32, vmem = jnp.bfloat16, jnp.float32, pltpu.VMEM
    inner, outer = rope_tables(block, width, range(parts))
    q2, g2 = (x.reshape(block * heads, width) for x in (q_pre, grad_out))
    k2, v2 = (x.reshape(block * kv_heads, width) for x in (k_pre, values))
    sent = (per * (2 * group + 2) * block + 16, width)
    back_sent = (per * (group + 2) * block, width)
    dma = pltpu.SemaphoreType.DMA
    q_shape, k_shape = q2.shape, k2.shape

    messages = call_any(
        functools.partial(spread_kernel, "seq", parts, groups, heads, kv_heads),
        [(sent, bf16, pl.ANY)] * (parts * groups),
        [vmem(q_shape, bf16), vmem(q_shape, bf16), vmem(k_shape, bf16), vmem(k_shape, bf16), vmem((1, block), jnp.int32)]
        + [vmem(q_shape, f32), vmem(q_shape, f32), vmem(k_shape, f32), vmem(k_shape, f32)]
        + [vmem((parts * groups, *sent), bf16), dma((5,)), dma((parts * groups,))],
        1 << 20, q2, g2, k2, v2, segment_ids,
    )
    gains = jnp.concatenate([q_gain[None], k_gain[None], jnp.zeros((6, width), f32)], axis=0)
    xor = lambda m, size: [(i, i ^ m) for i in range(size)]
    arrived = [
        [messages[grp * parts]]
        + [lax.ppermute(messages[grp * parts + m], "seq", xor(m, parts)) for m in range(1, parts)]
        for grp in range(groups)
    ]
    returned, shares = [], []
    for grp in range(groups):
        *results, share = call_any(
            functools.partial(heads_kernel, "seq", parts, per, group, back),
            [(back_sent, bf16, pl.ANY)] * parts + [((8, width), f32, vmem)],
            [vmem(inner.shape, f32), vmem(outer.shape, f32), vmem(gains.shape, f32)]
            + [vmem((parts, *sent), bf16), vmem((parts, *back_sent), bf16), dma((3 + parts,)), dma((parts,))],
            1 << 30, inner, outer, gains, *arrived[grp],
        )
        returned += [results[0]] + [lax.ppermute(results[m], "seq", xor(m, parts)) for m in range(1, parts)]
        shares.append(share)
    total = functools.reduce(jnp.add, shares)
    total = exchange_sum(total, "dp", spans, 1)
    total = exchange_sum(total, "seq", parts, 1, 2, 3)
    total = exchange_sum(total, "dp", spans, 2, 4, 6)
    grad_q, grad_k, grad_v = call_any(
        functools.partial(collect_kernel, "seq", parts, groups, heads, kv_heads),
        [(q_shape, bf16, pl.ANY), (k_shape, bf16, pl.ANY), (k_shape, bf16, pl.ANY)],
        [vmem((parts * groups, *back_sent), bf16)]
        + [vmem(q_shape, f32), vmem(k_shape, f32), vmem(k_shape, f32)]
        + [vmem(q_shape, bf16), vmem(k_shape, bf16), vmem(k_shape, bf16), dma((parts * groups,)), dma((3,))],
        1 << 20, *returned,
    )
    return (
        grad_q.reshape(q_pre.shape), grad_k.reshape(k_pre.shape), grad_v.reshape(values.shape), total[0], total[1],
    )


def solution(mesh):
    tokens = P("dp", "seq", None, None)
    spans, parts = mesh.shape["dp"], mesh.shape["seq"]
    body = by_heads if (spans, parts) == (8, 4) else by_tokens
    return jax.shard_map(
        functools.partial(body, spans, parts),
        mesh=mesh,
        in_specs=(tokens, tokens, tokens, tokens, P("dp", "seq"), P(), P()),
        out_specs=(tokens, tokens, tokens, P(), P()),
        check_vma=False,
    )
```

```python
import functools

import jax
import jax.numpy as jnp
import numpy as np
from jax import lax
from jax.experimental import pallas as pl
from jax.experimental.pallas import tpu as pltpu
from jax.sharding import PartitionSpec as P

PRESCALE = 168
EPS = 1e-06
ROPE_BASE = 1000000.0
ROPE_FACTOR = 8.0
GROUPS = 2
NEG = -1e30
SCALE = float(PRESCALE) ** (-0.5)
LOG2E = 1.4426950408889634
VMEM_LIMIT = 48 * 1024 * 1024
NT = (((1,), (1,)), ((), ()))
TN = (((0,), (0,)), ((), ()))


def rope_tables(block, width, blocks):
    half = width // 2
    freqs = ROPE_BASE ** (-(np.arange(half, dtype=np.float64) * 2.0 / width))
    freqs = np.concatenate([freqs, freqs])
    inner = (np.arange(block) / ROPE_FACTOR)[:, None] * freqs[None, :]
    outer = (np.asarray(blocks) * block / ROPE_FACTOR)[:, None] * freqs[None, :]
    f32 = lambda x: jnp.asarray(x.astype(np.float32))
    return f32(np.stack([np.cos(inner), np.sin(inner)])), f32(np.stack([np.cos(outer), np.sin(outer)], axis=1))


def rope_of(inner_ref, outer_ref, row):
    both = outer_ref[row]
    cb, sb = both[0:1, :], both[1:2, :]
    ct, st = inner_ref[0], inner_ref[1]
    cos = ct * cb - st * sb
    sin = st * cb + ct * sb
    lane = lax.broadcasted_iota(jnp.int32, sin.shape, 1)
    return cos, jnp.where(lane < sin.shape[1] // 2, -sin, sin)


def swap_halves(x):
    return pltpu.roll(x, x.shape[1] // 2, 1)


def unrotate(y, cos, sin):
    return y * cos + swap_halves(y * sin)


def pack_kernel(kv_heads, back, axis, k_ref, v_ref, seg_ref, gain_ref, inner_ref, outer_ref, *rest):
    outs, scratch = rest[:-1], rest[-1]
    block = seg_ref.shape[1]
    per = kv_heads // len(outs)
    cos, sin = rope_of(inner_ref, outer_ref, lax.axis_index(axis) + back)
    gain = gain_ref[...]
    scratch[...] = k_ref[...].astype(jnp.float32)
    for h in range(kv_heads):
        x = scratch[pl.ds(h, block, stride=kv_heads), :]
        r = x * lax.rsqrt(jnp.mean(x * x, axis=1, keepdims=True) + EPS) * gain
        y = r * cos + swap_halves(r) * sin
        outs[h // per][pl.ds((h % per) * block, block), :] = y.astype(jnp.bfloat16)
    scratch[...] = v_ref[...].astype(jnp.float32)
    seg = jnp.broadcast_to(seg_ref[...].astype(jnp.float32) + 1.0, (16, block)).astype(jnp.bfloat16)
    for h in range(kv_heads):
        x = scratch[pl.ds(h, block, stride=kv_heads), :]
        outs[h // per][pl.ds((per + h % per) * block, block), :] = x.astype(jnp.bfloat16)
    for out in outs:
        out[pl.ds(2 * per * block, 16), :] = seg


def query_kernel(heads, back, axis, q_ref, g_ref, gain_ref, inner_ref, outer_ref, qo_ref, go_ref, scratch):
    block = q_ref.shape[0] // heads
    cos, sin = rope_of(inner_ref, outer_ref, lax.axis_index(axis) + back)
    gain = gain_ref[...]
    scratch[...] = q_ref[...].astype(jnp.float32)
    for h in range(heads):
        x = scratch[pl.ds(h, block, stride=heads), :]
        r = x * lax.rsqrt(jnp.mean(x * x, axis=1, keepdims=True) + EPS) * gain
        y = r * cos + swap_halves(r) * sin
        qo_ref[pl.ds(h * block, block), :] = y.astype(jnp.bfloat16)
    scratch[...] = g_ref[...].astype(jnp.float32)
    for h in range(heads):
        go_ref[pl.ds(h * block, block), :] = scratch[pl.ds(h, block, stride=heads), :].astype(jnp.bfloat16)


def attend_kernel(per, group, back, q_ref, g_ref, *rest):
    blocks = rest[: back + 1]
    dq_ref, own_ref = rest[back + 1 : back + 3]
    part_refs = rest[back + 3 : 2 * back + 3]
    bias_ref = rest[-1]
    block = own_ref.shape[0] // (2 * per)
    rows = group * block
    ids = blocks[0][pl.ds(2 * per * block, 16), :].astype(jnp.float32)[0:1, :]
    ids = jnp.concatenate([ids] * group, axis=1)
    for d in range(back + 1):
        key_row = blocks[d][pl.ds(2 * per * block, 16), :].astype(jnp.float32)[0:1, :]
        key_ids = jnp.broadcast_to(key_row, (block, block)).T
        key_ids = jnp.concatenate([key_ids] * group, axis=1)
        seen = key_ids == ids
        if d == 0:
            key_at = lax.broadcasted_iota(jnp.int32, (block, rows), 0)
            query_at = lax.broadcasted_iota(jnp.int32, (block, rows), 1) & (block - 1)
            seen = seen & (key_at <= query_at)
        bias_ref[pl.ds(d * block, block), :] = jnp.where(seen, 0.0, NEG)
    for h in range(per):
        q = q_ref[pl.ds(h * rows, rows), :]
        g = g_ref[pl.ds(h * rows, rows), :]
        k = jnp.concatenate([b[pl.ds(h * block, block), :] for b in blocks], axis=0)
        v = jnp.concatenate([b[pl.ds((per + h) * block, block), :] for b in blocks], axis=0)
        scores = lax.dot_general(k, q, NT, preferred_element_type=jnp.float32)
        expo = jnp.exp2(scores * (SCALE * LOG2E) + bias_ref[...])
        prob_grads = lax.dot_general(v, g, NT, preferred_element_type=jnp.float32)
        inverse = 1.0 / jnp.sum(expo, axis=0, keepdims=True)
        delta = jnp.sum(expo * prob_grads, axis=0, keepdims=True) * inverse
        probs = expo * inverse
        score_grads = (probs * (prob_grads - delta)).astype(jnp.bfloat16)
        dv = jnp.dot(probs.astype(jnp.bfloat16), g, preferred_element_type=jnp.float32)
        dk = jnp.dot(score_grads, q, preferred_element_type=jnp.float32) * SCALE
        dq = lax.dot_general(score_grads, k, TN, preferred_element_type=jnp.float32) * SCALE
        dq_ref[pl.ds(h * rows, rows), :] = dq
        own_ref[pl.ds(h * block, block), :] = dk[:block]
        own_ref[pl.ds((per + h) * block, block), :] = dv[:block]
        for d in range(1, back + 1):
            part = part_refs[d - 1]
            part[pl.ds(h * block, block), :] = dk[d * block : (d + 1) * block].astype(jnp.bfloat16)
            part[pl.ds((per + h) * block, block), :] = dv[d * block : (d + 1) * block].astype(jnp.bfloat16)


def query_back_kernel(heads, kv_heads, groups, back, axis, *rest):
    q_ref, qgain_ref, kgain_ref, inner_ref, outer_ref = rest[:5]
    rest = rest[5:]
    dq_refs, own_refs = rest[:groups], rest[groups : 2 * groups]
    msg_refs = rest[2 * groups : (3 + back) * groups]
    part_refs = rest[(3 + back) * groups : (3 + 2 * back) * groups]
    gq_ref, gains_ref, scratch = rest[-3:]
    block = q_ref.shape[0] // heads
    width = q_ref.shape[1]
    per = kv_heads // groups
    here = lax.axis_index(axis) + back
    total = jnp.zeros((block, width), jnp.float32)
    for d in range(back + 1):
        cos, sin = rope_of(inner_ref, outer_ref, here - d)
        for g in range(groups):
            for h in range(per):
                at = pl.ds(h * block, block)
                dk = own_refs[g][at, :] if d == 0 else part_refs[g * back + d - 1][at, :].astype(jnp.float32)
                k = msg_refs[g * (back + 1) + d][at, :].astype(jnp.float32)
                total = total + unrotate(dk, cos, sin) * unrotate(k, cos, sin)
    kgain = jnp.sum(total, axis=0, keepdims=True) / kgain_ref[...]
    cos, sin = rope_of(inner_ref, outer_ref, here)
    scratch[...] = q_ref[...].astype(jnp.float32)
    gain = qgain_ref[...]
    total = jnp.zeros((block, width), jnp.float32)
    each = heads // groups
    for h in range(heads):
        x = scratch[pl.ds(h, block, stride=heads), :]
        scale = lax.rsqrt(jnp.mean(x * x, axis=1, keepdims=True) + EPS)
        normed = x * scale
        dr = unrotate(dq_refs[h // each][pl.ds((h % each) * block, block), :], cos, sin)
        total = total + dr * normed
        dn = dr * gain
        dx = scale * (dn - normed * jnp.mean(dn * normed, axis=1, keepdims=True))
        scratch[pl.ds(h, block, stride=heads), :] = dx
    gq_ref[...] = scratch[...].astype(jnp.bfloat16)
    qgain = jnp.sum(total, axis=0, keepdims=True)
    gains_ref[...] = jnp.concatenate([qgain, kgain, jnp.zeros((6, width), jnp.float32)], axis=0)


def key_back_kernel(kv_heads, groups, back, axis, *rest):
    k_ref, gain_ref, inner_ref, outer_ref = rest[:4]
    own_refs = rest[4 : 4 + groups]
    got_refs = rest[4 + groups : 4 + (1 + back) * groups]
    gk_ref, gv_ref, scratch = rest[-3:]
    block = k_ref.shape[0] // kv_heads
    per = kv_heads // groups
    cos, sin = rope_of(inner_ref, outer_ref, lax.axis_index(axis) + back)
    gain = gain_ref[...]

    def total(g, row):
        at = pl.ds(row * block, block)
        value = own_refs[g][at, :]
        for d in range(back):
            value = value + got_refs[g * back + d][at, :].astype(jnp.float32)
        return value

    scratch[...] = k_ref[...].astype(jnp.float32)
    for h in range(kv_heads):
        x = scratch[pl.ds(h, block, stride=kv_heads), :]
        scale = lax.rsqrt(jnp.mean(x * x, axis=1, keepdims=True) + EPS)
        normed = x * scale
        dn = unrotate(total(h // per, h % per), cos, sin) * gain
        dx = scale * (dn - normed * jnp.mean(dn * normed, axis=1, keepdims=True))
        scratch[pl.ds(h, block, stride=kv_heads), :] = dx
    gk_ref[...] = scratch[...].astype(jnp.bfloat16)
    for h in range(kv_heads):
        scratch[pl.ds(h, block, stride=kv_heads), :] = total(h // per, per + h % per)
    gv_ref[...] = scratch[...].astype(jnp.bfloat16)


def call(kernel, outs, scratch, cost, *args):
    vmem = pl.BlockSpec(memory_space=pltpu.VMEM)
    return pl.pallas_call(
        kernel,
        out_shape=[jax.ShapeDtypeStruct(s, t) for s, t in outs],
        in_specs=[vmem] * len(args),
        out_specs=[vmem] * len(outs),
        scratch_shapes=[pltpu.VMEM(s, jnp.float32) for s in scratch],
        compiler_params=pltpu.CompilerParams(vmem_limit_bytes=VMEM_LIMIT),
        cost_estimate=pl.CostEstimate(flops=cost, bytes_accessed=1 << 20, transcendentals=0),
    )(*args)


def sum_over(x, axis, size):
    if size & (size - 1):
        return lax.psum(x, axis)
    step = 1
    while step < size:
        x = x + lax.ppermute(x, axis, [(i, i ^ step) for i in range(size)])
        step *= 2
    return x


def by_tokens(spans, parts, q_pre, k_pre, values, grad_out, segment_ids, q_gain, k_gain):
    block, heads, width = q_pre.shape[1:]
    kv_heads = k_pre.shape[2]
    group = heads // kv_heads
    groups = GROUPS
    per = kv_heads // groups
    longest = parts * block // 2
    back = min(parts - 1, (longest - 2) // block + 1)
    bf16, f32 = jnp.bfloat16, jnp.float32
    inner, outer = rope_tables(block, width, range(-back, parts))
    q2, g2 = (x.reshape(block * heads, width) for x in (q_pre, grad_out))
    k2, v2 = (x.reshape(block * kv_heads, width) for x in (k_pre, values))
    qg, kg = q_gain.reshape(1, width), k_gain.reshape(1, width)

    message = (2 * per * block + 16, width)
    own = call(
        functools.partial(pack_kernel, kv_heads, back, "seq"),
        [(message, bf16)] * groups, [(block * kv_heads, width)], 1 << 28,
        k2, v2, segment_ids, kg, inner, outer,
    )
    window = [
        [own[g]] + [lax.ppermute(own[g], "seq", [(i, i + d) for i in range(parts - d)]) for d in range(1, back + 1)]
        for g in range(groups)
    ]
    q_rot, g_rot = call(
        functools.partial(query_kernel, heads, back, "seq"),
        [((heads * block, width), bf16)] * 2, [(heads * block, width)], 1 << 29,
        q2, g2, qg, inner, outer,
    )
    dqs, owns, shares, returned = [], [], [], []
    rows = group * block * per
    for g in range(groups):
        dq, kept, *share = call(
            functools.partial(attend_kernel, per, group, back),
            [((rows, width), f32), ((2 * per * block, width), f32)] + [((2 * per * block, width), bf16)] * back,
            [((back + 1) * block, group * block)], 1 << 30,
            lax.slice_in_dim(q_rot, g * rows, (g + 1) * rows), lax.slice_in_dim(g_rot, g * rows, (g + 1) * rows),
            *window[g],
        )
        dqs.append(dq)
        owns.append(kept)
        shares += share
        returned += [
            lax.ppermute(share[d - 1], "seq", [(i + d, i) for i in range(parts - d)]) for d in range(1, back + 1)
        ]
    grad_q, gains = call(
        functools.partial(query_back_kernel, heads, kv_heads, groups, back, "seq"),
        [((heads * block, width), bf16), ((8, width), f32)], [(heads * block, width)], 1 << 29,
        q2, qg, kg, inner, outer, *dqs, *owns, *[m for w in window for m in w], *shares,
    )
    gains = sum_over(sum_over(gains, "seq", parts), "dp", spans)
    grad_k, grad_v = call(
        functools.partial(key_back_kernel, kv_heads, groups, back, "seq"),
        [((kv_heads * block, width), bf16)] * 2, [(kv_heads * block, width)], 1 << 28,
        k2, kg, inner, outer, *owns, *returned,
    )
    return (
        grad_q.reshape(q_pre.shape),
        grad_k.reshape(k_pre.shape),
        grad_v.reshape(values.shape),
        gains[0],
        gains[1],
    )


def dma_all(pairs, sems):
    copies = [pltpu.make_async_copy(src, dst, sems.at[i]) for i, (src, dst) in enumerate(pairs)]
    for copy in copies:
        copy.start()
    return copies


def spread_kernel(axis, parts, groups, heads, kv_heads, q_hbm, g_hbm, k_hbm, v_hbm, seg_hbm, *rest):
    outs = rest[: parts * groups]
    q_in, g_in, k_in, v_in, seg_in, q_f32, g_f32, k_f32, v_f32, msg, in_sems, out_sems = rest[parts * groups :]
    block = seg_in.shape[1]
    group = heads // kv_heads
    per = kv_heads // parts // groups
    me = lax.axis_index(axis)
    loads = dma_all(
        [(k_hbm, k_in), (v_hbm, v_in), (q_hbm, q_in), (g_hbm, g_in), (seg_hbm, seg_in)], in_sems
    )
    for copy, src, dst in zip(loads, (k_in, v_in, q_in, g_in), (k_f32, v_f32, q_f32, g_f32)):
        copy.wait()
        dst[...] = src[...].astype(jnp.float32)
    loads[4].wait()
    ids = jnp.broadcast_to(seg_in[...].astype(jnp.float32), (16, block)).astype(jnp.bfloat16)
    stores = []
    for grp in range(groups):
        for part in range(parts):
            slot = grp * parts + part
            at = 0
            for p in range(per):
                kv = (part * groups + grp) * per + p
                pieces = [(q_f32, kv * group + i, heads) for i in range(group)]
                pieces += [(g_f32, kv * group + i, heads) for i in range(group)]
                pieces += [(k_f32, kv, kv_heads), (v_f32, kv, kv_heads)]
                for src, head, stride in pieces:
                    rows = src[pl.ds(head, block, stride=stride), :]
                    msg[slot, pl.ds(at, block), :] = rows.astype(jnp.bfloat16)
                    at += block
            msg[slot, pl.ds(at, 16), :] = ids
        for m in range(parts):
            i = grp * parts + m
            copy = pltpu.make_async_copy(msg.at[grp * parts + (me ^ m)], outs[i], out_sems.at[i])
            copy.start()
            stores.append(copy)
    for copy in stores:
        copy.wait()


def heads_kernel(axis, parts, grp, per, group, back, *rest):
    outs = rest[-8 - parts : -8]
    msgs = rest[-11 - 2 * parts : -11 - parts]
    inner_hbm, outer_hbm, gains_hbm = rest[-11 - parts : -8 - parts]
    share_ref, inner_ref, outer_ref, gains_ref, buf, res, in_sems, out_sems = rest[-8:]
    block, width = inner_ref.shape[1:]
    rows = group * block
    me = lax.axis_index(axis)
    loads = dma_all(
        [(inner_hbm, inner_ref), (outer_hbm, outer_ref), (gains_hbm, gains_ref)]
        + [(msgs[m], buf.at[me ^ m]) for m in range(parts)],
        in_sems,
    )
    for copy in loads:
        copy.wait()
    q_gain, k_gain = gains_ref[0:1, :], gains_ref[1:2, :]
    f32, bf16 = jnp.float32, jnp.bfloat16
    ropes = [rope_of(inner_ref, outer_ref, b) for b in range(parts)]
    last = per * (2 * group + 2) * block
    id_rows = [buf[b, pl.ds(last, 16), :].astype(f32)[0:1, :] for b in range(parts)]
    id_columns = [jnp.broadcast_to(row, (block, block)).T for row in id_rows]
    key_at = lax.broadcasted_iota(jnp.int32, (block, block), 0)
    query_at = lax.broadcasted_iota(jnp.int32, (block, block), 1)
    causal = key_at <= query_at

    def seen(key_block, query_block):
        same = id_columns[key_block] == id_rows[query_block]
        if key_block == query_block:
            same = same & causal
        return jnp.concatenate([same.astype(f32)] * group, axis=1) > 0.5

    def embed(x, gain, rope):
        scale = lax.rsqrt(jnp.mean(x * x, axis=1, keepdims=True) + EPS)
        normed = x * scale
        r = normed * gain
        return (r * rope[0] + swap_halves(r) * rope[1]).astype(bf16), normed, scale

    def embed_back(dy, gain, rope, normed, scale):
        dr = unrotate(dy, *rope)
        dn = dr * gain
        dx = scale * (dn - normed * jnp.mean(dn * normed, axis=1, keepdims=True))
        return dx.astype(bf16), dr * normed

    q_total = jnp.zeros((block, width), f32)
    k_total = jnp.zeros((block, width), f32)
    for p in range(per):
        base = p * (2 * group + 2) * block
        out_base = p * (group + 2) * block

        def piece(b, i):
            return buf[b, pl.ds(base + i * block, block), :]

        keys = [embed(piece(b, 2 * group).astype(f32), k_gain, ropes[b]) for b in range(parts)]
        dk = [jnp.zeros((block, width), f32)] * parts
        dv = [jnp.zeros((block, width), f32)] * parts
        for b in range(parts):
            first = max(0, b - back)
            queries = [embed(piece(b, i).astype(f32), q_gain, ropes[b]) for i in range(group)]
            q = jnp.concatenate([x[0] for x in queries], axis=0)
            g = buf[b, pl.ds(base + rows, rows), :]
            k = jnp.concatenate([keys[j][0] for j in range(first, b + 1)], axis=0)
            v = jnp.concatenate([piece(j, 2 * group + 1) for j in range(first, b + 1)], axis=0)
            mask = jnp.concatenate([seen(j, b) for j in range(first, b + 1)], axis=0)
            scores = lax.dot_general(k, q, NT, preferred_element_type=f32)
            expo = jnp.where(mask, jnp.exp2(scores * (SCALE * LOG2E)), 0.0)
            prob_grads = lax.dot_general(v, g, NT, preferred_element_type=f32)
            inverse = 1.0 / jnp.sum(expo, axis=0, keepdims=True)
            delta = jnp.sum(expo * prob_grads, axis=0, keepdims=True) * inverse
            probs = expo * inverse
            score_grads = (probs * (prob_grads - delta)).astype(bf16)
            dvs = jnp.dot(probs.astype(bf16), g, preferred_element_type=f32)
            dks = jnp.dot(score_grads, q, preferred_element_type=f32)
            dq = lax.dot_general(score_grads, k, TN, preferred_element_type=f32) * SCALE
            for i in range(group):
                dx, share = embed_back(dq[i * block : (i + 1) * block], q_gain, ropes[b], *queries[i][1:])
                res[b, pl.ds(out_base + i * block, block), :] = dx
                q_total = q_total + share
            for j in range(first, b + 1):
                at = slice((j - first) * block, (j - first + 1) * block)
                dk[j] = dk[j] + dks[at]
                dv[j] = dv[j] + dvs[at]
        for b in range(parts):
            dx, share = embed_back(dk[b] * SCALE, k_gain, ropes[b], *keys[b][1:])
            res[b, pl.ds(out_base + rows, block), :] = dx
            res[b, pl.ds(out_base + rows + block, block), :] = dv[b].astype(bf16)
            k_total = k_total + share
    mine = pl.ds(grp * res.shape[1], res.shape[1])
    stores = [pltpu.make_async_copy(res.at[me ^ m], outs[m].at[mine], out_sems.at[m]) for m in range(parts)]
    for copy in stores:
        copy.start()
    share_ref[...] = jnp.concatenate(
        [
            jnp.sum(q_total, axis=0, keepdims=True),
            jnp.sum(k_total, axis=0, keepdims=True),
            jnp.zeros((6, width), f32),
        ],
        axis=0,
    )
    for copy in stores:
        copy.wait()


def collect_kernel(axis, parts, groups, heads, kv_heads, *rest):
    msgs = rest[:parts]
    gq_hbm, gk_hbm, gv_hbm, buf, q_f32, k_f32, v_f32, q_out, k_out, v_out, in_sems, out_sems = rest[parts:]
    group = heads // kv_heads
    per = kv_heads // parts // groups
    block = q_out.shape[0] // heads
    me = lax.axis_index(axis)
    loads = dma_all([(msgs[m], buf.at[me ^ m]) for m in range(parts)], in_sems)
    for copy in loads:
        copy.wait()
    for part in range(parts):
        at = 0
        for grp in range(groups):
            for p in range(per):
                kv = (part * groups + grp) * per + p
                pieces = [(q_f32, kv * group + i, heads) for i in range(group)]
                pieces += [(k_f32, kv, kv_heads), (v_f32, kv, kv_heads)]
                for dst, head, stride in pieces:
                    rows = buf[part, pl.ds(at, block), :].astype(jnp.float32)
                    dst[pl.ds(head, block, stride=stride), :] = rows
                    at += block
    stores = []
    for i, (src, out, dst) in enumerate(((q_f32, q_out, gq_hbm), (k_f32, k_out, gk_hbm), (v_f32, v_out, gv_hbm))):
        out[...] = src[...].astype(jnp.bfloat16)
        copy = pltpu.make_async_copy(out, dst, out_sems.at[i])
        copy.start()
        stores.append(copy)
    for copy in stores:
        copy.wait()


def call_any(kernel, outs, scratch, cost, *args, limit=VMEM_LIMIT, aliases=None):
    return pl.pallas_call(
        kernel,
        out_shape=[jax.ShapeDtypeStruct(s, t) for s, t, _ in outs],
        in_specs=[pl.BlockSpec(memory_space=pltpu.HBM)] * len(args),
        out_specs=[pl.BlockSpec(memory_space=m) for _, _, m in outs],
        scratch_shapes=scratch,
        input_output_aliases=aliases or {},
        compiler_params=pltpu.CompilerParams(vmem_limit_bytes=limit),
        cost_estimate=pl.CostEstimate(flops=cost, bytes_accessed=1 << 20, transcendentals=0),
    )(*args)


def exchange_sum(x, axis, size, *steps):
    for step in steps:
        x = x + lax.ppermute(x, axis, [(i, i ^ step) for i in range(size)])
    return x


def by_heads(spans, parts, q_pre, k_pre, values, grad_out, segment_ids, q_gain, k_gain):
    block, heads, width = q_pre.shape[1:]
    kv_heads = k_pre.shape[2]
    group = heads // kv_heads
    groups = min(GROUPS, kv_heads // parts)
    per = kv_heads // parts // groups
    longest = parts * block // 2
    back = min(parts - 1, (longest - 2) // block + 1)
    bf16, f32, vmem = jnp.bfloat16, jnp.float32, pltpu.VMEM
    inner, outer = rope_tables(block, width, range(parts))
    q2, g2 = (x.reshape(block * heads, width) for x in (q_pre, grad_out))
    k2, v2 = (x.reshape(block * kv_heads, width) for x in (k_pre, values))
    sent = (per * (2 * group + 2) * block + 16, width)
    back_sent = (per * (group + 2) * block, width)
    dma = pltpu.SemaphoreType.DMA
    q_shape, k_shape = q2.shape, k2.shape

    messages = call_any(
        functools.partial(spread_kernel, "seq", parts, groups, heads, kv_heads),
        [(sent, bf16, pltpu.HBM)] * (parts * groups),
        [vmem(q_shape, bf16), vmem(q_shape, bf16), vmem(k_shape, bf16), vmem(k_shape, bf16), vmem((1, block), jnp.int32)]
        + [vmem(q_shape, f32), vmem(q_shape, f32), vmem(k_shape, f32), vmem(k_shape, f32)]
        + [vmem((parts * groups, *sent), bf16), dma((5,)), dma((parts * groups,))],
        1 << 20, q2, g2, k2, v2, segment_ids, limit=62 * 1024 * 1024,
    )
    gains = jnp.concatenate([q_gain[None], k_gain[None], jnp.zeros((6, width), f32)], axis=0)
    xor = lambda m, size: [(i, i ^ m) for i in range(size)]
    arrived = [
        [messages[grp * parts]]
        + [lax.ppermute(messages[grp * parts + m], "seq", xor(m, parts)) for m in range(1, parts)]
        for grp in range(groups)
    ]
    results, shares = [], []
    for grp in range(groups):
        *results, share = call_any(
            functools.partial(heads_kernel, "seq", parts, grp, per, group, back),
            [((groups * back_sent[0], width), bf16, pltpu.HBM)] * parts + [((8, width), f32, vmem)],
            [vmem(inner.shape, f32), vmem(outer.shape, f32), vmem(gains.shape, f32)]
            + [vmem((parts, *sent), bf16), vmem((parts, *back_sent), bf16), dma((3 + parts,)), dma((parts,))],
            1 << 34, *results, *arrived[grp], inner, outer, gains, aliases={m: m for m in range(len(results))},
        )
        shares.append(share)
    returned = [results[0]] + [lax.ppermute(results[m], "seq", xor(m, parts)) for m in range(1, parts)]
    total = functools.reduce(jnp.add, shares)
    total = exchange_sum(total, "dp", spans, 1, 2, 4)
    total = exchange_sum(total, "seq", parts, 1, 2)
    grad_q, grad_k, grad_v = call_any(
        functools.partial(collect_kernel, "seq", parts, groups, heads, kv_heads),
        [(q_shape, bf16, pltpu.HBM), (k_shape, bf16, pltpu.HBM), (k_shape, bf16, pltpu.HBM)],
        [vmem((parts, groups * back_sent[0], width), bf16)]
        + [vmem(q_shape, f32), vmem(k_shape, f32), vmem(k_shape, f32)]
        + [vmem(q_shape, bf16), vmem(k_shape, bf16), vmem(k_shape, bf16), dma((parts,)), dma((3,))],
        1 << 20, *returned,
    )
    return (
        grad_q.reshape(q_pre.shape), grad_k.reshape(k_pre.shape), grad_v.reshape(values.shape), total[0], total[1],
    )


def solution(mesh):
    tokens = P("dp", "seq", None, None)
    spans, parts = mesh.shape["dp"], mesh.shape["seq"]
    body = by_heads if (spans, parts) == (8, 4) else by_tokens
    return jax.shard_map(
        functools.partial(body, spans, parts),
        mesh=mesh,
        in_specs=(tokens, tokens, tokens, tokens, P("dp", "seq"), P(), P()),
        out_specs=(tokens, tokens, tokens, P(), P()),
        check_vma=False,
    )
```

```python
import functools

import jax
import jax.numpy as jnp
import numpy as np
from jax import lax
from jax.experimental import pallas as pl
from jax.experimental.pallas import tpu as pltpu
from jax.sharding import PartitionSpec as P

PRESCALE = 168
EPS = 1e-06
ROPE_BASE = 1000000.0
ROPE_FACTOR = 8.0
GROUPS = 2
NEG = -1e30
SCALE = float(PRESCALE) ** (-0.5)
LOG2E = 1.4426950408889634
VMEM_LIMIT = 48 * 1024 * 1024
HEADS_VMEM = 24 * 1024 * 1024
SPREAD_VMEM = 61 * 1024 * 1024
NT = (((1,), (1,)), ((), ()))
TN = (((0,), (0,)), ((), ()))


def rope_tables(block, width, blocks):
    half = width // 2
    freqs = ROPE_BASE ** (-(np.arange(half, dtype=np.float64) * 2.0 / width))
    freqs = np.concatenate([freqs, freqs])
    inner = (np.arange(block) / ROPE_FACTOR)[:, None] * freqs[None, :]
    outer = (np.asarray(blocks) * block / ROPE_FACTOR)[:, None] * freqs[None, :]
    f32 = lambda x: jnp.asarray(x.astype(np.float32))
    return f32(np.stack([np.cos(inner), np.sin(inner)])), f32(np.stack([np.cos(outer), np.sin(outer)], axis=1))


def rope_of(inner_ref, outer_ref, row):
    both = outer_ref[row]
    cb, sb = both[0:1, :], both[1:2, :]
    ct, st = inner_ref[0], inner_ref[1]
    cos = ct * cb - st * sb
    sin = st * cb + ct * sb
    lane = lax.broadcasted_iota(jnp.int32, sin.shape, 1)
    return cos, jnp.where(lane < sin.shape[1] // 2, -sin, sin)


def swap_halves(x):
    return pltpu.roll(x, x.shape[1] // 2, 1)


def unrotate(y, cos, sin):
    return y * cos + swap_halves(y * sin)


def pack_kernel(kv_heads, back, axis, k_ref, v_ref, seg_ref, gain_ref, inner_ref, outer_ref, *rest):
    outs, scratch = rest[:-1], rest[-1]
    block = seg_ref.shape[1]
    per = kv_heads // len(outs)
    cos, sin = rope_of(inner_ref, outer_ref, lax.axis_index(axis) + back)
    gain = gain_ref[...]
    scratch[...] = k_ref[...].astype(jnp.float32)
    for h in range(kv_heads):
        x = scratch[pl.ds(h, block, stride=kv_heads), :]
        r = x * lax.rsqrt(jnp.mean(x * x, axis=1, keepdims=True) + EPS) * gain
        y = r * cos + swap_halves(r) * sin
        outs[h // per][pl.ds((h % per) * block, block), :] = y.astype(jnp.bfloat16)
    scratch[...] = v_ref[...].astype(jnp.float32)
    seg = jnp.broadcast_to(seg_ref[...].astype(jnp.float32) + 1.0, (16, block)).astype(jnp.bfloat16)
    for h in range(kv_heads):
        x = scratch[pl.ds(h, block, stride=kv_heads), :]
        outs[h // per][pl.ds((per + h % per) * block, block), :] = x.astype(jnp.bfloat16)
    for out in outs:
        out[pl.ds(2 * per * block, 16), :] = seg


def query_kernel(heads, back, axis, q_ref, g_ref, gain_ref, inner_ref, outer_ref, qo_ref, go_ref, scratch):
    block = q_ref.shape[0] // heads
    cos, sin = rope_of(inner_ref, outer_ref, lax.axis_index(axis) + back)
    gain = gain_ref[...]
    scratch[...] = q_ref[...].astype(jnp.float32)
    for h in range(heads):
        x = scratch[pl.ds(h, block, stride=heads), :]
        r = x * lax.rsqrt(jnp.mean(x * x, axis=1, keepdims=True) + EPS) * gain
        y = r * cos + swap_halves(r) * sin
        qo_ref[pl.ds(h * block, block), :] = y.astype(jnp.bfloat16)
    scratch[...] = g_ref[...].astype(jnp.float32)
    for h in range(heads):
        go_ref[pl.ds(h * block, block), :] = scratch[pl.ds(h, block, stride=heads), :].astype(jnp.bfloat16)


def attend_kernel(per, group, back, q_ref, g_ref, *rest):
    blocks = rest[: back + 1]
    dq_ref, own_ref = rest[back + 1 : back + 3]
    part_refs = rest[back + 3 : 2 * back + 3]
    bias_ref = rest[-1]
    block = own_ref.shape[0] // (2 * per)
    rows = group * block
    ids = blocks[0][pl.ds(2 * per * block, 16), :].astype(jnp.float32)[0:1, :]
    ids = jnp.concatenate([ids] * group, axis=1)
    for d in range(back + 1):
        key_row = blocks[d][pl.ds(2 * per * block, 16), :].astype(jnp.float32)[0:1, :]
        key_ids = jnp.broadcast_to(key_row, (block, block)).T
        key_ids = jnp.concatenate([key_ids] * group, axis=1)
        seen = key_ids == ids
        if d == 0:
            key_at = lax.broadcasted_iota(jnp.int32, (block, rows), 0)
            query_at = lax.broadcasted_iota(jnp.int32, (block, rows), 1) & (block - 1)
            seen = seen & (key_at <= query_at)
        bias_ref[pl.ds(d * block, block), :] = jnp.where(seen, 0.0, NEG)
    for h in range(per):
        q = q_ref[pl.ds(h * rows, rows), :]
        g = g_ref[pl.ds(h * rows, rows), :]
        k = jnp.concatenate([b[pl.ds(h * block, block), :] for b in blocks], axis=0)
        v = jnp.concatenate([b[pl.ds((per + h) * block, block), :] for b in blocks], axis=0)
        scores = lax.dot_general(k, q, NT, preferred_element_type=jnp.float32)
        expo = jnp.exp2(scores * (SCALE * LOG2E) + bias_ref[...])
        prob_grads = lax.dot_general(v, g, NT, preferred_element_type=jnp.float32)
        inverse = 1.0 / jnp.sum(expo, axis=0, keepdims=True)
        delta = jnp.sum(expo * prob_grads, axis=0, keepdims=True) * inverse
        probs = expo * inverse
        score_grads = (probs * (prob_grads - delta)).astype(jnp.bfloat16)
        dv = jnp.dot(probs.astype(jnp.bfloat16), g, preferred_element_type=jnp.float32)
        dk = jnp.dot(score_grads, q, preferred_element_type=jnp.float32) * SCALE
        dq = lax.dot_general(score_grads, k, TN, preferred_element_type=jnp.float32) * SCALE
        dq_ref[pl.ds(h * rows, rows), :] = dq
        own_ref[pl.ds(h * block, block), :] = dk[:block]
        own_ref[pl.ds((per + h) * block, block), :] = dv[:block]
        for d in range(1, back + 1):
            part = part_refs[d - 1]
            part[pl.ds(h * block, block), :] = dk[d * block : (d + 1) * block].astype(jnp.bfloat16)
            part[pl.ds((per + h) * block, block), :] = dv[d * block : (d + 1) * block].astype(jnp.bfloat16)


def query_back_kernel(heads, kv_heads, groups, back, axis, *rest):
    q_ref, qgain_ref, kgain_ref, inner_ref, outer_ref = rest[:5]
    rest = rest[5:]
    dq_refs, own_refs = rest[:groups], rest[groups : 2 * groups]
    msg_refs = rest[2 * groups : (3 + back) * groups]
    part_refs = rest[(3 + back) * groups : (3 + 2 * back) * groups]
    gq_ref, gains_ref, scratch = rest[-3:]
    block = q_ref.shape[0] // heads
    width = q_ref.shape[1]
    per = kv_heads // groups
    here = lax.axis_index(axis) + back
    total = jnp.zeros((block, width), jnp.float32)
    for d in range(back + 1):
        cos, sin = rope_of(inner_ref, outer_ref, here - d)
        for g in range(groups):
            for h in range(per):
                at = pl.ds(h * block, block)
                dk = own_refs[g][at, :] if d == 0 else part_refs[g * back + d - 1][at, :].astype(jnp.float32)
                k = msg_refs[g * (back + 1) + d][at, :].astype(jnp.float32)
                total = total + unrotate(dk, cos, sin) * unrotate(k, cos, sin)
    kgain = jnp.sum(total, axis=0, keepdims=True) / kgain_ref[...]
    cos, sin = rope_of(inner_ref, outer_ref, here)
    scratch[...] = q_ref[...].astype(jnp.float32)
    gain = qgain_ref[...]
    total = jnp.zeros((block, width), jnp.float32)
    each = heads // groups
    for h in range(heads):
        x = scratch[pl.ds(h, block, stride=heads), :]
        scale = lax.rsqrt(jnp.mean(x * x, axis=1, keepdims=True) + EPS)
        normed = x * scale
        dr = unrotate(dq_refs[h // each][pl.ds((h % each) * block, block), :], cos, sin)
        total = total + dr * normed
        dn = dr * gain
        dx = scale * (dn - normed * jnp.mean(dn * normed, axis=1, keepdims=True))
        scratch[pl.ds(h, block, stride=heads), :] = dx
    gq_ref[...] = scratch[...].astype(jnp.bfloat16)
    qgain = jnp.sum(total, axis=0, keepdims=True)
    gains_ref[...] = jnp.concatenate([qgain, kgain, jnp.zeros((6, width), jnp.float32)], axis=0)


def key_back_kernel(kv_heads, groups, back, axis, *rest):
    k_ref, gain_ref, inner_ref, outer_ref = rest[:4]
    own_refs = rest[4 : 4 + groups]
    got_refs = rest[4 + groups : 4 + (1 + back) * groups]
    gk_ref, gv_ref, scratch = rest[-3:]
    block = k_ref.shape[0] // kv_heads
    per = kv_heads // groups
    cos, sin = rope_of(inner_ref, outer_ref, lax.axis_index(axis) + back)
    gain = gain_ref[...]

    def total(g, row):
        at = pl.ds(row * block, block)
        value = own_refs[g][at, :]
        for d in range(back):
            value = value + got_refs[g * back + d][at, :].astype(jnp.float32)
        return value

    scratch[...] = k_ref[...].astype(jnp.float32)
    for h in range(kv_heads):
        x = scratch[pl.ds(h, block, stride=kv_heads), :]
        scale = lax.rsqrt(jnp.mean(x * x, axis=1, keepdims=True) + EPS)
        normed = x * scale
        dn = unrotate(total(h // per, h % per), cos, sin) * gain
        dx = scale * (dn - normed * jnp.mean(dn * normed, axis=1, keepdims=True))
        scratch[pl.ds(h, block, stride=kv_heads), :] = dx
    gk_ref[...] = scratch[...].astype(jnp.bfloat16)
    for h in range(kv_heads):
        scratch[pl.ds(h, block, stride=kv_heads), :] = total(h // per, per + h % per)
    gv_ref[...] = scratch[...].astype(jnp.bfloat16)


def call(kernel, outs, scratch, cost, *args):
    vmem = pl.BlockSpec(memory_space=pltpu.VMEM)
    return pl.pallas_call(
        kernel,
        out_shape=[jax.ShapeDtypeStruct(s, t) for s, t in outs],
        in_specs=[vmem] * len(args),
        out_specs=[vmem] * len(outs),
        scratch_shapes=[pltpu.VMEM(s, jnp.float32) for s in scratch],
        compiler_params=pltpu.CompilerParams(vmem_limit_bytes=VMEM_LIMIT),
        cost_estimate=pl.CostEstimate(flops=cost, bytes_accessed=1 << 20, transcendentals=0),
    )(*args)


def sum_over(x, axis, size):
    if size & (size - 1):
        return lax.psum(x, axis)
    step = 1
    while step < size:
        x = x + lax.ppermute(x, axis, [(i, i ^ step) for i in range(size)])
        step *= 2
    return x


def by_tokens(spans, parts, q_pre, k_pre, values, grad_out, segment_ids, q_gain, k_gain):
    block, heads, width = q_pre.shape[1:]
    kv_heads = k_pre.shape[2]
    group = heads // kv_heads
    groups = GROUPS
    per = kv_heads // groups
    longest = parts * block // 2
    back = min(parts - 1, (longest - 2) // block + 1)
    bf16, f32 = jnp.bfloat16, jnp.float32
    inner, outer = rope_tables(block, width, range(-back, parts))
    q2, g2 = (x.reshape(block * heads, width) for x in (q_pre, grad_out))
    k2, v2 = (x.reshape(block * kv_heads, width) for x in (k_pre, values))
    qg, kg = q_gain.reshape(1, width), k_gain.reshape(1, width)

    message = (2 * per * block + 16, width)
    own = call(
        functools.partial(pack_kernel, kv_heads, back, "seq"),
        [(message, bf16)] * groups, [(block * kv_heads, width)], 1 << 28,
        k2, v2, segment_ids, kg, inner, outer,
    )
    window = [
        [own[g]] + [lax.ppermute(own[g], "seq", [(i, i + d) for i in range(parts - d)]) for d in range(1, back + 1)]
        for g in range(groups)
    ]
    q_rot, g_rot = call(
        functools.partial(query_kernel, heads, back, "seq"),
        [((heads * block, width), bf16)] * 2, [(heads * block, width)], 1 << 29,
        q2, g2, qg, inner, outer,
    )
    dqs, owns, shares, returned = [], [], [], []
    rows = group * block * per
    for g in range(groups):
        dq, kept, *share = call(
            functools.partial(attend_kernel, per, group, back),
            [((rows, width), f32), ((2 * per * block, width), f32)] + [((2 * per * block, width), bf16)] * back,
            [((back + 1) * block, group * block)], 1 << 30,
            lax.slice_in_dim(q_rot, g * rows, (g + 1) * rows), lax.slice_in_dim(g_rot, g * rows, (g + 1) * rows),
            *window[g],
        )
        dqs.append(dq)
        owns.append(kept)
        shares += share
        returned += [
            lax.ppermute(share[d - 1], "seq", [(i + d, i) for i in range(parts - d)]) for d in range(1, back + 1)
        ]
    grad_q, gains = call(
        functools.partial(query_back_kernel, heads, kv_heads, groups, back, "seq"),
        [((heads * block, width), bf16), ((8, width), f32)], [(heads * block, width)], 1 << 29,
        q2, qg, kg, inner, outer, *dqs, *owns, *[m for w in window for m in w], *shares,
    )
    gains = sum_over(sum_over(gains, "seq", parts), "dp", spans)
    grad_k, grad_v = call(
        functools.partial(key_back_kernel, kv_heads, groups, back, "seq"),
        [((kv_heads * block, width), bf16)] * 2, [(kv_heads * block, width)], 1 << 28,
        k2, kg, inner, outer, *owns, *returned,
    )
    return (
        grad_q.reshape(q_pre.shape),
        grad_k.reshape(k_pre.shape),
        grad_v.reshape(values.shape),
        gains[0],
        gains[1],
    )


def spread_kernel(axis, parts, groups, heads, kv_heads, q_hbm, g_hbm, k_hbm, v_hbm, seg_hbm, *rest):
    outs = rest[: parts * groups]
    q_in, g_in, k_in, v_in, seg_in, q_f32, g_f32, k_f32, v_f32, sems = rest[parts * groups :]
    block = seg_in.shape[1]
    group = heads // kv_heads
    per = kv_heads // parts // groups
    me = lax.axis_index(axis)
    pairs = [(seg_hbm, seg_in)]
    for src, dst in ((k_hbm, k_in), (v_hbm, v_in), (q_hbm, q_in), (g_hbm, g_in)):
        half = dst.shape[0] // 2
        pairs += [(src.at[pl.ds(i * half, half)], dst.at[pl.ds(i * half, half)]) for i in range(2)]
    loads = [pltpu.make_async_copy(src, dst, sems.at[i]) for i, (src, dst) in enumerate(pairs)]
    for copy in loads:
        copy.start()
    loads[0].wait()
    ids = jnp.broadcast_to(seg_in[...].astype(jnp.float32), (16, block)).astype(jnp.bfloat16)
    for n, (src, dst) in enumerate(((k_in, k_f32), (v_in, v_f32), (q_in, q_f32), (g_in, g_f32))):
        half = dst.shape[0] // 2
        for i in range(2):
            loads[1 + 2 * n + i].wait()
            dst[pl.ds(i * half, half), :] = src[pl.ds(i * half, half), :].astype(jnp.float32)
    for grp in range(groups):
        for m in range(parts):
            out = outs[grp * parts + m]
            at = 0
            for p in range(per):
                kv = ((me ^ m) * groups + grp) * per + p
                pieces = [(q_f32, kv * group + i, heads) for i in range(group)]
                pieces += [(g_f32, kv * group + i, heads) for i in range(group)]
                pieces += [(k_f32, kv, kv_heads), (v_f32, kv, kv_heads)]
                for src, head, stride in pieces:
                    rows = src[pl.ds(head, block, stride=stride), :]
                    out[pl.ds(at, block), :] = rows.astype(jnp.bfloat16)
                    at += block
            out[pl.ds(at, 16), :] = ids


def eye(size):
    row = lax.broadcasted_iota(jnp.int32, (size, size), 0)
    return (row == lax.broadcasted_iota(jnp.int32, (size, size), 1)).astype(jnp.bfloat16)


def turned(x, unit):
    return lax.dot_general(unit, x, NT, preferred_element_type=jnp.float32)


def heads_kernel(axis, parts, grp, per, group, back, *rest):
    earlier, msgs = rest[: grp * parts], rest[grp * parts : grp * parts + parts]
    table_ref, gains_ref = rest[parts + grp * parts : parts + grp * parts + 2]
    outs = rest[-parts - 12 : -12]
    share_ref, qt_ref, kt_ref, k_ref, v_ref, g_ref, qn_ref, kn_ref, qs_ref, ks_ref, id_ref, res_ref = rest[-12:]
    block, width = table_ref.shape[3], msgs[0].shape[1]
    half = width // 2
    rows = group * block
    f32, bf16 = jnp.float32, jnp.bfloat16
    me = lax.axis_index(axis)
    unit, unit_rows = eye(width), eye(rows)
    q_gain = jnp.broadcast_to(gains_ref[0:1, :], (width, width)).T
    k_gain = jnp.broadcast_to(gains_ref[1:2, :], (width, width)).T
    q_gain = jnp.concatenate([q_gain] * group, axis=1)
    last = per * (2 * group + 2) * block

    def rotated(x, c, s):
        a, b = x[:half], x[half:]
        return jnp.concatenate([a * c - b * s, b * c + a * s], axis=0)

    def embed(x, gain, c, s):
        scale = lax.rsqrt(jnp.sum(x * x, axis=0, keepdims=True) * (1.0 / width) + EPS)
        normed = x * scale
        return rotated(normed * gain, c, s).astype(bf16), normed, scale

    def embed_back(dy, gain, c, s, normed, scale):
        dr = rotated(dy, c, -s)
        share = dr * normed
        dn = dr * gain
        mean = jnp.sum(dn * normed, axis=0, keepdims=True) * (1.0 / width)
        return ((scale * SCALE) * (dn - normed * mean)).astype(bf16), share

    def rope(b, copies):
        c, s = table_ref[b, 0], table_ref[b, 1]
        return jnp.concatenate([c] * copies, axis=1), jnp.concatenate([s] * copies, axis=1)

    for m in range(parts):
        b = me ^ m
        id_ref[b] = jnp.broadcast_to(msgs[m][pl.ds(last, 16), :].astype(f32)[0:1, :], (8, block))
        for p in range(per):
            base = p * (2 * group + 2) * block
            at = b * per + p
            y, normed, scale = embed(turned(msgs[m][pl.ds(base, rows), :], unit), q_gain, *rope(b, group))
            qt_ref[at], qn_ref[at], qs_ref[at] = y, normed, jnp.broadcast_to(scale, (8, rows))
            g_ref[at] = msgs[m][pl.ds(base + rows, rows), :]
            y, normed, scale = embed(turned(msgs[m][pl.ds(base + 2 * rows, block), :], unit), k_gain, *rope(b, 1))
            kt_ref[at], kn_ref[at], ks_ref[at] = y, normed, jnp.broadcast_to(scale, (8, block))
            k_ref[at] = turned(y, unit).astype(bf16)
            v_ref[at] = msgs[m][pl.ds(base + 2 * rows + block, block), :]

    id_rows = [id_ref[b][0:1, :] for b in range(parts)]
    id_columns = [turned(jnp.broadcast_to(row, (block, block)).astype(bf16), unit) for row in id_rows]
    key_at = lax.broadcasted_iota(jnp.int32, (block, block), 0)
    query_at = lax.broadcasted_iota(jnp.int32, (block, block), 1)
    causal = jnp.where(key_at <= query_at, 0.0, NEG)

    def bias(key_block, query_block):
        value = jnp.where(id_columns[key_block] == id_rows[query_block], 0.0, NEG)
        if key_block == query_block:
            value = value + causal
        return jnp.concatenate([value] * group, axis=1)

    q_total = jnp.zeros((width, rows), f32)
    k_total = jnp.zeros((width, block), f32)
    for p in range(per):
        out_base = p * (group + 2) * block
        dk = [None] * parts
        dv = [None] * parts
        for b in range(parts):
            span = range(max(0, b - back), b + 1)
            qt, g = qt_ref[b * per + p], g_ref[b * per + p]
            k = jnp.concatenate([k_ref[j * per + p] for j in span], axis=0)
            kt = jnp.concatenate([kt_ref[j * per + p] for j in span], axis=1)
            v = jnp.concatenate([v_ref[j * per + p] for j in span], axis=0)
            hidden = jnp.concatenate([bias(j, b) for j in span], axis=0)
            scores = jnp.dot(k, qt, preferred_element_type=f32)
            expo = jnp.exp2(scores * (SCALE * LOG2E) + hidden)
            prob_grads = lax.dot_general(v, g, NT, preferred_element_type=f32)
            inverse = 1.0 / jnp.sum(expo, axis=0, keepdims=True)
            delta = jnp.sum(expo * prob_grads, axis=0, keepdims=True) * inverse
            probs = expo * inverse
            score_grads = (probs * (prob_grads - delta)).astype(bf16)
            dvs = jnp.dot(probs.astype(bf16), g, preferred_element_type=f32)
            dks = lax.dot_general(qt, score_grads, NT, preferred_element_type=f32)
            dq = jnp.dot(kt, score_grads, preferred_element_type=f32)
            for i, j in enumerate(span):
                cut = slice(i * block, (i + 1) * block)
                dk[j] = dks[:, cut] if dk[j] is None else dk[j] + dks[:, cut]
                dv[j] = dvs[cut] if dv[j] is None else dv[j] + dvs[cut]
            at = b * per + p
            dx, share = embed_back(dq, q_gain, *rope(b, group), qn_ref[at], qs_ref[at][0:1, :])
            q_total = q_total + share
            res_ref[b, pl.ds(out_base, rows), :] = turned(dx, unit_rows).astype(bf16)
        for b in range(parts):
            at = b * per + p
            dx, share = embed_back(dk[b], k_gain, *rope(b, 1), kn_ref[at], ks_ref[at][0:1, :])
            k_total = k_total + share
            res_ref[b, pl.ds(out_base + rows, block), :] = turned(dx, unit).astype(bf16)
            res_ref[b, pl.ds(out_base + rows + block, block), :] = dv[b].astype(bf16)
    size = res_ref.shape[1]
    for m in range(parts):
        for i in range(grp):
            outs[m][pl.ds(i * size, size), :] = earlier[i * parts + m][...]
        outs[m][pl.ds(grp * size, size), :] = res_ref[me ^ m]
    ones = jnp.ones((8, rows), f32)
    exact = functools.partial(
        lax.dot_general, dimension_numbers=NT, precision=lax.Precision.HIGHEST, preferred_element_type=f32
    )
    q_share, k_share = exact(ones, q_total), exact(ones[:, :block], k_total)
    row = lax.broadcasted_iota(jnp.int32, (8, width), 0)
    share_ref[...] = jnp.where(row == 0, q_share, jnp.where(row == 1, k_share, 0.0)) * SCALE


def collect_kernel(axis, parts, groups, heads, kv_heads, *rest):
    msgs = rest[:parts]
    gq_hbm, gk_hbm, gv_hbm, q_f32, k_f32, v_f32, q_out, k_out, v_out, sems = rest[parts:]
    group = heads // kv_heads
    per = kv_heads // parts // groups
    block = q_out.shape[0] // heads
    me = lax.axis_index(axis)
    for m in range(parts):
        at = 0
        for grp in range(groups):
            for p in range(per):
                kv = ((me ^ m) * groups + grp) * per + p
                pieces = [(q_f32, kv * group + i, heads) for i in range(group)]
                pieces += [(k_f32, kv, kv_heads), (v_f32, kv, kv_heads)]
                for dst, head, stride in pieces:
                    rows = msgs[m][pl.ds(at, block), :].astype(jnp.float32)
                    dst[pl.ds(head, block, stride=stride), :] = rows
                    at += block
    stores = []
    for src, out, dst in ((q_f32, q_out, gq_hbm), (k_f32, k_out, gk_hbm), (v_f32, v_out, gv_hbm)):
        half = out.shape[0] // 2
        for i in range(2):
            cut = pl.ds(i * half, half)
            out[cut, :] = src[cut, :].astype(jnp.bfloat16)
            copy = pltpu.make_async_copy(out.at[cut], dst.at[cut], sems.at[len(stores)])
            copy.start()
            stores.append(copy)
    for copy in stores:
        copy.wait()


def call_in(kernel, ins, outs, scratch, cost, *args, limit=HEADS_VMEM):
    return pl.pallas_call(
        kernel,
        out_shape=[jax.ShapeDtypeStruct(s, t) for s, t, _ in outs],
        in_specs=[pl.BlockSpec(memory_space=m) for m in ins],
        out_specs=[pl.BlockSpec(memory_space=m) for _, _, m in outs],
        scratch_shapes=scratch,
        compiler_params=pltpu.CompilerParams(vmem_limit_bytes=limit),
        cost_estimate=pl.CostEstimate(flops=cost, bytes_accessed=1 << 20, transcendentals=0),
    )(*args)


def exchange_sum(x, axis, size, *partners):
    got = [lax.ppermute(x, axis, [(i, i ^ m) for i in range(size)]) for m in partners]
    return x + got[0] if len(got) == 1 else (x + got[0]) + (got[1] + got[2])


def by_heads(spans, parts, q_pre, k_pre, values, grad_out, segment_ids, q_gain, k_gain):
    block, heads, width = q_pre.shape[1:]
    kv_heads = k_pre.shape[2]
    group = heads // kv_heads
    groups = min(GROUPS, kv_heads // parts)
    per = kv_heads // parts // groups
    rows = group * block
    longest = parts * block // 2
    back = min(parts - 1, (longest - 2) // block + 1)
    bf16, f32, vmem, hbm = jnp.bfloat16, jnp.float32, pltpu.VMEM, pltpu.HBM
    freqs = ROPE_BASE ** (-(np.arange(width // 2, dtype=np.float64) * 2.0 / width))
    angles = (np.arange(parts * block) / ROPE_FACTOR).reshape(parts, 1, block) * freqs[:, None]
    table = jnp.asarray(np.stack([np.cos(angles), np.sin(angles)], axis=1).astype(np.float32))
    q2, g2 = (x.reshape(block * heads, width) for x in (q_pre, grad_out))
    k2, v2 = (x.reshape(block * kv_heads, width) for x in (k_pre, values))
    sent = (per * (2 * group + 2) * block + 16, width)
    back_sent = (per * (group + 2) * block, width)
    dma = pltpu.SemaphoreType.DMA
    q_shape, k_shape = q2.shape, k2.shape

    messages = call_in(
        functools.partial(spread_kernel, "seq", parts, groups, heads, kv_heads),
        [hbm] * 5, [(sent, bf16, vmem)] * (parts * groups),
        [vmem(q_shape, bf16), vmem(q_shape, bf16), vmem(k_shape, bf16), vmem(k_shape, bf16), vmem((1, block), jnp.int32)]
        + [vmem(q_shape, f32), vmem(q_shape, f32), vmem(k_shape, f32), vmem(k_shape, f32), dma((9,))],
        1 << 20, q2, g2, k2, v2, segment_ids, limit=SPREAD_VMEM,
    )
    gains = jnp.concatenate([q_gain[None], k_gain[None], jnp.zeros((6, width), f32)], axis=0)
    xor = lambda m, size: [(i, i ^ m) for i in range(size)]
    arrived = [
        [messages[grp * parts]]
        + [lax.ppermute(messages[grp * parts + m], "seq", xor(m, parts)) for m in range(1, parts)]
        for grp in range(groups)
    ]
    results, shares = [], []
    for grp in range(groups):
        inputs = [*results, *arrived[grp], table, gains]
        *made, share = call_in(
            functools.partial(heads_kernel, "seq", parts, grp, per, group, back),
            [vmem] * len(inputs),
            [(((grp + 1) * back_sent[0], width), bf16, vmem)] * parts + [((8, width), f32, vmem)],
            [vmem((parts * per, width, rows), bf16), vmem((parts * per, width, block), bf16)]
            + [vmem((parts * per, block, width), bf16), vmem((parts * per, block, width), bf16)]
            + [vmem((parts * per, rows, width), bf16)]
            + [vmem((parts * per, width, rows), f32), vmem((parts * per, width, block), f32)]
            + [vmem((parts * per, 8, rows), f32), vmem((parts * per, 8, block), f32), vmem((parts, 8, block), f32)]
            + [vmem((parts, *back_sent), bf16)],
            1 << 34, *inputs,
        )
        results = made
        shares.append(share)
    first, second, third = (lax.ppermute(results[m], "seq", xor(m, parts)) for m in (1, 2, 3))
    total = exchange_sum(functools.reduce(jnp.add, shares), "dp", spans, 1)
    total = exchange_sum(exchange_sum(total, "dp", spans, 2), "dp", spans, 4)
    total, first, second = lax.optimization_barrier((total, first, second))
    total = exchange_sum(total, "seq", parts, 1, 2, 3)
    grad_q, grad_k, grad_v = call_in(
        functools.partial(collect_kernel, "seq", parts, groups, heads, kv_heads),
        [vmem] * parts, [(q_shape, bf16, hbm), (k_shape, bf16, hbm), (k_shape, bf16, hbm)],
        [vmem(q_shape, f32), vmem(k_shape, f32), vmem(k_shape, f32)]
        + [vmem(q_shape, bf16), vmem(k_shape, bf16), vmem(k_shape, bf16), dma((6,))],
        1 << 20, results[0], first, second, third,
    )
    return (
        grad_q.reshape(q_pre.shape), grad_k.reshape(k_pre.shape), grad_v.reshape(values.shape), total[0], total[1],
    )


def solution(mesh):
    tokens = P("dp", "seq", None, None)
    spans, parts = mesh.shape["dp"], mesh.shape["seq"]
    body = by_heads if (spans, parts) == (8, 4) else by_tokens
    return jax.shard_map(
        functools.partial(body, spans, parts),
        mesh=mesh,
        in_specs=(tokens, tokens, tokens, tokens, P("dp", "seq"), P(), P()),
        out_specs=(tokens, tokens, tokens, P(), P()),
        check_vma=False,
    )
```

```python
import functools

import jax
import jax.numpy as jnp
import numpy as np
from jax import lax
from jax.experimental import pallas as pl
from jax.experimental.pallas import tpu as pltpu
from jax.sharding import PartitionSpec as P

PRESCALE = 168
EPS = 1e-06
ROPE_BASE = 1000000.0
ROPE_FACTOR = 8.0
GROUPS = 2
NEG = -1e30
SCALE = float(PRESCALE) ** (-0.5)
LOG2E = 1.4426950408889634
VMEM_LIMIT = 48 * 1024 * 1024
HEADS_VMEM = 24 * 1024 * 1024
SPREAD_VMEM = 61 * 1024 * 1024
NT = (((1,), (1,)), ((), ()))
TN = (((0,), (0,)), ((), ()))


def rope_tables(block, width, blocks):
    half = width // 2
    freqs = ROPE_BASE ** (-(np.arange(half, dtype=np.float64) * 2.0 / width))
    freqs = np.concatenate([freqs, freqs])
    inner = (np.arange(block) / ROPE_FACTOR)[:, None] * freqs[None, :]
    outer = (np.asarray(blocks) * block / ROPE_FACTOR)[:, None] * freqs[None, :]
    f32 = lambda x: jnp.asarray(x.astype(np.float32))
    return f32(np.stack([np.cos(inner), np.sin(inner)])), f32(np.stack([np.cos(outer), np.sin(outer)], axis=1))


def rope_of(inner_ref, outer_ref, row):
    both = outer_ref[row]
    cb, sb = both[0:1, :], both[1:2, :]
    ct, st = inner_ref[0], inner_ref[1]
    cos = ct * cb - st * sb
    sin = st * cb + ct * sb
    lane = lax.broadcasted_iota(jnp.int32, sin.shape, 1)
    return cos, jnp.where(lane < sin.shape[1] // 2, -sin, sin)


def swap_halves(x):
    return pltpu.roll(x, x.shape[1] // 2, 1)


def unrotate(y, cos, sin):
    return y * cos + swap_halves(y * sin)


def pack_kernel(kv_heads, back, axis, k_ref, v_ref, seg_ref, gain_ref, inner_ref, outer_ref, *rest):
    outs, scratch = rest[:-1], rest[-1]
    block = seg_ref.shape[1]
    per = kv_heads // len(outs)
    cos, sin = rope_of(inner_ref, outer_ref, lax.axis_index(axis) + back)
    gain = gain_ref[...]
    scratch[...] = k_ref[...].astype(jnp.float32)
    for h in range(kv_heads):
        x = scratch[pl.ds(h, block, stride=kv_heads), :]
        r = x * lax.rsqrt(jnp.mean(x * x, axis=1, keepdims=True) + EPS) * gain
        y = r * cos + swap_halves(r) * sin
        outs[h // per][pl.ds((h % per) * block, block), :] = y.astype(jnp.bfloat16)
    scratch[...] = v_ref[...].astype(jnp.float32)
    seg = jnp.broadcast_to(seg_ref[...].astype(jnp.float32) + 1.0, (16, block)).astype(jnp.bfloat16)
    for h in range(kv_heads):
        x = scratch[pl.ds(h, block, stride=kv_heads), :]
        outs[h // per][pl.ds((per + h % per) * block, block), :] = x.astype(jnp.bfloat16)
    for out in outs:
        out[pl.ds(2 * per * block, 16), :] = seg


def query_kernel(heads, back, axis, q_ref, g_ref, gain_ref, inner_ref, outer_ref, qo_ref, go_ref, scratch):
    block = q_ref.shape[0] // heads
    cos, sin = rope_of(inner_ref, outer_ref, lax.axis_index(axis) + back)
    gain = gain_ref[...]
    scratch[...] = q_ref[...].astype(jnp.float32)
    for h in range(heads):
        x = scratch[pl.ds(h, block, stride=heads), :]
        r = x * lax.rsqrt(jnp.mean(x * x, axis=1, keepdims=True) + EPS) * gain
        y = r * cos + swap_halves(r) * sin
        qo_ref[pl.ds(h * block, block), :] = y.astype(jnp.bfloat16)
    scratch[...] = g_ref[...].astype(jnp.float32)
    for h in range(heads):
        go_ref[pl.ds(h * block, block), :] = scratch[pl.ds(h, block, stride=heads), :].astype(jnp.bfloat16)


def attend_kernel(per, group, back, q_ref, g_ref, *rest):
    blocks = rest[: back + 1]
    dq_ref, own_ref = rest[back + 1 : back + 3]
    part_refs = rest[back + 3 : 2 * back + 3]
    bias_ref = rest[-1]
    block = own_ref.shape[0] // (2 * per)
    rows = group * block
    ids = blocks[0][pl.ds(2 * per * block, 16), :].astype(jnp.float32)[0:1, :]
    ids = jnp.concatenate([ids] * group, axis=1)
    for d in range(back + 1):
        key_row = blocks[d][pl.ds(2 * per * block, 16), :].astype(jnp.float32)[0:1, :]
        key_ids = jnp.broadcast_to(key_row, (block, block)).T
        key_ids = jnp.concatenate([key_ids] * group, axis=1)
        seen = key_ids == ids
        if d == 0:
            key_at = lax.broadcasted_iota(jnp.int32, (block, rows), 0)
            query_at = lax.broadcasted_iota(jnp.int32, (block, rows), 1) & (block - 1)
            seen = seen & (key_at <= query_at)
        bias_ref[pl.ds(d * block, block), :] = jnp.where(seen, 0.0, NEG)
    for h in range(per):
        q = q_ref[pl.ds(h * rows, rows), :]
        g = g_ref[pl.ds(h * rows, rows), :]
        k = jnp.concatenate([b[pl.ds(h * block, block), :] for b in blocks], axis=0)
        v = jnp.concatenate([b[pl.ds((per + h) * block, block), :] for b in blocks], axis=0)
        scores = lax.dot_general(k, q, NT, preferred_element_type=jnp.float32)
        expo = jnp.exp2(scores * (SCALE * LOG2E) + bias_ref[...])
        prob_grads = lax.dot_general(v, g, NT, preferred_element_type=jnp.float32)
        inverse = 1.0 / jnp.sum(expo, axis=0, keepdims=True)
        delta = jnp.sum(expo * prob_grads, axis=0, keepdims=True) * inverse
        probs = expo * inverse
        score_grads = (probs * (prob_grads - delta)).astype(jnp.bfloat16)
        dv = jnp.dot(probs.astype(jnp.bfloat16), g, preferred_element_type=jnp.float32)
        dk = jnp.dot(score_grads, q, preferred_element_type=jnp.float32) * SCALE
        dq = lax.dot_general(score_grads, k, TN, preferred_element_type=jnp.float32) * SCALE
        dq_ref[pl.ds(h * rows, rows), :] = dq
        own_ref[pl.ds(h * block, block), :] = dk[:block]
        own_ref[pl.ds((per + h) * block, block), :] = dv[:block]
        for d in range(1, back + 1):
            part = part_refs[d - 1]
            part[pl.ds(h * block, block), :] = dk[d * block : (d + 1) * block].astype(jnp.bfloat16)
            part[pl.ds((per + h) * block, block), :] = dv[d * block : (d + 1) * block].astype(jnp.bfloat16)


def query_back_kernel(heads, kv_heads, groups, back, axis, *rest):
    q_ref, qgain_ref, kgain_ref, inner_ref, outer_ref = rest[:5]
    rest = rest[5:]
    dq_refs, own_refs = rest[:groups], rest[groups : 2 * groups]
    msg_refs = rest[2 * groups : (3 + back) * groups]
    part_refs = rest[(3 + back) * groups : (3 + 2 * back) * groups]
    gq_ref, gains_ref, scratch = rest[-3:]
    block = q_ref.shape[0] // heads
    width = q_ref.shape[1]
    per = kv_heads // groups
    here = lax.axis_index(axis) + back
    total = jnp.zeros((block, width), jnp.float32)
    for d in range(back + 1):
        cos, sin = rope_of(inner_ref, outer_ref, here - d)
        for g in range(groups):
            for h in range(per):
                at = pl.ds(h * block, block)
                dk = own_refs[g][at, :] if d == 0 else part_refs[g * back + d - 1][at, :].astype(jnp.float32)
                k = msg_refs[g * (back + 1) + d][at, :].astype(jnp.float32)
                total = total + unrotate(dk, cos, sin) * unrotate(k, cos, sin)
    kgain = jnp.sum(total, axis=0, keepdims=True) / kgain_ref[...]
    cos, sin = rope_of(inner_ref, outer_ref, here)
    scratch[...] = q_ref[...].astype(jnp.float32)
    gain = qgain_ref[...]
    total = jnp.zeros((block, width), jnp.float32)
    each = heads // groups
    for h in range(heads):
        x = scratch[pl.ds(h, block, stride=heads), :]
        scale = lax.rsqrt(jnp.mean(x * x, axis=1, keepdims=True) + EPS)
        normed = x * scale
        dr = unrotate(dq_refs[h // each][pl.ds((h % each) * block, block), :], cos, sin)
        total = total + dr * normed
        dn = dr * gain
        dx = scale * (dn - normed * jnp.mean(dn * normed, axis=1, keepdims=True))
        scratch[pl.ds(h, block, stride=heads), :] = dx
    gq_ref[...] = scratch[...].astype(jnp.bfloat16)
    qgain = jnp.sum(total, axis=0, keepdims=True)
    gains_ref[...] = jnp.concatenate([qgain, kgain, jnp.zeros((6, width), jnp.float32)], axis=0)


def key_back_kernel(kv_heads, groups, back, axis, *rest):
    k_ref, gain_ref, inner_ref, outer_ref = rest[:4]
    own_refs = rest[4 : 4 + groups]
    got_refs = rest[4 + groups : 4 + (1 + back) * groups]
    gk_ref, gv_ref, scratch = rest[-3:]
    block = k_ref.shape[0] // kv_heads
    per = kv_heads // groups
    cos, sin = rope_of(inner_ref, outer_ref, lax.axis_index(axis) + back)
    gain = gain_ref[...]

    def total(g, row):
        at = pl.ds(row * block, block)
        value = own_refs[g][at, :]
        for d in range(back):
            value = value + got_refs[g * back + d][at, :].astype(jnp.float32)
        return value

    scratch[...] = k_ref[...].astype(jnp.float32)
    for h in range(kv_heads):
        x = scratch[pl.ds(h, block, stride=kv_heads), :]
        scale = lax.rsqrt(jnp.mean(x * x, axis=1, keepdims=True) + EPS)
        normed = x * scale
        dn = unrotate(total(h // per, h % per), cos, sin) * gain
        dx = scale * (dn - normed * jnp.mean(dn * normed, axis=1, keepdims=True))
        scratch[pl.ds(h, block, stride=kv_heads), :] = dx
    gk_ref[...] = scratch[...].astype(jnp.bfloat16)
    for h in range(kv_heads):
        scratch[pl.ds(h, block, stride=kv_heads), :] = total(h // per, per + h % per)
    gv_ref[...] = scratch[...].astype(jnp.bfloat16)


def call(kernel, outs, scratch, cost, *args):
    vmem = pl.BlockSpec(memory_space=pltpu.VMEM)
    return pl.pallas_call(
        kernel,
        out_shape=[jax.ShapeDtypeStruct(s, t) for s, t in outs],
        in_specs=[vmem] * len(args),
        out_specs=[vmem] * len(outs),
        scratch_shapes=[pltpu.VMEM(s, jnp.float32) for s in scratch],
        compiler_params=pltpu.CompilerParams(vmem_limit_bytes=VMEM_LIMIT),
        cost_estimate=pl.CostEstimate(flops=cost, bytes_accessed=1 << 20, transcendentals=0),
    )(*args)


def sum_over(x, axis, size):
    if size & (size - 1):
        return lax.psum(x, axis)
    step = 1
    while step < size:
        x = x + lax.ppermute(x, axis, [(i, i ^ step) for i in range(size)])
        step *= 2
    return x


def by_tokens(spans, parts, q_pre, k_pre, values, grad_out, segment_ids, q_gain, k_gain):
    block, heads, width = q_pre.shape[1:]
    kv_heads = k_pre.shape[2]
    group = heads // kv_heads
    groups = GROUPS
    per = kv_heads // groups
    longest = parts * block // 2
    back = min(parts - 1, (longest - 2) // block + 1)
    bf16, f32 = jnp.bfloat16, jnp.float32
    inner, outer = rope_tables(block, width, range(-back, parts))
    q2, g2 = (x.reshape(block * heads, width) for x in (q_pre, grad_out))
    k2, v2 = (x.reshape(block * kv_heads, width) for x in (k_pre, values))
    qg, kg = q_gain.reshape(1, width), k_gain.reshape(1, width)

    message = (2 * per * block + 16, width)
    own = call(
        functools.partial(pack_kernel, kv_heads, back, "seq"),
        [(message, bf16)] * groups, [(block * kv_heads, width)], 1 << 28,
        k2, v2, segment_ids, kg, inner, outer,
    )
    window = [
        [own[g]] + [lax.ppermute(own[g], "seq", [(i, i + d) for i in range(parts - d)]) for d in range(1, back + 1)]
        for g in range(groups)
    ]
    q_rot, g_rot = call(
        functools.partial(query_kernel, heads, back, "seq"),
        [((heads * block, width), bf16)] * 2, [(heads * block, width)], 1 << 29,
        q2, g2, qg, inner, outer,
    )
    dqs, owns, shares, returned = [], [], [], []
    rows = group * block * per
    for g in range(groups):
        dq, kept, *share = call(
            functools.partial(attend_kernel, per, group, back),
            [((rows, width), f32), ((2 * per * block, width), f32)] + [((2 * per * block, width), bf16)] * back,
            [((back + 1) * block, group * block)], 1 << 30,
            lax.slice_in_dim(q_rot, g * rows, (g + 1) * rows), lax.slice_in_dim(g_rot, g * rows, (g + 1) * rows),
            *window[g],
        )
        dqs.append(dq)
        owns.append(kept)
        shares += share
        returned += [
            lax.ppermute(share[d - 1], "seq", [(i + d, i) for i in range(parts - d)]) for d in range(1, back + 1)
        ]
    grad_q, gains = call(
        functools.partial(query_back_kernel, heads, kv_heads, groups, back, "seq"),
        [((heads * block, width), bf16), ((8, width), f32)], [(heads * block, width)], 1 << 29,
        q2, qg, kg, inner, outer, *dqs, *owns, *[m for w in window for m in w], *shares,
    )
    gains = sum_over(sum_over(gains, "seq", parts), "dp", spans)
    grad_k, grad_v = call(
        functools.partial(key_back_kernel, kv_heads, groups, back, "seq"),
        [((kv_heads * block, width), bf16)] * 2, [(kv_heads * block, width)], 1 << 28,
        k2, kg, inner, outer, *owns, *returned,
    )
    return (
        grad_q.reshape(q_pre.shape),
        grad_k.reshape(k_pre.shape),
        grad_v.reshape(values.shape),
        gains[0],
        gains[1],
    )


def spread_kernel(axis, parts, groups, per, a_hbm, b_hbm, *rest):
    with_ids = groups is None
    groups = groups or 1
    seg_hbm, rest = rest[:1], rest[1:]
    outs = rest[: parts * groups]
    a_in, b_in, a_f32, b_f32, seg_in, msg, in_sems, out_sems = rest[parts * groups :]
    block = seg_in.shape[1]
    heads = a_in.shape[0] // block
    me = lax.axis_index(axis)
    pairs = [(a_hbm, a_in), (b_hbm, b_in)] + ([(seg_hbm[0], seg_in)] if with_ids else [])
    loads = [pltpu.make_async_copy(src, dst, in_sems.at[i]) for i, (src, dst) in enumerate(pairs)]
    for copy in loads:
        copy.start()
    for copy, src, dst in zip(loads, (a_in, b_in), (a_f32, b_f32)):
        copy.wait()
        dst[...] = src[...].astype(jnp.float32)
    if with_ids:
        loads[2].wait()
        ids = jnp.broadcast_to(seg_in[...].astype(jnp.float32), (16, block)).astype(jnp.bfloat16)
    stores = []
    for grp in range(groups):
        for m in (*range(1, parts), 0):
            slot = grp * parts + m
            first = ((me ^ m) * groups + grp) * per
            at = 0
            for src in (a_f32, b_f32):
                for h in range(per):
                    rows = src[pl.ds(first + h, block, stride=heads), :]
                    msg[slot, pl.ds(at, block), :] = rows.astype(jnp.bfloat16)
                    at += block
            if with_ids:
                msg[slot, pl.ds(at, 16), :] = ids
            copy = pltpu.make_async_copy(msg.at[slot], outs[slot], out_sems.at[slot])
            copy.start()
            stores.append(copy)
    for copy in stores:
        copy.wait()


def turned(x):
    return x.astype(jnp.float32).T


def rotated(x, c, s):
    half = x.shape[0] // 2
    a, b = x[:half], x[half:]
    return jnp.concatenate([a * c - b * s, b * c + a * s], axis=0)


def embed(x, gain, c, s):
    scale = lax.rsqrt(jnp.sum(x * x, axis=0, keepdims=True) * (1.0 / x.shape[0]) + EPS)
    normed = x * scale
    return rotated(normed * gain, c, s).astype(jnp.bfloat16), normed, scale


def embed_back(dy, gain, c, s, normed, scale):
    dr = rotated(dy, c, -s)
    share = dr * normed
    dn = dr * gain
    mean = jnp.sum(dn * normed, axis=0, keepdims=True) * (1.0 / dy.shape[0])
    return ((scale * SCALE) * (dn - normed * mean)).astype(jnp.bfloat16), share


def rope(table_ref, b, copies):
    c, s = table_ref[b, 0], table_ref[b, 1]
    return jnp.concatenate([c] * copies, axis=1), jnp.concatenate([s] * copies, axis=1)


def gain_columns(gains_ref, row, copies):
    width = gains_ref.shape[1]
    return jnp.concatenate([jnp.broadcast_to(gains_ref[row : row + 1, :], (width, width)).T] * copies, axis=1)


def keys_kernel(axis, parts, *rest):
    msgs, table_ref, gains_ref = rest[:parts], rest[parts], rest[parts + 1]
    kt_ref, k_ref, v_ref, kn_ref, ks_ref, id_ref = rest[parts + 2 :]
    block = table_ref.shape[3]
    owned = v_ref.shape[1]
    f32, bf16 = jnp.float32, jnp.bfloat16
    me = lax.axis_index(axis)
    gain = gain_columns(gains_ref, 1, 1)
    for m in range(parts):
        b = me ^ m
        id_ref[b] = jnp.broadcast_to(msgs[m][pl.ds(2 * owned * block, 16), :].astype(f32)[0:1, :], (8, block))
        for h in range(owned):
            y, normed, scale = embed(turned(msgs[m][pl.ds(h * block, block), :]), gain, *rope(table_ref, b, 1))
            kt_ref[b, h], kn_ref[b, h], ks_ref[b, h] = y, normed, jnp.broadcast_to(scale, (8, block))
            k_ref[b, h] = turned(y).astype(bf16)
            v_ref[b, h] = msgs[m][pl.ds((owned + h) * block, block), :]


def heads_kernel(axis, parts, grp, per, group, back, *rest):
    earlier, rest = rest[: grp * parts], rest[grp * parts :]
    msgs, rest = rest[:parts], rest[parts:]
    kt_ref, k_ref, v_ref, kn_ref, ks_ref, id_ref, table_ref, gains_ref = rest[:8]
    outs, share_ref = rest[8 : 8 + parts], rest[8 + parts]
    qt_ref, g_ref, qn_ref, qs_ref, res_ref = rest[9 + parts :]
    block, width = table_ref.shape[3], gains_ref.shape[1]
    rows = group * block
    f32, bf16 = jnp.float32, jnp.bfloat16
    me = lax.axis_index(axis)
    q_gain, k_gain = gain_columns(gains_ref, 0, group), gain_columns(gains_ref, 1, 1)
    for m in range(parts):
        b = me ^ m
        for p in range(per):
            at = b * per + p
            x = turned(msgs[m][pl.ds(p * rows, rows), :])
            y, normed, scale = embed(x, q_gain, *rope(table_ref, b, group))
            qt_ref[at], qn_ref[at], qs_ref[at] = y, normed, jnp.broadcast_to(scale, (8, rows))
            g_ref[at] = msgs[m][pl.ds((per + p) * rows, rows), :]

    id_rows = [id_ref[b][0:1, :] for b in range(parts)]
    id_columns = [jnp.broadcast_to(row, (block, block)).T for row in id_rows]
    key_at = lax.broadcasted_iota(jnp.int32, (block, block), 0)
    query_at = lax.broadcasted_iota(jnp.int32, (block, block), 1)
    causal = jnp.where(key_at <= query_at, 0.0, NEG)

    def bias(key_block, query_block):
        value = jnp.where(id_columns[key_block] == id_rows[query_block], 0.0, NEG)
        if key_block == query_block:
            value = value + causal
        return jnp.concatenate([value] * group, axis=1)

    q_total = jnp.zeros((width, rows), f32)
    k_total = jnp.zeros((width, block), f32)
    for p in range(per):
        out_base = p * (group + 2) * block
        dk = [None] * parts
        dv = [None] * parts
        for b in range(parts):
            span = range(max(0, b - back), b + 1)
            qt, g = qt_ref[b * per + p], g_ref[b * per + p]
            k = jnp.concatenate([k_ref[j, grp * per + p] for j in span], axis=0)
            kt = jnp.concatenate([kt_ref[j, grp * per + p] for j in span], axis=1)
            v = jnp.concatenate([v_ref[j, grp * per + p] for j in span], axis=0)
            hidden = jnp.concatenate([bias(j, b) for j in span], axis=0)
            scores = jnp.dot(k, qt, preferred_element_type=f32)
            expo = jnp.exp2(scores * (SCALE * LOG2E) + hidden)
            prob_grads = lax.dot_general(v, g, NT, preferred_element_type=f32)
            inverse = 1.0 / jnp.sum(expo, axis=0, keepdims=True)
            delta = jnp.sum(expo * prob_grads, axis=0, keepdims=True) * inverse
            probs = expo * inverse
            score_grads = (probs * (prob_grads - delta)).astype(bf16)
            dvs = jnp.dot(probs.astype(bf16), g, preferred_element_type=f32)
            dks = lax.dot_general(qt, score_grads, NT, preferred_element_type=f32)
            dq = jnp.dot(kt, score_grads, preferred_element_type=f32)
            for i, j in enumerate(span):
                cut = slice(i * block, (i + 1) * block)
                dk[j] = dks[:, cut] if dk[j] is None else dk[j] + dks[:, cut]
                dv[j] = dvs[cut] if dv[j] is None else dv[j] + dvs[cut]
            at = b * per + p
            dx, share = embed_back(dq, q_gain, *rope(table_ref, b, group), qn_ref[at], qs_ref[at][0:1, :])
            q_total = q_total + share
            res_ref[b, pl.ds(out_base, rows), :] = turned(dx).astype(bf16)
        for b in range(parts):
            dx, share = embed_back(dk[b], k_gain, *rope(table_ref, b, 1), kn_ref[b, grp * per + p], ks_ref[b, grp * per + p][0:1, :])
            k_total = k_total + share
            res_ref[b, pl.ds(out_base + rows, block), :] = turned(dx).astype(bf16)
            res_ref[b, pl.ds(out_base + rows + block, block), :] = dv[b].astype(bf16)
    size = res_ref.shape[1]
    for m in range(parts):
        for i in range(grp):
            outs[m][pl.ds(i * size, size), :] = earlier[i * parts + m][...]
        outs[m][pl.ds(grp * size, size), :] = res_ref[me ^ m]
    ones = jnp.ones((8, rows), f32)
    exact = functools.partial(
        lax.dot_general, dimension_numbers=NT, precision=lax.Precision.HIGHEST, preferred_element_type=f32
    )
    q_share, k_share = exact(ones, q_total), exact(ones[:, :block], k_total)
    row = lax.broadcasted_iota(jnp.int32, (8, width), 0)
    share_ref[...] = jnp.where(row == 0, q_share, jnp.where(row == 1, k_share, 0.0)) * SCALE


def collect_kernel(axis, parts, groups, heads, kv_heads, *rest):
    msgs = rest[:parts]
    gq_hbm, gk_hbm, gv_hbm, q_f32, k_f32, v_f32, q_out, k_out, v_out, sems = rest[parts:]
    group = heads // kv_heads
    per = kv_heads // parts // groups
    block = q_out.shape[0] // heads
    me = lax.axis_index(axis)
    for m in range(parts):
        at = 0
        for grp in range(groups):
            for p in range(per):
                kv = ((me ^ m) * groups + grp) * per + p
                pieces = [(q_f32, kv * group + i, heads) for i in range(group)]
                pieces += [(k_f32, kv, kv_heads), (v_f32, kv, kv_heads)]
                for dst, head, stride in pieces:
                    rows = msgs[m][pl.ds(at, block), :].astype(jnp.float32)
                    dst[pl.ds(head, block, stride=stride), :] = rows
                    at += block
    stores = []
    for src, out, dst in ((q_f32, q_out, gq_hbm), (k_f32, k_out, gk_hbm), (v_f32, v_out, gv_hbm)):
        half = out.shape[0] // 2
        for i in range(2):
            cut = pl.ds(i * half, half)
            out[cut, :] = src[cut, :].astype(jnp.bfloat16)
            copy = pltpu.make_async_copy(out.at[cut], dst.at[cut], sems.at[len(stores)])
            copy.start()
            stores.append(copy)
    for copy in stores:
        copy.wait()


def call_in(kernel, ins, outs, scratch, cost, *args, limit=HEADS_VMEM):
    return pl.pallas_call(
        kernel,
        out_shape=[jax.ShapeDtypeStruct(s, t) for s, t, _ in outs],
        in_specs=[pl.BlockSpec(memory_space=m) for m in ins],
        out_specs=[pl.BlockSpec(memory_space=m) for _, _, m in outs],
        scratch_shapes=scratch,
        compiler_params=pltpu.CompilerParams(vmem_limit_bytes=limit),
        cost_estimate=pl.CostEstimate(flops=cost, bytes_accessed=1 << 20, transcendentals=0),
    )(*args)


def exchange_sum(x, axis, size, *partners):
    got = [lax.ppermute(x, axis, [(i, i ^ m) for i in range(size)]) for m in partners]
    return x + got[0] if len(got) == 1 else (x + got[0]) + (got[1] + got[2])


def by_heads(spans, parts, q_pre, k_pre, values, grad_out, segment_ids, q_gain, k_gain):
    block, heads, width = q_pre.shape[1:]
    kv_heads = k_pre.shape[2]
    group = heads // kv_heads
    groups = min(GROUPS, kv_heads // parts)
    per = kv_heads // parts // groups
    rows = group * block
    longest = parts * block // 2
    back = min(parts - 1, (longest - 2) // block + 1)
    bf16, f32, vmem, hbm = jnp.bfloat16, jnp.float32, pltpu.VMEM, pltpu.HBM
    freqs = ROPE_BASE ** (-(np.arange(width // 2, dtype=np.float64) * 2.0 / width))
    angles = (np.arange(parts * block) / ROPE_FACTOR).reshape(parts, 1, block) * freqs[:, None]
    table = jnp.asarray(np.stack([np.cos(angles), np.sin(angles)], axis=1).astype(np.float32))
    q2, g2 = (x.reshape(block * heads, width) for x in (q_pre, grad_out))
    k2, v2 = (x.reshape(block * kv_heads, width) for x in (k_pre, values))
    owned = kv_heads // parts
    kv_sent = (2 * owned * block + 16, width)
    sent = (per * 2 * rows, width)
    back_sent = (per * (group + 2) * block, width)
    dma = pltpu.SemaphoreType.DMA
    q_shape, k_shape = q2.shape, k2.shape

    def spread(count, each, shape, message, cost, *arrays):
        number = parts * (count or 1)
        return call_in(
            functools.partial(spread_kernel, "seq", parts, count, each),
            [hbm] * len(arrays), [(message, bf16, hbm)] * number,
            [vmem(shape, bf16), vmem(shape, bf16), vmem(shape, f32), vmem(shape, f32), vmem((1, block), jnp.int32)]
            + [vmem((number, *message), bf16), dma((len(arrays),)), dma((number,))],
            cost, *arrays, limit=SPREAD_VMEM,
        )

    xor = lambda m, size: [(i, i ^ m) for i in range(size)]
    send = lambda out: [out[0]] + [lax.ppermute(out[m], "seq", xor(m, parts)) for m in range(1, parts)]
    kv_messages = spread(None, owned, k_shape, kv_sent, 1 << 20, k2, v2, segment_ids)
    kv_arrived = send(kv_messages)
    messages = spread(groups, per * group, q_shape, sent, 1 << 33, q2, g2, kv_messages[0])
    arrived = [send(messages[grp * parts : (grp + 1) * parts]) for grp in range(groups)]
    gains = jnp.concatenate([q_gain[None], k_gain[None], jnp.zeros((6, width), f32)], axis=0)
    held = (parts, owned)
    keys = call_in(
        functools.partial(keys_kernel, "seq", parts), [vmem] * (parts + 2),
        [((*held, width, block), bf16, vmem), ((*held, block, width), bf16, vmem), ((*held, block, width), bf16, vmem)]
        + [((*held, width, block), f32, vmem), ((*held, 8, block), f32, vmem), ((parts, 8, block), f32, vmem)],
        [], 1 << 33, *kv_arrived, table, gains,
    )
    results, shares = [], []
    for grp in range(groups):
        inputs = [*results, *arrived[grp], *keys, table, gains]
        *made, share = call_in(
            functools.partial(heads_kernel, "seq", parts, grp, per, group, back),
            [vmem] * len(inputs),
            [(((grp + 1) * back_sent[0], width), bf16, vmem)] * parts + [((8, width), f32, vmem)],
            [vmem((parts * per, width, rows), bf16), vmem((parts * per, rows, width), bf16)]
            + [vmem((parts * per, width, rows), f32), vmem((parts * per, 8, rows), f32), vmem((parts, *back_sent), bf16)],
            1 << 34, *inputs,
        )
        results = made
        shares.append(share)
    first, second, third = (lax.ppermute(results[m], "seq", xor(m, parts)) for m in (1, 2, 3))
    total = exchange_sum(functools.reduce(jnp.add, shares), "dp", spans, 1)
    total = exchange_sum(exchange_sum(total, "dp", spans, 2), "dp", spans, 4)
    total, first, second = lax.optimization_barrier((total, first, second))
    total = exchange_sum(total, "seq", parts, 1, 2, 3)
    grad_q, grad_k, grad_v = call_in(
        functools.partial(collect_kernel, "seq", parts, groups, heads, kv_heads),
        [vmem] * parts, [(q_shape, bf16, hbm), (k_shape, bf16, hbm), (k_shape, bf16, hbm)],
        [vmem(q_shape, f32), vmem(k_shape, f32), vmem(k_shape, f32)]
        + [vmem(q_shape, bf16), vmem(k_shape, bf16), vmem(k_shape, bf16), dma((6,))],
        1 << 20, results[0], first, second, third,
    )
    return (
        grad_q.reshape(q_pre.shape), grad_k.reshape(k_pre.shape), grad_v.reshape(values.shape), total[0], total[1],
    )


def solution(mesh):
    tokens = P("dp", "seq", None, None)
    spans, parts = mesh.shape["dp"], mesh.shape["seq"]
    body = by_heads if (spans, parts) == (8, 4) else by_tokens
    return jax.shard_map(
        functools.partial(body, spans, parts),
        mesh=mesh,
        in_specs=(tokens, tokens, tokens, tokens, P("dp", "seq"), P(), P()),
        out_specs=(tokens, tokens, tokens, P(), P()),
        check_vma=False,
    )
```

```python
import functools

import jax
import jax.numpy as jnp
import numpy as np
from jax import lax
from jax.experimental import pallas as pl
from jax.experimental.pallas import tpu as pltpu
from jax.sharding import PartitionSpec as P

PRESCALE = 168
EPS = 1e-06
ROPE_BASE = 1000000.0
ROPE_FACTOR = 8.0
GROUPS = 2
PIECES = 4
NEG = -1e30
SCALE = float(PRESCALE) ** (-0.5)
LOG2E = 1.4426950408889634
VMEM_LIMIT = 48 * 1024 * 1024
HEADS_VMEM = 24 * 1024 * 1024
SPREAD_VMEM = 61 * 1024 * 1024
NT = (((1,), (1,)), ((), ()))
TN = (((0,), (0,)), ((), ()))


def rope_tables(block, width, blocks):
    half = width // 2
    freqs = ROPE_BASE ** (-(np.arange(half, dtype=np.float64) * 2.0 / width))
    freqs = np.concatenate([freqs, freqs])
    inner = (np.arange(block) / ROPE_FACTOR)[:, None] * freqs[None, :]
    outer = (np.asarray(blocks) * block / ROPE_FACTOR)[:, None] * freqs[None, :]
    f32 = lambda x: jnp.asarray(x.astype(np.float32))
    return f32(np.stack([np.cos(inner), np.sin(inner)])), f32(np.stack([np.cos(outer), np.sin(outer)], axis=1))


def rope_of(inner_ref, outer_ref, row):
    both = outer_ref[row]
    cb, sb = both[0:1, :], both[1:2, :]
    ct, st = inner_ref[0], inner_ref[1]
    cos = ct * cb - st * sb
    sin = st * cb + ct * sb
    lane = lax.broadcasted_iota(jnp.int32, sin.shape, 1)
    return cos, jnp.where(lane < sin.shape[1] // 2, -sin, sin)


def swap_halves(x):
    return pltpu.roll(x, x.shape[1] // 2, 1)


def unrotate(y, cos, sin):
    return y * cos + swap_halves(y * sin)


def pack_kernel(kv_heads, back, axis, k_ref, v_ref, seg_ref, gain_ref, inner_ref, outer_ref, *rest):
    outs, scratch = rest[:-1], rest[-1]
    block = seg_ref.shape[1]
    per = kv_heads // len(outs)
    cos, sin = rope_of(inner_ref, outer_ref, lax.axis_index(axis) + back)
    gain = gain_ref[...]
    scratch[...] = k_ref[...].astype(jnp.float32)
    for h in range(kv_heads):
        x = scratch[pl.ds(h, block, stride=kv_heads), :]
        r = x * lax.rsqrt(jnp.mean(x * x, axis=1, keepdims=True) + EPS) * gain
        y = r * cos + swap_halves(r) * sin
        outs[h // per][pl.ds((h % per) * block, block), :] = y.astype(jnp.bfloat16)
    scratch[...] = v_ref[...].astype(jnp.float32)
    seg = jnp.broadcast_to(seg_ref[...].astype(jnp.float32) + 1.0, (16, block)).astype(jnp.bfloat16)
    for h in range(kv_heads):
        x = scratch[pl.ds(h, block, stride=kv_heads), :]
        outs[h // per][pl.ds((per + h % per) * block, block), :] = x.astype(jnp.bfloat16)
    for out in outs:
        out[pl.ds(2 * per * block, 16), :] = seg


def query_kernel(heads, back, axis, q_ref, g_ref, gain_ref, inner_ref, outer_ref, qo_ref, go_ref, scratch):
    block = q_ref.shape[0] // heads
    cos, sin = rope_of(inner_ref, outer_ref, lax.axis_index(axis) + back)
    gain = gain_ref[...]
    scratch[...] = q_ref[...].astype(jnp.float32)
    for h in range(heads):
        x = scratch[pl.ds(h, block, stride=heads), :]
        r = x * lax.rsqrt(jnp.mean(x * x, axis=1, keepdims=True) + EPS) * gain
        y = r * cos + swap_halves(r) * sin
        qo_ref[pl.ds(h * block, block), :] = y.astype(jnp.bfloat16)
    scratch[...] = g_ref[...].astype(jnp.float32)
    for h in range(heads):
        go_ref[pl.ds(h * block, block), :] = scratch[pl.ds(h, block, stride=heads), :].astype(jnp.bfloat16)


def attend_kernel(per, group, back, q_ref, g_ref, *rest):
    blocks = rest[: back + 1]
    dq_ref, own_ref = rest[back + 1 : back + 3]
    part_refs = rest[back + 3 : 2 * back + 3]
    bias_ref = rest[-1]
    block = own_ref.shape[0] // (2 * per)
    rows = group * block
    ids = blocks[0][pl.ds(2 * per * block, 16), :].astype(jnp.float32)[0:1, :]
    ids = jnp.concatenate([ids] * group, axis=1)
    for d in range(back + 1):
        key_row = blocks[d][pl.ds(2 * per * block, 16), :].astype(jnp.float32)[0:1, :]
        key_ids = jnp.broadcast_to(key_row, (block, block)).T
        key_ids = jnp.concatenate([key_ids] * group, axis=1)
        seen = key_ids == ids
        if d == 0:
            key_at = lax.broadcasted_iota(jnp.int32, (block, rows), 0)
            query_at = lax.broadcasted_iota(jnp.int32, (block, rows), 1) & (block - 1)
            seen = seen & (key_at <= query_at)
        bias_ref[pl.ds(d * block, block), :] = jnp.where(seen, 0.0, NEG)
    for h in range(per):
        q = q_ref[pl.ds(h * rows, rows), :]
        g = g_ref[pl.ds(h * rows, rows), :]
        k = jnp.concatenate([b[pl.ds(h * block, block), :] for b in blocks], axis=0)
        v = jnp.concatenate([b[pl.ds((per + h) * block, block), :] for b in blocks], axis=0)
        scores = lax.dot_general(k, q, NT, preferred_element_type=jnp.float32)
        expo = jnp.exp2(scores * (SCALE * LOG2E) + bias_ref[...])
        prob_grads = lax.dot_general(v, g, NT, preferred_element_type=jnp.float32)
        inverse = 1.0 / jnp.sum(expo, axis=0, keepdims=True)
        delta = jnp.sum(expo * prob_grads, axis=0, keepdims=True) * inverse
        probs = expo * inverse
        score_grads = (probs * (prob_grads - delta)).astype(jnp.bfloat16)
        dv = jnp.dot(probs.astype(jnp.bfloat16), g, preferred_element_type=jnp.float32)
        dk = jnp.dot(score_grads, q, preferred_element_type=jnp.float32) * SCALE
        dq = lax.dot_general(score_grads, k, TN, preferred_element_type=jnp.float32) * SCALE
        dq_ref[pl.ds(h * rows, rows), :] = dq
        own_ref[pl.ds(h * block, block), :] = dk[:block]
        own_ref[pl.ds((per + h) * block, block), :] = dv[:block]
        for d in range(1, back + 1):
            part = part_refs[d - 1]
            part[pl.ds(h * block, block), :] = dk[d * block : (d + 1) * block].astype(jnp.bfloat16)
            part[pl.ds((per + h) * block, block), :] = dv[d * block : (d + 1) * block].astype(jnp.bfloat16)


def query_back_kernel(heads, kv_heads, groups, back, axis, *rest):
    q_ref, qgain_ref, kgain_ref, inner_ref, outer_ref = rest[:5]
    rest = rest[5:]
    dq_refs, own_refs = rest[:groups], rest[groups : 2 * groups]
    msg_refs = rest[2 * groups : (3 + back) * groups]
    part_refs = rest[(3 + back) * groups : (3 + 2 * back) * groups]
    gq_ref, gains_ref, scratch = rest[-3:]
    block = q_ref.shape[0] // heads
    width = q_ref.shape[1]
    per = kv_heads // groups
    here = lax.axis_index(axis) + back
    total = jnp.zeros((block, width), jnp.float32)
    for d in range(back + 1):
        cos, sin = rope_of(inner_ref, outer_ref, here - d)
        for g in range(groups):
            for h in range(per):
                at = pl.ds(h * block, block)
                dk = own_refs[g][at, :] if d == 0 else part_refs[g * back + d - 1][at, :].astype(jnp.float32)
                k = msg_refs[g * (back + 1) + d][at, :].astype(jnp.float32)
                total = total + unrotate(dk, cos, sin) * unrotate(k, cos, sin)
    kgain = jnp.sum(total, axis=0, keepdims=True) / kgain_ref[...]
    cos, sin = rope_of(inner_ref, outer_ref, here)
    scratch[...] = q_ref[...].astype(jnp.float32)
    gain = qgain_ref[...]
    total = jnp.zeros((block, width), jnp.float32)
    each = heads // groups
    for h in range(heads):
        x = scratch[pl.ds(h, block, stride=heads), :]
        scale = lax.rsqrt(jnp.mean(x * x, axis=1, keepdims=True) + EPS)
        normed = x * scale
        dr = unrotate(dq_refs[h // each][pl.ds((h % each) * block, block), :], cos, sin)
        total = total + dr * normed
        dn = dr * gain
        dx = scale * (dn - normed * jnp.mean(dn * normed, axis=1, keepdims=True))
        scratch[pl.ds(h, block, stride=heads), :] = dx
    gq_ref[...] = scratch[...].astype(jnp.bfloat16)
    qgain = jnp.sum(total, axis=0, keepdims=True)
    gains_ref[...] = jnp.concatenate([qgain, kgain, jnp.zeros((6, width), jnp.float32)], axis=0)


def key_back_kernel(kv_heads, groups, back, axis, *rest):
    k_ref, gain_ref, inner_ref, outer_ref = rest[:4]
    own_refs = rest[4 : 4 + groups]
    got_refs = rest[4 + groups : 4 + (1 + back) * groups]
    gk_ref, gv_ref, scratch = rest[-3:]
    block = k_ref.shape[0] // kv_heads
    per = kv_heads // groups
    cos, sin = rope_of(inner_ref, outer_ref, lax.axis_index(axis) + back)
    gain = gain_ref[...]

    def total(g, row):
        at = pl.ds(row * block, block)
        value = own_refs[g][at, :]
        for d in range(back):
            value = value + got_refs[g * back + d][at, :].astype(jnp.float32)
        return value

    scratch[...] = k_ref[...].astype(jnp.float32)
    for h in range(kv_heads):
        x = scratch[pl.ds(h, block, stride=kv_heads), :]
        scale = lax.rsqrt(jnp.mean(x * x, axis=1, keepdims=True) + EPS)
        normed = x * scale
        dn = unrotate(total(h // per, h % per), cos, sin) * gain
        dx = scale * (dn - normed * jnp.mean(dn * normed, axis=1, keepdims=True))
        scratch[pl.ds(h, block, stride=kv_heads), :] = dx
    gk_ref[...] = scratch[...].astype(jnp.bfloat16)
    for h in range(kv_heads):
        scratch[pl.ds(h, block, stride=kv_heads), :] = total(h // per, per + h % per)
    gv_ref[...] = scratch[...].astype(jnp.bfloat16)


def call(kernel, outs, scratch, cost, *args):
    vmem = pl.BlockSpec(memory_space=pltpu.VMEM)
    return pl.pallas_call(
        kernel,
        out_shape=[jax.ShapeDtypeStruct(s, t) for s, t in outs],
        in_specs=[vmem] * len(args),
        out_specs=[vmem] * len(outs),
        scratch_shapes=[pltpu.VMEM(s, jnp.float32) for s in scratch],
        compiler_params=pltpu.CompilerParams(vmem_limit_bytes=VMEM_LIMIT),
        cost_estimate=pl.CostEstimate(flops=cost, bytes_accessed=1 << 20, transcendentals=0),
    )(*args)


def sum_over(x, axis, size):
    if size & (size - 1):
        return lax.psum(x, axis)
    step = 1
    while step < size:
        x = x + lax.ppermute(x, axis, [(i, i ^ step) for i in range(size)])
        step *= 2
    return x


def by_tokens(spans, parts, q_pre, k_pre, values, grad_out, segment_ids, q_gain, k_gain):
    block, heads, width = q_pre.shape[1:]
    kv_heads = k_pre.shape[2]
    group = heads // kv_heads
    groups = GROUPS
    per = kv_heads // groups
    longest = parts * block // 2
    back = min(parts - 1, (longest - 2) // block + 1)
    bf16, f32 = jnp.bfloat16, jnp.float32
    inner, outer = rope_tables(block, width, range(-back, parts))
    q2, g2 = (x.reshape(block * heads, width) for x in (q_pre, grad_out))
    k2, v2 = (x.reshape(block * kv_heads, width) for x in (k_pre, values))
    qg, kg = q_gain.reshape(1, width), k_gain.reshape(1, width)

    message = (2 * per * block + 16, width)
    own = call(
        functools.partial(pack_kernel, kv_heads, back, "seq"),
        [(message, bf16)] * groups, [(block * kv_heads, width)], 1 << 28,
        k2, v2, segment_ids, kg, inner, outer,
    )
    window = [
        [own[g]] + [lax.ppermute(own[g], "seq", [(i, i + d) for i in range(parts - d)]) for d in range(1, back + 1)]
        for g in range(groups)
    ]
    q_rot, g_rot = call(
        functools.partial(query_kernel, heads, back, "seq"),
        [((heads * block, width), bf16)] * 2, [(heads * block, width)], 1 << 29,
        q2, g2, qg, inner, outer,
    )
    dqs, owns, shares, returned = [], [], [], []
    rows = group * block * per
    for g in range(groups):
        dq, kept, *share = call(
            functools.partial(attend_kernel, per, group, back),
            [((rows, width), f32), ((2 * per * block, width), f32)] + [((2 * per * block, width), bf16)] * back,
            [((back + 1) * block, group * block)], 1 << 30,
            lax.slice_in_dim(q_rot, g * rows, (g + 1) * rows), lax.slice_in_dim(g_rot, g * rows, (g + 1) * rows),
            *window[g],
        )
        dqs.append(dq)
        owns.append(kept)
        shares += share
        returned += [
            lax.ppermute(share[d - 1], "seq", [(i + d, i) for i in range(parts - d)]) for d in range(1, back + 1)
        ]
    grad_q, gains = call(
        functools.partial(query_back_kernel, heads, kv_heads, groups, back, "seq"),
        [((heads * block, width), bf16), ((8, width), f32)], [(heads * block, width)], 1 << 29,
        q2, qg, kg, inner, outer, *dqs, *owns, *[m for w in window for m in w], *shares,
    )
    gains = sum_over(sum_over(gains, "seq", parts), "dp", spans)
    grad_k, grad_v = call(
        functools.partial(key_back_kernel, kv_heads, groups, back, "seq"),
        [((kv_heads * block, width), bf16)] * 2, [(kv_heads * block, width)], 1 << 28,
        k2, kg, inner, outer, *owns, *returned,
    )
    return (
        grad_q.reshape(q_pre.shape),
        grad_k.reshape(k_pre.shape),
        grad_v.reshape(values.shape),
        gains[0],
        gains[1],
    )


def spread_kernel(axis, parts, groups, per, a_hbm, b_hbm, *rest):
    with_ids = groups is None
    groups = groups or 1
    seg_hbm, rest = rest[:1], rest[1:]
    outs = rest[: parts * groups]
    a_in, b_in, a_f32, b_f32, seg_in, msg, in_sems, out_sems = rest[parts * groups :]
    block = seg_in.shape[1]
    heads = a_in.shape[0] // block
    me = lax.axis_index(axis)
    pairs = [(a_hbm, a_in), (b_hbm, b_in)] + ([(seg_hbm[0], seg_in)] if with_ids else [])
    loads = [pltpu.make_async_copy(src, dst, in_sems.at[i]) for i, (src, dst) in enumerate(pairs)]
    for copy in loads:
        copy.start()
    for copy, src, dst in zip(loads, (a_in, b_in), (a_f32, b_f32)):
        copy.wait()
        dst[...] = src[...].astype(jnp.float32)
    if with_ids:
        loads[2].wait()
        ids = jnp.broadcast_to(seg_in[...].astype(jnp.float32), (16, block)).astype(jnp.bfloat16)
    stores = []
    for grp in range(groups):
        for m in (*range(1, parts), 0):
            slot = grp * parts + m
            first = ((me ^ m) * groups + grp) * per
            at = 0
            for src in (a_f32, b_f32):
                for h in range(per):
                    rows = src[pl.ds(first + h, block, stride=heads), :]
                    msg[slot, pl.ds(at, block), :] = rows.astype(jnp.bfloat16)
                    at += block
            if with_ids:
                msg[slot, pl.ds(at, 16), :] = ids
            copy = pltpu.make_async_copy(msg.at[slot], outs[slot], out_sems.at[slot])
            copy.start()
            stores.append(copy)
    for copy in stores:
        copy.wait()


def turned(x):
    return x.astype(jnp.float32).T


def rotated(x, c, s):
    half = x.shape[0] // 2
    a, b = x[:half], x[half:]
    return jnp.concatenate([a * c - b * s, b * c + a * s], axis=0)


def embed(x, gain, c, s):
    scale = lax.rsqrt(jnp.sum(x * x, axis=0, keepdims=True) * (1.0 / x.shape[0]) + EPS)
    normed = x * scale
    return rotated(normed * gain, c, s).astype(jnp.bfloat16), normed, scale


def embed_back(dy, gain, c, s, normed, scale):
    dr = rotated(dy, c, -s)
    share = dr * normed
    dn = dr * gain
    mean = jnp.sum(dn * normed, axis=0, keepdims=True) * (1.0 / dy.shape[0])
    return ((scale * SCALE) * (dn - normed * mean)).astype(jnp.bfloat16), share


def rope(table_ref, b, copies):
    c, s = table_ref[b, 0], table_ref[b, 1]
    return jnp.concatenate([c] * copies, axis=1), jnp.concatenate([s] * copies, axis=1)


def gain_columns(gains_ref, row, copies):
    width = gains_ref.shape[1]
    return jnp.concatenate([jnp.broadcast_to(gains_ref[row : row + 1, :], (width, width)).T] * copies, axis=1)


def keys_kernel(axis, parts, *rest):
    msgs, table_ref, gains_ref = rest[:parts], rest[parts], rest[parts + 1]
    kt_ref, k_ref, v_ref, kn_ref, ks_ref, id_ref = rest[parts + 2 :]
    block = table_ref.shape[3]
    owned = v_ref.shape[1]
    f32, bf16 = jnp.float32, jnp.bfloat16
    me = lax.axis_index(axis)
    gain = gain_columns(gains_ref, 1, 1)
    for m in range(parts):
        b = me ^ m
        id_ref[b] = jnp.broadcast_to(msgs[m][pl.ds(2 * owned * block, 16), :].astype(f32)[0:1, :], (8, block))
        for h in range(owned):
            y, normed, scale = embed(turned(msgs[m][pl.ds(h * block, block), :]), gain, *rope(table_ref, b, 1))
            kt_ref[b, h], kn_ref[b, h], ks_ref[b, h] = y, normed, jnp.broadcast_to(scale, (8, block))
            k_ref[b, h] = turned(y).astype(bf16)
            v_ref[b, h] = msgs[m][pl.ds((owned + h) * block, block), :]


def heads_kernel(axis, parts, grp, per, group, back, *rest):
    earlier, rest = rest[: grp * parts], rest[grp * parts :]
    msgs, rest = rest[:parts], rest[parts:]
    kt_ref, k_ref, v_ref, kn_ref, ks_ref, id_ref, table_ref, gains_ref = rest[:8]
    outs, share_ref = rest[8 : 8 + parts], rest[8 + parts]
    qt_ref, g_ref, qn_ref, qs_ref, res_ref = rest[9 + parts :]
    block, width = table_ref.shape[3], gains_ref.shape[1]
    rows = group * block
    f32, bf16 = jnp.float32, jnp.bfloat16
    me = lax.axis_index(axis)
    q_gain, k_gain = gain_columns(gains_ref, 0, group), gain_columns(gains_ref, 1, 1)
    for m in range(parts):
        b = me ^ m
        for p in range(per):
            at = b * per + p
            x = turned(msgs[m][pl.ds(p * rows, rows), :])
            y, normed, scale = embed(x, q_gain, *rope(table_ref, b, group))
            qt_ref[at], qn_ref[at], qs_ref[at] = y, normed, jnp.broadcast_to(scale, (8, rows))
            g_ref[at] = msgs[m][pl.ds((per + p) * rows, rows), :]

    id_rows = [id_ref[b][0:1, :] for b in range(parts)]
    id_columns = [jnp.broadcast_to(row, (block, block)).T for row in id_rows]
    key_at = lax.broadcasted_iota(jnp.int32, (block, block), 0)
    query_at = lax.broadcasted_iota(jnp.int32, (block, block), 1)
    causal = jnp.where(key_at <= query_at, 0.0, NEG)

    def bias(key_block, query_block):
        value = jnp.where(id_columns[key_block] == id_rows[query_block], 0.0, NEG)
        if key_block == query_block:
            value = value + causal
        return jnp.concatenate([value] * group, axis=1)

    q_total = jnp.zeros((width, rows), f32)
    k_total = jnp.zeros((width, block), f32)
    for p in range(per):
        out_base = p * (group + 2) * block
        dk = [None] * parts
        dv = [None] * parts
        for b in range(parts):
            span = range(max(0, b - back), b + 1)
            qt, g = qt_ref[b * per + p], g_ref[b * per + p]
            k = jnp.concatenate([k_ref[j, grp * per + p] for j in span], axis=0)
            kt = jnp.concatenate([kt_ref[j, grp * per + p] for j in span], axis=1)
            v = jnp.concatenate([v_ref[j, grp * per + p] for j in span], axis=0)
            hidden = jnp.concatenate([bias(j, b) for j in span], axis=0)
            scores = jnp.dot(k, qt, preferred_element_type=f32)
            expo = jnp.exp2(scores * (SCALE * LOG2E) + hidden)
            prob_grads = lax.dot_general(v, g, NT, preferred_element_type=f32)
            inverse = 1.0 / jnp.sum(expo, axis=0, keepdims=True)
            delta = jnp.sum(expo * prob_grads, axis=0, keepdims=True) * inverse
            probs = expo * inverse
            score_grads = (probs * (prob_grads - delta)).astype(bf16)
            dvs = jnp.dot(probs.astype(bf16), g, preferred_element_type=f32)
            dks = lax.dot_general(qt, score_grads, NT, preferred_element_type=f32)
            dq = jnp.dot(kt, score_grads, preferred_element_type=f32)
            for i, j in enumerate(span):
                cut = slice(i * block, (i + 1) * block)
                dk[j] = dks[:, cut] if dk[j] is None else dk[j] + dks[:, cut]
                dv[j] = dvs[cut] if dv[j] is None else dv[j] + dvs[cut]
            at = b * per + p
            dx, share = embed_back(dq, q_gain, *rope(table_ref, b, group), qn_ref[at], qs_ref[at][0:1, :])
            q_total = q_total + share
            res_ref[b, pl.ds(out_base, rows), :] = turned(dx).astype(bf16)
        for b in range(parts):
            dx, share = embed_back(dk[b], k_gain, *rope(table_ref, b, 1), kn_ref[b, grp * per + p], ks_ref[b, grp * per + p][0:1, :])
            k_total = k_total + share
            res_ref[b, pl.ds(out_base + rows, block), :] = turned(dx).astype(bf16)
            res_ref[b, pl.ds(out_base + rows + block, block), :] = dv[b].astype(bf16)
    size = res_ref.shape[1]
    for m in range(parts):
        for i in range(grp):
            outs[m][pl.ds(i * size, size), :] = earlier[i * parts + m][...]
        outs[m][pl.ds(grp * size, size), :] = res_ref[me ^ m]
    ones = jnp.ones((8, rows), f32)
    exact = functools.partial(
        lax.dot_general, dimension_numbers=NT, precision=lax.Precision.HIGHEST, preferred_element_type=f32
    )
    q_share, k_share = exact(ones, q_total), exact(ones[:, :block], k_total)
    row = lax.broadcasted_iota(jnp.int32, (8, width), 0)
    share_ref[...] = jnp.where(row == 0, q_share, jnp.where(row == 1, k_share, 0.0)) * SCALE


def collect_kernel(axis, parts, groups, heads, kv_heads, *rest):
    msgs = rest[:parts]
    gq_hbm, gk_hbm, gv_hbm, q_f32, k_f32, v_f32, q_out, k_out, v_out, sems = rest[parts:]
    group = heads // kv_heads
    per = kv_heads // parts // groups
    block = q_out.shape[0] // heads
    me = lax.axis_index(axis)
    arrays = ((q_f32, q_out, gq_hbm, heads), (k_f32, k_out, gk_hbm, kv_heads), (v_f32, v_out, gv_hbm, kv_heads))
    tokens = block // PIECES
    stores = []
    for piece in range(PIECES):
        start = piece * tokens
        for m in range(parts):
            at = start
            for grp in range(groups):
                for p in range(per):
                    kv = ((me ^ m) * groups + grp) * per + p
                    places = [(0, kv * group + i) for i in range(group)] + [(1, kv), (2, kv)]
                    for which, head in places:
                        dst, _, _, stride = arrays[which]
                        rows = msgs[m][pl.ds(at, tokens), :].astype(jnp.float32)
                        dst[pl.ds(start * stride + head, tokens, stride=stride), :] = rows
                        at += block
        for src, out, dst, stride in arrays:
            cut = pl.ds(start * stride, tokens * stride)
            out[cut, :] = src[cut, :].astype(jnp.bfloat16)
            copy = pltpu.make_async_copy(out.at[cut], dst.at[cut], sems.at[len(stores)])
            copy.start()
            stores.append(copy)
    for copy in stores:
        copy.wait()


def call_in(kernel, ins, outs, scratch, cost, *args, limit=HEADS_VMEM):
    return pl.pallas_call(
        kernel,
        out_shape=[jax.ShapeDtypeStruct(s, t) for s, t, _ in outs],
        in_specs=[pl.BlockSpec(memory_space=m) for m in ins],
        out_specs=[pl.BlockSpec(memory_space=m) for _, _, m in outs],
        scratch_shapes=scratch,
        compiler_params=pltpu.CompilerParams(vmem_limit_bytes=limit),
        cost_estimate=pl.CostEstimate(flops=cost, bytes_accessed=1 << 20, transcendentals=0),
    )(*args)


def exchange_sum(x, axis, size, *partners):
    got = [lax.ppermute(x, axis, [(i, i ^ m) for i in range(size)]) for m in partners]
    return x + got[0] if len(got) == 1 else (x + got[0]) + (got[1] + got[2])


def by_heads(spans, parts, q_pre, k_pre, values, grad_out, segment_ids, q_gain, k_gain):
    block, heads, width = q_pre.shape[1:]
    kv_heads = k_pre.shape[2]
    group = heads // kv_heads
    groups = min(GROUPS, kv_heads // parts)
    per = kv_heads // parts // groups
    rows = group * block
    longest = parts * block // 2
    back = min(parts - 1, (longest - 2) // block + 1)
    bf16, f32, vmem, hbm = jnp.bfloat16, jnp.float32, pltpu.VMEM, pltpu.HBM
    freqs = ROPE_BASE ** (-(np.arange(width // 2, dtype=np.float64) * 2.0 / width))
    angles = (np.arange(parts * block) / ROPE_FACTOR).reshape(parts, 1, block) * freqs[:, None]
    table = jnp.asarray(np.stack([np.cos(angles), np.sin(angles)], axis=1).astype(np.float32))
    q2, g2 = (x.reshape(block * heads, width) for x in (q_pre, grad_out))
    k2, v2 = (x.reshape(block * kv_heads, width) for x in (k_pre, values))
    owned = kv_heads // parts
    kv_sent = (2 * owned * block + 16, width)
    sent = (per * 2 * rows, width)
    back_sent = (per * (group + 2) * block, width)
    dma = pltpu.SemaphoreType.DMA
    q_shape, k_shape = q2.shape, k2.shape

    def spread(count, each, shape, message, cost, *arrays):
        number = parts * (count or 1)
        return call_in(
            functools.partial(spread_kernel, "seq", parts, count, each),
            [hbm] * len(arrays), [(message, bf16, hbm)] * number,
            [vmem(shape, bf16), vmem(shape, bf16), vmem(shape, f32), vmem(shape, f32), vmem((1, block), jnp.int32)]
            + [vmem((number, *message), bf16), dma((len(arrays),)), dma((number,))],
            cost, *arrays, limit=SPREAD_VMEM,
        )

    xor = lambda m, size: [(i, i ^ m) for i in range(size)]
    send = lambda out: [out[0]] + [lax.ppermute(out[m], "seq", xor(m, parts)) for m in range(1, parts)]
    kv_messages = spread(None, owned, k_shape, kv_sent, 1 << 20, k2, v2, segment_ids)
    kv_arrived = send(kv_messages)
    messages = spread(groups, per * group, q_shape, sent, 1 << 33, q2, g2, kv_messages[0])
    arrived = [send(messages[grp * parts : (grp + 1) * parts]) for grp in range(groups)]
    gains = jnp.concatenate([q_gain[None], k_gain[None], jnp.zeros((6, width), f32)], axis=0)
    held = (parts, owned)
    keys = call_in(
        functools.partial(keys_kernel, "seq", parts), [vmem] * (parts + 2),
        [((*held, width, block), bf16, vmem), ((*held, block, width), bf16, vmem), ((*held, block, width), bf16, vmem)]
        + [((*held, width, block), f32, vmem), ((*held, 8, block), f32, vmem), ((parts, 8, block), f32, vmem)],
        [], 1 << 33, *kv_arrived, table, gains,
    )
    results, shares = [], []
    for grp in range(groups):
        inputs = [*results, *arrived[grp], *keys, table, gains]
        *made, share = call_in(
            functools.partial(heads_kernel, "seq", parts, grp, per, group, back),
            [vmem] * len(inputs),
            [(((grp + 1) * back_sent[0], width), bf16, vmem)] * parts + [((8, width), f32, vmem)],
            [vmem((parts * per, width, rows), bf16), vmem((parts * per, rows, width), bf16)]
            + [vmem((parts * per, width, rows), f32), vmem((parts * per, 8, rows), f32), vmem((parts, *back_sent), bf16)],
            1 << 34, *inputs,
        )
        results = made
        shares.append(share)
    go = lambda m: lax.ppermute(results[m], "seq", xor(m, parts))
    total = functools.reduce(jnp.add, shares)
    first, second, third = go(1), go(2), go(3)
    total = exchange_sum(total, "seq", parts, 1, 2, 3)
    total = exchange_sum(exchange_sum(exchange_sum(total, "dp", spans, 1), "dp", spans, 2), "dp", spans, 4)
    grad_q, grad_k, grad_v = call_in(
        functools.partial(collect_kernel, "seq", parts, groups, heads, kv_heads),
        [vmem] * parts, [(q_shape, bf16, hbm), (k_shape, bf16, hbm), (k_shape, bf16, hbm)],
        [vmem(q_shape, f32), vmem(k_shape, f32), vmem(k_shape, f32)]
        + [vmem(q_shape, bf16), vmem(k_shape, bf16), vmem(k_shape, bf16), dma((3 * PIECES,))],
        1 << 20, results[0], first, second, third,
    )
    return (
        grad_q.reshape(q_pre.shape), grad_k.reshape(k_pre.shape), grad_v.reshape(values.shape), total[0], total[1],
    )


def solution(mesh):
    tokens = P("dp", "seq", None, None)
    spans, parts = mesh.shape["dp"], mesh.shape["seq"]
    body = by_heads if (spans, parts) == (8, 4) else by_tokens
    return jax.shard_map(
        functools.partial(body, spans, parts),
        mesh=mesh,
        in_specs=(tokens, tokens, tokens, tokens, P("dp", "seq"), P(), P()),
        out_specs=(tokens, tokens, tokens, P(), P()),
        check_vma=False,
    )
```

```python
import functools

import jax
import jax.numpy as jnp
import numpy as np
from jax import lax
from jax.experimental import pallas as pl
from jax.experimental.pallas import tpu as pltpu
from jax.sharding import PartitionSpec as P

PRESCALE = 168
EPS = 1e-06
ROPE_BASE = 1000000.0
ROPE_FACTOR = 8.0
GROUPS = 2
PIECES = 4
NEG = -1e30
SCALE = float(PRESCALE) ** (-0.5)
LOG2E = 1.4426950408889634
VMEM_LIMIT = 48 * 1024 * 1024
HEADS_VMEM = 24 * 1024 * 1024
SPREAD_VMEM = 61 * 1024 * 1024
NT = (((1,), (1,)), ((), ()))
TN = (((0,), (0,)), ((), ()))


def rope_tables(block, width, blocks):
    half = width // 2
    freqs = ROPE_BASE ** (-(np.arange(half, dtype=np.float64) * 2.0 / width))
    freqs = np.concatenate([freqs, freqs])
    inner = (np.arange(block) / ROPE_FACTOR)[:, None] * freqs[None, :]
    outer = (np.asarray(blocks) * block / ROPE_FACTOR)[:, None] * freqs[None, :]
    f32 = lambda x: jnp.asarray(x.astype(np.float32))
    return f32(np.stack([np.cos(inner), np.sin(inner)])), f32(np.stack([np.cos(outer), np.sin(outer)], axis=1))


def rope_of(inner_ref, outer_ref, row):
    both = outer_ref[row]
    cb, sb = both[0:1, :], both[1:2, :]
    ct, st = inner_ref[0], inner_ref[1]
    cos = ct * cb - st * sb
    sin = st * cb + ct * sb
    lane = lax.broadcasted_iota(jnp.int32, sin.shape, 1)
    return cos, jnp.where(lane < sin.shape[1] // 2, -sin, sin)


def swap_halves(x):
    return pltpu.roll(x, x.shape[1] // 2, 1)


def unrotate(y, cos, sin):
    return y * cos + swap_halves(y * sin)


def pack_kernel(kv_heads, back, axis, k_ref, v_ref, seg_ref, gain_ref, inner_ref, outer_ref, *rest):
    outs, scratch = rest[:-1], rest[-1]
    block = seg_ref.shape[1]
    per = kv_heads // len(outs)
    cos, sin = rope_of(inner_ref, outer_ref, lax.axis_index(axis) + back)
    gain = gain_ref[...]
    scratch[...] = k_ref[...].astype(jnp.float32)
    for h in range(kv_heads):
        x = scratch[pl.ds(h, block, stride=kv_heads), :]
        r = x * lax.rsqrt(jnp.mean(x * x, axis=1, keepdims=True) + EPS) * gain
        y = r * cos + swap_halves(r) * sin
        outs[h // per][pl.ds((h % per) * block, block), :] = y.astype(jnp.bfloat16)
    scratch[...] = v_ref[...].astype(jnp.float32)
    seg = jnp.broadcast_to(seg_ref[...].astype(jnp.float32) + 1.0, (16, block)).astype(jnp.bfloat16)
    for h in range(kv_heads):
        x = scratch[pl.ds(h, block, stride=kv_heads), :]
        outs[h // per][pl.ds((per + h % per) * block, block), :] = x.astype(jnp.bfloat16)
    for out in outs:
        out[pl.ds(2 * per * block, 16), :] = seg


def query_kernel(heads, back, axis, q_ref, g_ref, gain_ref, inner_ref, outer_ref, qo_ref, go_ref, scratch):
    block = q_ref.shape[0] // heads
    cos, sin = rope_of(inner_ref, outer_ref, lax.axis_index(axis) + back)
    gain = gain_ref[...]
    scratch[...] = q_ref[...].astype(jnp.float32)
    for h in range(heads):
        x = scratch[pl.ds(h, block, stride=heads), :]
        r = x * lax.rsqrt(jnp.mean(x * x, axis=1, keepdims=True) + EPS) * gain
        y = r * cos + swap_halves(r) * sin
        qo_ref[pl.ds(h * block, block), :] = y.astype(jnp.bfloat16)
    scratch[...] = g_ref[...].astype(jnp.float32)
    for h in range(heads):
        go_ref[pl.ds(h * block, block), :] = scratch[pl.ds(h, block, stride=heads), :].astype(jnp.bfloat16)


def attend_kernel(per, group, back, q_ref, g_ref, *rest):
    blocks = rest[: back + 1]
    dq_ref, own_ref = rest[back + 1 : back + 3]
    part_refs = rest[back + 3 : 2 * back + 3]
    bias_ref = rest[-1]
    block = own_ref.shape[0] // (2 * per)
    rows = group * block
    ids = blocks[0][pl.ds(2 * per * block, 16), :].astype(jnp.float32)[0:1, :]
    ids = jnp.concatenate([ids] * group, axis=1)
    for d in range(back + 1):
        key_row = blocks[d][pl.ds(2 * per * block, 16), :].astype(jnp.float32)[0:1, :]
        key_ids = jnp.broadcast_to(key_row, (block, block)).T
        key_ids = jnp.concatenate([key_ids] * group, axis=1)
        seen = key_ids == ids
        if d == 0:
            key_at = lax.broadcasted_iota(jnp.int32, (block, rows), 0)
            query_at = lax.broadcasted_iota(jnp.int32, (block, rows), 1) & (block - 1)
            seen = seen & (key_at <= query_at)
        bias_ref[pl.ds(d * block, block), :] = jnp.where(seen, 0.0, NEG)
    for h in range(per):
        q = q_ref[pl.ds(h * rows, rows), :]
        g = g_ref[pl.ds(h * rows, rows), :]
        k = jnp.concatenate([b[pl.ds(h * block, block), :] for b in blocks], axis=0)
        v = jnp.concatenate([b[pl.ds((per + h) * block, block), :] for b in blocks], axis=0)
        scores = lax.dot_general(k, q, NT, preferred_element_type=jnp.float32)
        expo = jnp.exp2(scores * (SCALE * LOG2E) + bias_ref[...])
        prob_grads = lax.dot_general(v, g, NT, preferred_element_type=jnp.float32)
        inverse = 1.0 / jnp.sum(expo, axis=0, keepdims=True)
        delta = jnp.sum(expo * prob_grads, axis=0, keepdims=True) * inverse
        probs = expo * inverse
        score_grads = (probs * (prob_grads - delta)).astype(jnp.bfloat16)
        dv = jnp.dot(probs.astype(jnp.bfloat16), g, preferred_element_type=jnp.float32)
        dk = jnp.dot(score_grads, q, preferred_element_type=jnp.float32) * SCALE
        dq = lax.dot_general(score_grads, k, TN, preferred_element_type=jnp.float32) * SCALE
        dq_ref[pl.ds(h * rows, rows), :] = dq
        own_ref[pl.ds(h * block, block), :] = dk[:block]
        own_ref[pl.ds((per + h) * block, block), :] = dv[:block]
        for d in range(1, back + 1):
            part = part_refs[d - 1]
            part[pl.ds(h * block, block), :] = dk[d * block : (d + 1) * block].astype(jnp.bfloat16)
            part[pl.ds((per + h) * block, block), :] = dv[d * block : (d + 1) * block].astype(jnp.bfloat16)


def query_back_kernel(heads, kv_heads, groups, back, axis, *rest):
    q_ref, qgain_ref, kgain_ref, inner_ref, outer_ref = rest[:5]
    rest = rest[5:]
    dq_refs, own_refs = rest[:groups], rest[groups : 2 * groups]
    msg_refs = rest[2 * groups : (3 + back) * groups]
    part_refs = rest[(3 + back) * groups : (3 + 2 * back) * groups]
    gq_ref, gains_ref, scratch = rest[-3:]
    block = q_ref.shape[0] // heads
    width = q_ref.shape[1]
    per = kv_heads // groups
    here = lax.axis_index(axis) + back
    total = jnp.zeros((block, width), jnp.float32)
    for d in range(back + 1):
        cos, sin = rope_of(inner_ref, outer_ref, here - d)
        for g in range(groups):
            for h in range(per):
                at = pl.ds(h * block, block)
                dk = own_refs[g][at, :] if d == 0 else part_refs[g * back + d - 1][at, :].astype(jnp.float32)
                k = msg_refs[g * (back + 1) + d][at, :].astype(jnp.float32)
                total = total + unrotate(dk, cos, sin) * unrotate(k, cos, sin)
    kgain = jnp.sum(total, axis=0, keepdims=True) / kgain_ref[...]
    cos, sin = rope_of(inner_ref, outer_ref, here)
    scratch[...] = q_ref[...].astype(jnp.float32)
    gain = qgain_ref[...]
    total = jnp.zeros((block, width), jnp.float32)
    each = heads // groups
    for h in range(heads):
        x = scratch[pl.ds(h, block, stride=heads), :]
        scale = lax.rsqrt(jnp.mean(x * x, axis=1, keepdims=True) + EPS)
        normed = x * scale
        dr = unrotate(dq_refs[h // each][pl.ds((h % each) * block, block), :], cos, sin)
        total = total + dr * normed
        dn = dr * gain
        dx = scale * (dn - normed * jnp.mean(dn * normed, axis=1, keepdims=True))
        scratch[pl.ds(h, block, stride=heads), :] = dx
    gq_ref[...] = scratch[...].astype(jnp.bfloat16)
    qgain = jnp.sum(total, axis=0, keepdims=True)
    gains_ref[...] = jnp.concatenate([qgain, kgain, jnp.zeros((6, width), jnp.float32)], axis=0)


def key_back_kernel(kv_heads, groups, back, axis, *rest):
    k_ref, gain_ref, inner_ref, outer_ref = rest[:4]
    own_refs = rest[4 : 4 + groups]
    got_refs = rest[4 + groups : 4 + (1 + back) * groups]
    gk_ref, gv_ref, scratch = rest[-3:]
    block = k_ref.shape[0] // kv_heads
    per = kv_heads // groups
    cos, sin = rope_of(inner_ref, outer_ref, lax.axis_index(axis) + back)
    gain = gain_ref[...]

    def total(g, row):
        at = pl.ds(row * block, block)
        value = own_refs[g][at, :]
        for d in range(back):
            value = value + got_refs[g * back + d][at, :].astype(jnp.float32)
        return value

    scratch[...] = k_ref[...].astype(jnp.float32)
    for h in range(kv_heads):
        x = scratch[pl.ds(h, block, stride=kv_heads), :]
        scale = lax.rsqrt(jnp.mean(x * x, axis=1, keepdims=True) + EPS)
        normed = x * scale
        dn = unrotate(total(h // per, h % per), cos, sin) * gain
        dx = scale * (dn - normed * jnp.mean(dn * normed, axis=1, keepdims=True))
        scratch[pl.ds(h, block, stride=kv_heads), :] = dx
    gk_ref[...] = scratch[...].astype(jnp.bfloat16)
    for h in range(kv_heads):
        scratch[pl.ds(h, block, stride=kv_heads), :] = total(h // per, per + h % per)
    gv_ref[...] = scratch[...].astype(jnp.bfloat16)


def call(kernel, outs, scratch, cost, *args):
    vmem = pl.BlockSpec(memory_space=pltpu.VMEM)
    return pl.pallas_call(
        kernel,
        out_shape=[jax.ShapeDtypeStruct(s, t) for s, t in outs],
        in_specs=[vmem] * len(args),
        out_specs=[vmem] * len(outs),
        scratch_shapes=[pltpu.VMEM(s, jnp.float32) for s in scratch],
        compiler_params=pltpu.CompilerParams(vmem_limit_bytes=VMEM_LIMIT),
        cost_estimate=pl.CostEstimate(flops=cost, bytes_accessed=1 << 20, transcendentals=0),
    )(*args)


def sum_over(x, axis, size):
    if size & (size - 1):
        return lax.psum(x, axis)
    step = 1
    while step < size:
        x = x + lax.ppermute(x, axis, [(i, i ^ step) for i in range(size)])
        step *= 2
    return x


def by_tokens(spans, parts, q_pre, k_pre, values, grad_out, segment_ids, q_gain, k_gain):
    block, heads, width = q_pre.shape[1:]
    kv_heads = k_pre.shape[2]
    group = heads // kv_heads
    groups = GROUPS
    per = kv_heads // groups
    longest = parts * block // 2
    back = min(parts - 1, (longest - 2) // block + 1)
    bf16, f32 = jnp.bfloat16, jnp.float32
    inner, outer = rope_tables(block, width, range(-back, parts))
    q2, g2 = (x.reshape(block * heads, width) for x in (q_pre, grad_out))
    k2, v2 = (x.reshape(block * kv_heads, width) for x in (k_pre, values))
    qg, kg = q_gain.reshape(1, width), k_gain.reshape(1, width)

    message = (2 * per * block + 16, width)
    own = call(
        functools.partial(pack_kernel, kv_heads, back, "seq"),
        [(message, bf16)] * groups, [(block * kv_heads, width)], 1 << 28,
        k2, v2, segment_ids, kg, inner, outer,
    )
    window = [
        [own[g]] + [lax.ppermute(own[g], "seq", [(i, i + d) for i in range(parts - d)]) for d in range(1, back + 1)]
        for g in range(groups)
    ]
    q_rot, g_rot = call(
        functools.partial(query_kernel, heads, back, "seq"),
        [((heads * block, width), bf16)] * 2, [(heads * block, width)], 1 << 29,
        q2, g2, qg, inner, outer,
    )
    dqs, owns, shares, returned = [], [], [], []
    rows = group * block * per
    for g in range(groups):
        dq, kept, *share = call(
            functools.partial(attend_kernel, per, group, back),
            [((rows, width), f32), ((2 * per * block, width), f32)] + [((2 * per * block, width), bf16)] * back,
            [((back + 1) * block, group * block)], 1 << 30,
            lax.slice_in_dim(q_rot, g * rows, (g + 1) * rows), lax.slice_in_dim(g_rot, g * rows, (g + 1) * rows),
            *window[g],
        )
        dqs.append(dq)
        owns.append(kept)
        shares += share
        returned += [
            lax.ppermute(share[d - 1], "seq", [(i + d, i) for i in range(parts - d)]) for d in range(1, back + 1)
        ]
    grad_q, gains = call(
        functools.partial(query_back_kernel, heads, kv_heads, groups, back, "seq"),
        [((heads * block, width), bf16), ((8, width), f32)], [(heads * block, width)], 1 << 29,
        q2, qg, kg, inner, outer, *dqs, *owns, *[m for w in window for m in w], *shares,
    )
    gains = sum_over(sum_over(gains, "seq", parts), "dp", spans)
    grad_k, grad_v = call(
        functools.partial(key_back_kernel, kv_heads, groups, back, "seq"),
        [((kv_heads * block, width), bf16)] * 2, [(kv_heads * block, width)], 1 << 28,
        k2, kg, inner, outer, *owns, *returned,
    )
    return (
        grad_q.reshape(q_pre.shape),
        grad_k.reshape(k_pre.shape),
        grad_v.reshape(values.shape),
        gains[0],
        gains[1],
    )


def head_rows(refs, first, per, block):
    for ref in refs:
        for h in range(per):
            yield ref[pl.ds(first + h, block, stride=ref.shape[0] // block), :].astype(jnp.bfloat16)


def spread_keys_kernel(axis, parts, per, a_hbm, b_hbm, seg_hbm, *rest):
    outs = rest[:parts]
    a_in, b_in, a_f32, b_f32, seg_in, msg, in_sems, out_sems = rest[parts:]
    block = seg_in.shape[1]
    me = lax.axis_index(axis)
    pairs = ((a_hbm, a_in), (b_hbm, b_in), (seg_hbm, seg_in))
    loads = [pltpu.make_async_copy(src, dst, in_sems.at[i]) for i, (src, dst) in enumerate(pairs)]
    for copy in loads:
        copy.start()
    for copy, src, dst in zip(loads, (a_in, b_in), (a_f32, b_f32)):
        copy.wait()
        dst[...] = src[...].astype(jnp.float32)
    loads[2].wait()
    ids = jnp.broadcast_to(seg_in[...].astype(jnp.float32), (16, block)).astype(jnp.bfloat16)
    stores = []
    for m in (*range(1, parts), 0):
        for i, rows in enumerate(head_rows((a_f32, b_f32), (me ^ m) * per, per, block)):
            msg[m, pl.ds(i * block, block), :] = rows
        msg[m, pl.ds(2 * per * block, 16), :] = ids
        copy = pltpu.make_async_copy(msg.at[m], outs[m], out_sems.at[m])
        copy.start()
        stores.append(copy)
    for copy in stores:
        copy.wait()


def spread_queries_kernel(axis, parts, groups, per, a_ref, b_ref, *rest):
    outs, a_f32, b_f32 = rest[-2 - parts * groups : -2], rest[-2], rest[-1]
    block = outs[0].shape[0] // (2 * per)
    me = lax.axis_index(axis)
    for src, dst in ((a_ref, a_f32), (b_ref, b_f32)):
        dst[...] = src[...].astype(jnp.float32)
    for grp in range(groups):
        for m in range(parts):
            for i, rows in enumerate(head_rows((a_f32, b_f32), ((me ^ m) * groups + grp) * per, per, block)):
                outs[grp * parts + m][pl.ds(i * block, block), :] = rows


def turned(x):
    return x.astype(jnp.float32).T


def rotated(x, c, s):
    half = x.shape[0] // 2
    a, b = x[:half], x[half:]
    return jnp.concatenate([a * c - b * s, b * c + a * s], axis=0)


def embed(x, gain, c, s):
    scale = lax.rsqrt(jnp.sum(x * x, axis=0, keepdims=True) * (1.0 / x.shape[0]) + EPS)
    normed = x * scale
    return rotated(normed * gain, c, s).astype(jnp.bfloat16), normed, scale


def embed_back(dy, gain, c, s, normed, scale):
    dr = rotated(dy, c, -s)
    share = dr * normed
    dn = dr * gain
    mean = jnp.sum(dn * normed, axis=0, keepdims=True) * (1.0 / dy.shape[0])
    return ((scale * SCALE) * (dn - normed * mean)).astype(jnp.bfloat16), share


def rope(table_ref, b, copies):
    c, s = table_ref[b, 0], table_ref[b, 1]
    return jnp.concatenate([c] * copies, axis=1), jnp.concatenate([s] * copies, axis=1)


def gain_columns(gains_ref, row, copies):
    width = gains_ref.shape[1]
    return jnp.concatenate([jnp.broadcast_to(gains_ref[row : row + 1, :], (width, width)).T] * copies, axis=1)


def keys_kernel(axis, parts, *rest):
    msgs, table_ref, gains_ref = rest[:parts], rest[parts], rest[parts + 1]
    kt_ref, k_ref, v_ref, kn_ref, ks_ref, id_ref = rest[parts + 2 :]
    block = table_ref.shape[3]
    owned = v_ref.shape[1]
    f32, bf16 = jnp.float32, jnp.bfloat16
    me = lax.axis_index(axis)
    gain = gain_columns(gains_ref, 1, 1)
    for m in range(parts):
        b = me ^ m
        id_ref[b] = jnp.broadcast_to(msgs[m][pl.ds(2 * owned * block, 16), :].astype(f32)[0:1, :], (8, block))
        for h in range(owned):
            y, normed, scale = embed(turned(msgs[m][pl.ds(h * block, block), :]), gain, *rope(table_ref, b, 1))
            kt_ref[b, h], kn_ref[b, h], ks_ref[b, h] = y, normed, jnp.broadcast_to(scale, (8, block))
            k_ref[b, h] = turned(y).astype(bf16)
            v_ref[b, h] = msgs[m][pl.ds((owned + h) * block, block), :]


def heads_kernel(axis, parts, grp, per, group, back, *rest):
    earlier, rest = rest[: grp * parts], rest[grp * parts :]
    msgs, rest = rest[:parts], rest[parts:]
    kt_ref, k_ref, v_ref, kn_ref, ks_ref, id_ref, table_ref, gains_ref = rest[:8]
    outs, share_ref = rest[8 : 8 + parts], rest[8 + parts]
    qt_ref, g_ref, qn_ref, qs_ref, res_ref = rest[9 + parts :]
    block, width = table_ref.shape[3], gains_ref.shape[1]
    rows = group * block
    f32, bf16 = jnp.float32, jnp.bfloat16
    me = lax.axis_index(axis)
    q_gain, k_gain = gain_columns(gains_ref, 0, group), gain_columns(gains_ref, 1, 1)
    for m in range(parts):
        b = me ^ m
        for p in range(per):
            at = b * per + p
            x = turned(msgs[m][pl.ds(p * rows, rows), :])
            y, normed, scale = embed(x, q_gain, *rope(table_ref, b, group))
            qt_ref[at], qn_ref[at], qs_ref[at] = y, normed, jnp.broadcast_to(scale, (8, rows))
            g_ref[at] = msgs[m][pl.ds((per + p) * rows, rows), :]

    id_rows = [id_ref[b][0:1, :] for b in range(parts)]
    id_columns = [jnp.broadcast_to(row, (block, block)).T for row in id_rows]
    key_at = lax.broadcasted_iota(jnp.int32, (block, block), 0)
    query_at = lax.broadcasted_iota(jnp.int32, (block, block), 1)
    causal = jnp.where(key_at <= query_at, 0.0, NEG)

    def bias(key_block, query_block):
        value = jnp.where(id_columns[key_block] == id_rows[query_block], 0.0, NEG)
        if key_block == query_block:
            value = value + causal
        return jnp.concatenate([value] * group, axis=1)

    q_total = jnp.zeros((width, rows), f32)
    k_total = jnp.zeros((width, block), f32)
    for p in range(per):
        out_base = p * (group + 2) * block
        dk = [None] * parts
        dv = [None] * parts
        spans = [range(max(0, b - back), b + 1) for b in range(parts)]
        qts = [qt_ref[b * per + p] for b in range(parts)]
        gs = [g_ref[b * per + p] for b in range(parts)]
        first = []
        for b, span in enumerate(spans):
            k = jnp.concatenate([k_ref[j, grp * per + p] for j in span], axis=0)
            v = jnp.concatenate([v_ref[j, grp * per + p] for j in span], axis=0)
            scores = jnp.dot(k, qts[b], preferred_element_type=f32)
            prob_grads = lax.dot_general(v, gs[b], NT, preferred_element_type=f32)
            first.append((scores, prob_grads))
        second = []
        for b, span in enumerate(spans):
            scores, prob_grads = first[b]
            hidden = jnp.concatenate([bias(j, b) for j in span], axis=0)
            expo = jnp.exp2(scores * (SCALE * LOG2E) + hidden)
            inverse = 1.0 / jnp.sum(expo, axis=0, keepdims=True)
            delta = jnp.sum(expo * prob_grads, axis=0, keepdims=True) * inverse
            probs = expo * inverse
            score_grads = (probs * (prob_grads - delta)).astype(bf16)
            second.append((probs.astype(bf16), score_grads))
        third = []
        for b, span in enumerate(spans):
            probs, score_grads = second[b]
            kt = jnp.concatenate([kt_ref[j, grp * per + p] for j in span], axis=1)
            third.append(jnp.dot(kt, score_grads, preferred_element_type=f32))
            dvs = jnp.dot(probs, gs[b], preferred_element_type=f32)
            dks = lax.dot_general(qts[b], score_grads, NT, preferred_element_type=f32)
            for i, j in enumerate(span):
                cut = slice(i * block, (i + 1) * block)
                dk[j] = dks[:, cut] if dk[j] is None else dk[j] + dks[:, cut]
                dv[j] = dvs[cut] if dv[j] is None else dv[j] + dvs[cut]
        for b, dq in enumerate(third):
            at = b * per + p
            dx, share = embed_back(dq, q_gain, *rope(table_ref, b, group), qn_ref[at], qs_ref[at][0:1, :])
            q_total = q_total + share
            res_ref[b, pl.ds(out_base, rows), :] = turned(dx).astype(bf16)
        for b in range(parts):
            dx, share = embed_back(dk[b], k_gain, *rope(table_ref, b, 1), kn_ref[b, grp * per + p], ks_ref[b, grp * per + p][0:1, :])
            k_total = k_total + share
            res_ref[b, pl.ds(out_base + rows, block), :] = turned(dx).astype(bf16)
            res_ref[b, pl.ds(out_base + rows + block, block), :] = dv[b].astype(bf16)
    size = res_ref.shape[1]
    for m in range(parts):
        for i in range(grp):
            outs[m][pl.ds(i * size, size), :] = earlier[i * parts + m][...]
        outs[m][pl.ds(grp * size, size), :] = res_ref[me ^ m]
    q_share = sum(q_total[:, i * block : (i + 1) * block] for i in range(group))
    q_share = jnp.sum(q_share.T, axis=0, keepdims=True)
    k_share = jnp.sum(k_total.T, axis=0, keepdims=True)
    row = lax.broadcasted_iota(jnp.int32, (8, width), 0)
    share_ref[...] = jnp.where(row == 0, q_share, jnp.where(row == 1, k_share, 0.0)) * SCALE


def collect_kernel(axis, parts, groups, heads, kv_heads, *rest):
    msgs = rest[:parts]
    gq_hbm, gk_hbm, gv_hbm, q_f32, k_f32, v_f32, q_out, k_out, v_out, sems = rest[parts:]
    group = heads // kv_heads
    per = kv_heads // parts // groups
    block = q_out.shape[0] // heads
    me = lax.axis_index(axis)
    arrays = ((q_f32, q_out, gq_hbm, heads), (k_f32, k_out, gk_hbm, kv_heads), (v_f32, v_out, gv_hbm, kv_heads))
    tokens = block // PIECES
    stores = []
    for piece in range(PIECES):
        start = piece * tokens
        for m in range(parts):
            at = start
            for grp in range(groups):
                for p in range(per):
                    kv = ((me ^ m) * groups + grp) * per + p
                    places = [(0, kv * group + i) for i in range(group)] + [(1, kv), (2, kv)]
                    for which, head in places:
                        dst, _, _, stride = arrays[which]
                        rows = msgs[m][pl.ds(at, tokens), :].astype(jnp.float32)
                        dst[pl.ds(start * stride + head, tokens, stride=stride), :] = rows
                        at += block
        for src, out, dst, stride in arrays:
            cut = pl.ds(start * stride, tokens * stride)
            out[cut, :] = src[cut, :].astype(jnp.bfloat16)
            copy = pltpu.make_async_copy(out.at[cut], dst.at[cut], sems.at[len(stores)])
            copy.start()
            stores.append(copy)
    for copy in stores:
        copy.wait()


def call_in(kernel, ins, outs, scratch, cost, *args, limit=HEADS_VMEM):
    return pl.pallas_call(
        kernel,
        out_shape=[jax.ShapeDtypeStruct(s, t) for s, t, _ in outs],
        in_specs=[pl.BlockSpec(memory_space=m) for m in ins],
        out_specs=[pl.BlockSpec(memory_space=m) for _, _, m in outs],
        scratch_shapes=scratch,
        compiler_params=pltpu.CompilerParams(vmem_limit_bytes=limit),
        cost_estimate=pl.CostEstimate(flops=cost, bytes_accessed=1 << 20, transcendentals=0),
    )(*args)


def exchange_sum(x, axis, size, *partners):
    got = [lax.ppermute(x, axis, [(i, i ^ m) for i in range(size)]) for m in partners]
    return x + got[0] if len(got) == 1 else (x + got[0]) + (got[1] + got[2])


def by_heads(spans, parts, q_pre, k_pre, values, grad_out, segment_ids, q_gain, k_gain):
    block, heads, width = q_pre.shape[1:]
    kv_heads = k_pre.shape[2]
    group = heads // kv_heads
    groups = min(GROUPS, kv_heads // parts)
    per = kv_heads // parts // groups
    rows = group * block
    longest = parts * block // 2
    back = min(parts - 1, (longest - 2) // block + 1)
    bf16, f32, vmem, hbm = jnp.bfloat16, jnp.float32, pltpu.VMEM, pltpu.HBM
    freqs = ROPE_BASE ** (-(np.arange(width // 2, dtype=np.float64) * 2.0 / width))
    angles = (np.arange(parts * block) / ROPE_FACTOR).reshape(parts, 1, block) * freqs[:, None]
    table = jnp.asarray(np.stack([np.cos(angles), np.sin(angles)], axis=1).astype(np.float32))
    q2, g2 = (x.reshape(block * heads, width) for x in (q_pre, grad_out))
    k2, v2 = (x.reshape(block * kv_heads, width) for x in (k_pre, values))
    owned = kv_heads // parts
    kv_sent = (2 * owned * block + 16, width)
    sent = (per * 2 * rows, width)
    back_sent = (per * (group + 2) * block, width)
    dma = pltpu.SemaphoreType.DMA
    q_shape, k_shape = q2.shape, k2.shape

    xor = lambda m, size: [(i, i ^ m) for i in range(size)]
    send = lambda out: [out[0]] + [lax.ppermute(out[m], "seq", xor(m, parts)) for m in range(1, parts)]
    kv_messages = call_in(
        functools.partial(spread_keys_kernel, "seq", parts, owned),
        [hbm] * 3, [(kv_sent, bf16, hbm)] * parts,
        [vmem(k_shape, bf16), vmem(k_shape, bf16), vmem(k_shape, f32), vmem(k_shape, f32), vmem((1, block), jnp.int32)]
        + [vmem((parts, *kv_sent), bf16), dma((3,)), dma((parts,))],
        1 << 20, k2, v2, segment_ids, limit=SPREAD_VMEM,
    )
    kv_arrived = send(kv_messages)
    messages = call_in(
        functools.partial(spread_queries_kernel, "seq", parts, groups, per * group),
        [vmem] * 2, [(sent, bf16, vmem)] * (parts * groups),
        [vmem(q_shape, f32), vmem(q_shape, f32)], 1 << 33, q2, g2,
    )
    arrived = [send(messages[grp * parts : (grp + 1) * parts]) for grp in range(groups)]
    gains = jnp.concatenate([q_gain[None], k_gain[None], jnp.zeros((6, width), f32)], axis=0)
    held = (parts, owned)
    keys = call_in(
        functools.partial(keys_kernel, "seq", parts), [vmem] * (parts + 2),
        [((*held, width, block), bf16, vmem), ((*held, block, width), bf16, vmem), ((*held, block, width), bf16, vmem)]
        + [((*held, width, block), f32, vmem), ((*held, 8, block), f32, vmem), ((parts, 8, block), f32, vmem)],
        [], 1 << 33, *kv_arrived, table, gains,
    )
    results, shares = [], []
    for grp in range(groups):
        inputs = [*results, *arrived[grp], *keys, table, gains]
        *made, share = call_in(
            functools.partial(heads_kernel, "seq", parts, grp, per, group, back),
            [vmem] * len(inputs),
            [(((grp + 1) * back_sent[0], width), bf16, vmem)] * parts + [((8, width), f32, vmem)],
            [vmem((parts * per, width, rows), bf16), vmem((parts * per, rows, width), bf16)]
            + [vmem((parts * per, width, rows), f32), vmem((parts * per, 8, rows), f32), vmem((parts, *back_sent), bf16)],
            1 << 34, *inputs,
        )
        results = made
        shares.append(share)
    go = lambda m: lax.ppermute(results[m], "seq", xor(m, parts))
    total = functools.reduce(jnp.add, shares)
    first, second, third = go(1), go(2), go(3)
    total = exchange_sum(total, "seq", parts, 1, 2, 3)
    total = exchange_sum(exchange_sum(exchange_sum(total, "dp", spans, 1), "dp", spans, 2), "dp", spans, 4)
    grad_q, grad_k, grad_v = call_in(
        functools.partial(collect_kernel, "seq", parts, groups, heads, kv_heads),
        [vmem] * parts, [(q_shape, bf16, hbm), (k_shape, bf16, hbm), (k_shape, bf16, hbm)],
        [vmem(q_shape, f32), vmem(k_shape, f32), vmem(k_shape, f32)]
        + [vmem(q_shape, bf16), vmem(k_shape, bf16), vmem(k_shape, bf16), dma((3 * PIECES,))],
        1 << 20, results[0], first, second, third,
    )
    return (
        grad_q.reshape(q_pre.shape), grad_k.reshape(k_pre.shape), grad_v.reshape(values.shape), total[0], total[1],
    )


def solution(mesh):
    tokens = P("dp", "seq", None, None)
    spans, parts = mesh.shape["dp"], mesh.shape["seq"]
    body = by_heads if (spans, parts) == (8, 4) else by_tokens
    return jax.shard_map(
        functools.partial(body, spans, parts),
        mesh=mesh,
        in_specs=(tokens, tokens, tokens, tokens, P("dp", "seq"), P(), P()),
        out_specs=(tokens, tokens, tokens, P(), P()),
        check_vma=False,
    )
```

```python
import functools

import jax
import jax.numpy as jnp
import numpy as np
from jax import lax
from jax.experimental import pallas as pl
from jax.experimental.pallas import tpu as pltpu
from jax.sharding import PartitionSpec as P

PRESCALE = 168
EPS = 1e-06
ROPE_BASE = 1000000.0
ROPE_FACTOR = 8.0
GROUPS = 2
PIECES = 4
NEG = -1e30
SCALE = float(PRESCALE) ** (-0.5)
LOG2E = 1.4426950408889634
VMEM_LIMIT = 48 * 1024 * 1024
HEADS_VMEM = 24 * 1024 * 1024
SPREAD_VMEM = 426 * 128 * 1024
NT = (((1,), (1,)), ((), ()))
TN = (((0,), (0,)), ((), ()))


def rope_tables(block, width, blocks):
    half = width // 2
    freqs = ROPE_BASE ** (-(np.arange(half, dtype=np.float64) * 2.0 / width))
    freqs = np.concatenate([freqs, freqs])
    inner = (np.arange(block) / ROPE_FACTOR)[:, None] * freqs[None, :]
    outer = (np.asarray(blocks) * block / ROPE_FACTOR)[:, None] * freqs[None, :]
    f32 = lambda x: jnp.asarray(x.astype(np.float32))
    return f32(np.stack([np.cos(inner), np.sin(inner)])), f32(np.stack([np.cos(outer), np.sin(outer)], axis=1))


def rope_of(inner_ref, outer_ref, row):
    both = outer_ref[row]
    cb, sb = both[0:1, :], both[1:2, :]
    ct, st = inner_ref[0], inner_ref[1]
    cos = ct * cb - st * sb
    sin = st * cb + ct * sb
    lane = lax.broadcasted_iota(jnp.int32, sin.shape, 1)
    return cos, jnp.where(lane < sin.shape[1] // 2, -sin, sin)


def swap_halves(x):
    return pltpu.roll(x, x.shape[1] // 2, 1)


def unrotate(y, cos, sin):
    return y * cos + swap_halves(y * sin)


def pack_kernel(kv_heads, back, axis, k_ref, v_ref, seg_ref, gain_ref, inner_ref, outer_ref, *rest):
    outs, scratch = rest[:-1], rest[-1]
    block = seg_ref.shape[1]
    per = kv_heads // len(outs)
    cos, sin = rope_of(inner_ref, outer_ref, lax.axis_index(axis) + back)
    gain = gain_ref[...]
    scratch[...] = k_ref[...].astype(jnp.float32)
    for h in range(kv_heads):
        x = scratch[pl.ds(h, block, stride=kv_heads), :]
        r = x * lax.rsqrt(jnp.mean(x * x, axis=1, keepdims=True) + EPS) * gain
        y = r * cos + swap_halves(r) * sin
        outs[h // per][pl.ds((h % per) * block, block), :] = y.astype(jnp.bfloat16)
    scratch[...] = v_ref[...].astype(jnp.float32)
    seg = jnp.broadcast_to(seg_ref[...].astype(jnp.float32) + 1.0, (16, block)).astype(jnp.bfloat16)
    for h in range(kv_heads):
        x = scratch[pl.ds(h, block, stride=kv_heads), :]
        outs[h // per][pl.ds((per + h % per) * block, block), :] = x.astype(jnp.bfloat16)
    for out in outs:
        out[pl.ds(2 * per * block, 16), :] = seg


def query_kernel(heads, back, axis, q_ref, g_ref, gain_ref, inner_ref, outer_ref, qo_ref, go_ref, scratch):
    block = q_ref.shape[0] // heads
    cos, sin = rope_of(inner_ref, outer_ref, lax.axis_index(axis) + back)
    gain = gain_ref[...]
    scratch[...] = q_ref[...].astype(jnp.float32)
    for h in range(heads):
        x = scratch[pl.ds(h, block, stride=heads), :]
        r = x * lax.rsqrt(jnp.mean(x * x, axis=1, keepdims=True) + EPS) * gain
        y = r * cos + swap_halves(r) * sin
        qo_ref[pl.ds(h * block, block), :] = y.astype(jnp.bfloat16)
    scratch[...] = g_ref[...].astype(jnp.float32)
    for h in range(heads):
        go_ref[pl.ds(h * block, block), :] = scratch[pl.ds(h, block, stride=heads), :].astype(jnp.bfloat16)


def attend_kernel(per, group, back, q_ref, g_ref, *rest):
    blocks = rest[: back + 1]
    dq_ref, own_ref = rest[back + 1 : back + 3]
    part_refs = rest[back + 3 : 2 * back + 3]
    bias_ref = rest[-1]
    block = own_ref.shape[0] // (2 * per)
    rows = group * block
    ids = blocks[0][pl.ds(2 * per * block, 16), :].astype(jnp.float32)[0:1, :]
    ids = jnp.concatenate([ids] * group, axis=1)
    for d in range(back + 1):
        key_row = blocks[d][pl.ds(2 * per * block, 16), :].astype(jnp.float32)[0:1, :]
        key_ids = jnp.broadcast_to(key_row, (block, block)).T
        key_ids = jnp.concatenate([key_ids] * group, axis=1)
        seen = key_ids == ids
        if d == 0:
            key_at = lax.broadcasted_iota(jnp.int32, (block, rows), 0)
            query_at = lax.broadcasted_iota(jnp.int32, (block, rows), 1) & (block - 1)
            seen = seen & (key_at <= query_at)
        bias_ref[pl.ds(d * block, block), :] = jnp.where(seen, 0.0, NEG)
    for h in range(per):
        q = q_ref[pl.ds(h * rows, rows), :]
        g = g_ref[pl.ds(h * rows, rows), :]
        k = jnp.concatenate([b[pl.ds(h * block, block), :] for b in blocks], axis=0)
        v = jnp.concatenate([b[pl.ds((per + h) * block, block), :] for b in blocks], axis=0)
        scores = lax.dot_general(k, q, NT, preferred_element_type=jnp.float32)
        expo = jnp.exp2(scores * (SCALE * LOG2E) + bias_ref[...])
        prob_grads = lax.dot_general(v, g, NT, preferred_element_type=jnp.float32)
        inverse = 1.0 / jnp.sum(expo, axis=0, keepdims=True)
        delta = jnp.sum(expo * prob_grads, axis=0, keepdims=True) * inverse
        probs = expo * inverse
        score_grads = (probs * (prob_grads - delta)).astype(jnp.bfloat16)
        dv = jnp.dot(probs.astype(jnp.bfloat16), g, preferred_element_type=jnp.float32)
        dk = jnp.dot(score_grads, q, preferred_element_type=jnp.float32) * SCALE
        dq = lax.dot_general(score_grads, k, TN, preferred_element_type=jnp.float32) * SCALE
        dq_ref[pl.ds(h * rows, rows), :] = dq
        own_ref[pl.ds(h * block, block), :] = dk[:block]
        own_ref[pl.ds((per + h) * block, block), :] = dv[:block]
        for d in range(1, back + 1):
            part = part_refs[d - 1]
            part[pl.ds(h * block, block), :] = dk[d * block : (d + 1) * block].astype(jnp.bfloat16)
            part[pl.ds((per + h) * block, block), :] = dv[d * block : (d + 1) * block].astype(jnp.bfloat16)


def query_back_kernel(heads, kv_heads, groups, back, axis, *rest):
    q_ref, qgain_ref, kgain_ref, inner_ref, outer_ref = rest[:5]
    rest = rest[5:]
    dq_refs, own_refs = rest[:groups], rest[groups : 2 * groups]
    msg_refs = rest[2 * groups : (3 + back) * groups]
    part_refs = rest[(3 + back) * groups : (3 + 2 * back) * groups]
    gq_ref, gains_ref, scratch = rest[-3:]
    block = q_ref.shape[0] // heads
    width = q_ref.shape[1]
    per = kv_heads // groups
    here = lax.axis_index(axis) + back
    total = jnp.zeros((block, width), jnp.float32)
    for d in range(back + 1):
        cos, sin = rope_of(inner_ref, outer_ref, here - d)
        for g in range(groups):
            for h in range(per):
                at = pl.ds(h * block, block)
                dk = own_refs[g][at, :] if d == 0 else part_refs[g * back + d - 1][at, :].astype(jnp.float32)
                k = msg_refs[g * (back + 1) + d][at, :].astype(jnp.float32)
                total = total + unrotate(dk, cos, sin) * unrotate(k, cos, sin)
    kgain = jnp.sum(total, axis=0, keepdims=True) / kgain_ref[...]
    cos, sin = rope_of(inner_ref, outer_ref, here)
    scratch[...] = q_ref[...].astype(jnp.float32)
    gain = qgain_ref[...]
    total = jnp.zeros((block, width), jnp.float32)
    each = heads // groups
    for h in range(heads):
        x = scratch[pl.ds(h, block, stride=heads), :]
        scale = lax.rsqrt(jnp.mean(x * x, axis=1, keepdims=True) + EPS)
        normed = x * scale
        dr = unrotate(dq_refs[h // each][pl.ds((h % each) * block, block), :], cos, sin)
        total = total + dr * normed
        dn = dr * gain
        dx = scale * (dn - normed * jnp.mean(dn * normed, axis=1, keepdims=True))
        scratch[pl.ds(h, block, stride=heads), :] = dx
    gq_ref[...] = scratch[...].astype(jnp.bfloat16)
    qgain = jnp.sum(total, axis=0, keepdims=True)
    gains_ref[...] = jnp.concatenate([qgain, kgain, jnp.zeros((6, width), jnp.float32)], axis=0)


def key_back_kernel(kv_heads, groups, back, axis, *rest):
    k_ref, gain_ref, inner_ref, outer_ref = rest[:4]
    own_refs = rest[4 : 4 + groups]
    got_refs = rest[4 + groups : 4 + (1 + back) * groups]
    gk_ref, gv_ref, scratch = rest[-3:]
    block = k_ref.shape[0] // kv_heads
    per = kv_heads // groups
    cos, sin = rope_of(inner_ref, outer_ref, lax.axis_index(axis) + back)
    gain = gain_ref[...]

    def total(g, row):
        at = pl.ds(row * block, block)
        value = own_refs[g][at, :]
        for d in range(back):
            value = value + got_refs[g * back + d][at, :].astype(jnp.float32)
        return value

    scratch[...] = k_ref[...].astype(jnp.float32)
    for h in range(kv_heads):
        x = scratch[pl.ds(h, block, stride=kv_heads), :]
        scale = lax.rsqrt(jnp.mean(x * x, axis=1, keepdims=True) + EPS)
        normed = x * scale
        dn = unrotate(total(h // per, h % per), cos, sin) * gain
        dx = scale * (dn - normed * jnp.mean(dn * normed, axis=1, keepdims=True))
        scratch[pl.ds(h, block, stride=kv_heads), :] = dx
    gk_ref[...] = scratch[...].astype(jnp.bfloat16)
    for h in range(kv_heads):
        scratch[pl.ds(h, block, stride=kv_heads), :] = total(h // per, per + h % per)
    gv_ref[...] = scratch[...].astype(jnp.bfloat16)


def call(kernel, outs, scratch, cost, *args):
    vmem = pl.BlockSpec(memory_space=pltpu.VMEM)
    return pl.pallas_call(
        kernel,
        out_shape=[jax.ShapeDtypeStruct(s, t) for s, t in outs],
        in_specs=[vmem] * len(args),
        out_specs=[vmem] * len(outs),
        scratch_shapes=[pltpu.VMEM(s, jnp.float32) for s in scratch],
        compiler_params=pltpu.CompilerParams(vmem_limit_bytes=VMEM_LIMIT),
        cost_estimate=pl.CostEstimate(flops=cost, bytes_accessed=1 << 20, transcendentals=0),
    )(*args)


def sum_over(x, axis, size):
    if size & (size - 1):
        return lax.psum(x, axis)
    step = 1
    while step < size:
        x = x + lax.ppermute(x, axis, [(i, i ^ step) for i in range(size)])
        step *= 2
    return x


def by_tokens(spans, parts, q_pre, k_pre, values, grad_out, segment_ids, q_gain, k_gain):
    block, heads, width = q_pre.shape[1:]
    kv_heads = k_pre.shape[2]
    group = heads // kv_heads
    groups = GROUPS
    per = kv_heads // groups
    longest = parts * block // 2
    back = min(parts - 1, (longest - 2) // block + 1)
    bf16, f32 = jnp.bfloat16, jnp.float32
    inner, outer = rope_tables(block, width, range(-back, parts))
    q2, g2 = (x.reshape(block * heads, width) for x in (q_pre, grad_out))
    k2, v2 = (x.reshape(block * kv_heads, width) for x in (k_pre, values))
    qg, kg = q_gain.reshape(1, width), k_gain.reshape(1, width)

    message = (2 * per * block + 16, width)
    own = call(
        functools.partial(pack_kernel, kv_heads, back, "seq"),
        [(message, bf16)] * groups, [(block * kv_heads, width)], 1 << 28,
        k2, v2, segment_ids, kg, inner, outer,
    )
    window = [
        [own[g]] + [lax.ppermute(own[g], "seq", [(i, i + d) for i in range(parts - d)]) for d in range(1, back + 1)]
        for g in range(groups)
    ]
    q_rot, g_rot = call(
        functools.partial(query_kernel, heads, back, "seq"),
        [((heads * block, width), bf16)] * 2, [(heads * block, width)], 1 << 29,
        q2, g2, qg, inner, outer,
    )
    dqs, owns, shares, returned = [], [], [], []
    rows = group * block * per
    for g in range(groups):
        dq, kept, *share = call(
            functools.partial(attend_kernel, per, group, back),
            [((rows, width), f32), ((2 * per * block, width), f32)] + [((2 * per * block, width), bf16)] * back,
            [((back + 1) * block, group * block)], 1 << 30,
            lax.slice_in_dim(q_rot, g * rows, (g + 1) * rows), lax.slice_in_dim(g_rot, g * rows, (g + 1) * rows),
            *window[g],
        )
        dqs.append(dq)
        owns.append(kept)
        shares += share
        returned += [
            lax.ppermute(share[d - 1], "seq", [(i + d, i) for i in range(parts - d)]) for d in range(1, back + 1)
        ]
    grad_q, gains = call(
        functools.partial(query_back_kernel, heads, kv_heads, groups, back, "seq"),
        [((heads * block, width), bf16), ((8, width), f32)], [(heads * block, width)], 1 << 29,
        q2, qg, kg, inner, outer, *dqs, *owns, *[m for w in window for m in w], *shares,
    )
    gains = sum_over(sum_over(gains, "seq", parts), "dp", spans)
    grad_k, grad_v = call(
        functools.partial(key_back_kernel, kv_heads, groups, back, "seq"),
        [((kv_heads * block, width), bf16)] * 2, [(kv_heads * block, width)], 1 << 28,
        k2, kg, inner, outer, *owns, *returned,
    )
    return (
        grad_q.reshape(q_pre.shape),
        grad_k.reshape(k_pre.shape),
        grad_v.reshape(values.shape),
        gains[0],
        gains[1],
    )


def head_rows(refs, first, per, block):
    for ref in refs:
        for h in range(per):
            yield ref[pl.ds(first + h, block, stride=ref.shape[0] // block), :].astype(jnp.bfloat16)


def spread_keys_kernel(axis, parts, per, a_hbm, b_hbm, *rest):
    outs = rest[:parts]
    a_in, b_in, a_f32, b_f32, in_sems = rest[parts:]
    block = outs[0].shape[0] // (2 * per)
    me = lax.axis_index(axis)
    loads = [pltpu.make_async_copy(src, dst, in_sems.at[i]) for i, (src, dst) in enumerate(((a_hbm, a_in), (b_hbm, b_in)))]
    for copy in loads:
        copy.start()
    for copy, src, dst in zip(loads, (a_in, b_in), (a_f32, b_f32)):
        copy.wait()
        dst[...] = src[...].astype(jnp.float32)
    for m in range(parts):
        for i, rows in enumerate(head_rows((a_f32, b_f32), (me ^ m) * per, per, block)):
            outs[m][pl.ds(i * block, block), :] = rows


def spread_queries_kernel(axis, parts, groups, per, a_ref, b_ref, seg_ref, *rest):
    outs, a_f32, b_f32 = rest[-2 - parts * groups : -2], rest[-2], rest[-1]
    block = seg_ref.shape[1]
    ids = jnp.broadcast_to(seg_ref[...].astype(jnp.float32), (16, block)).astype(jnp.bfloat16)
    me = lax.axis_index(axis)
    for src, dst in ((a_ref, a_f32), (b_ref, b_f32)):
        dst[...] = src[...].astype(jnp.float32)
    for grp in range(groups):
        for m in range(parts):
            for i, rows in enumerate(head_rows((a_f32, b_f32), ((me ^ m) * groups + grp) * per, per, block)):
                outs[grp * parts + m][pl.ds(i * block, block), :] = rows
            outs[m][pl.ds(2 * per * block, 16), :] = ids


def turned(x):
    return x.astype(jnp.float32).T


def rotated(x, c, s):
    half = x.shape[0] // 2
    a, b = x[:half], x[half:]
    return jnp.concatenate([a * c - b * s, b * c + a * s], axis=0)


def embed(x, gain, c, s):
    scale = lax.rsqrt(jnp.sum(x * x, axis=0, keepdims=True) * (1.0 / x.shape[0]) + EPS)
    normed = x * scale
    return rotated(normed * gain, c, s).astype(jnp.bfloat16), normed, scale


def embed_back(dy, gain, c, s, normed, scale):
    dr = rotated(dy, c, -s)
    share = dr * normed
    dn = dr * gain
    mean = jnp.sum(dn * normed, axis=0, keepdims=True) * (1.0 / dy.shape[0])
    return ((scale * SCALE) * (dn - normed * mean)).astype(jnp.bfloat16), share


def rope(table_ref, b, copies):
    c, s = table_ref[b, 0], table_ref[b, 1]
    return jnp.concatenate([c] * copies, axis=1), jnp.concatenate([s] * copies, axis=1)


def gain_columns(gains_ref, row, copies):
    width = gains_ref.shape[1]
    return jnp.concatenate([jnp.broadcast_to(gains_ref[row : row + 1, :], (width, width)).T] * copies, axis=1)


def keys_kernel(axis, parts, *rest):
    msgs, table_ref, gains_ref = rest[:parts], rest[parts], rest[parts + 1]
    kt_ref, k_ref, v_ref, kn_ref, ks_ref = rest[parts + 2 :]
    block = table_ref.shape[3]
    owned = v_ref.shape[1]
    f32, bf16 = jnp.float32, jnp.bfloat16
    me = lax.axis_index(axis)
    gain = gain_columns(gains_ref, 1, 1)
    for m in range(parts):
        b = me ^ m
        for h in range(owned):
            y, normed, scale = embed(turned(msgs[m][pl.ds(h * block, block), :]), gain, *rope(table_ref, b, 1))
            kt_ref[b, h], kn_ref[b, h], ks_ref[b, h] = y, normed, jnp.broadcast_to(scale, (8, block))
            k_ref[b, h] = turned(y).astype(bf16)
            v_ref[b, h] = msgs[m][pl.ds((owned + h) * block, block), :]


def heads_kernel(axis, parts, grp, per, group, back, *rest):
    earlier, rest = rest[: grp * parts], rest[grp * parts :]
    msgs, rest = rest[:parts], rest[parts:]
    kt_ref, k_ref, v_ref, kn_ref, ks_ref, table_ref, gains_ref = rest[:7]
    rest = rest[7:]
    if grp:
        id_ref, rest = rest[0], rest[1:]
    outs, share_ref, rest = rest[:parts], rest[parts], rest[parts + 1 :]
    if not grp:
        id_ref, rest = rest[0], rest[1:]
    qt_ref, g_ref, qn_ref, qs_ref, res_ref = rest
    block, width = table_ref.shape[3], gains_ref.shape[1]
    rows = group * block
    f32, bf16 = jnp.float32, jnp.bfloat16
    me = lax.axis_index(axis)
    q_gain, k_gain = gain_columns(gains_ref, 0, group), gain_columns(gains_ref, 1, 1)
    for m in range(parts):
        b = me ^ m
        if not grp:
            ids = msgs[m][pl.ds(2 * per * rows, 16), :].astype(f32)[0:1, :]
            id_ref[b] = jnp.broadcast_to(ids, (8, block))
        for p in range(per):
            at = b * per + p
            x = turned(msgs[m][pl.ds(p * rows, rows), :])
            y, normed, scale = embed(x, q_gain, *rope(table_ref, b, group))
            qt_ref[at], qn_ref[at], qs_ref[at] = y, normed, jnp.broadcast_to(scale, (8, rows))
            g_ref[at] = msgs[m][pl.ds((per + p) * rows, rows), :]

    id_rows = [id_ref[b][0:1, :] for b in range(parts)]
    id_columns = [jnp.broadcast_to(row, (block, block)).T for row in id_rows]
    key_at = lax.broadcasted_iota(jnp.int32, (block, block), 0)
    query_at = lax.broadcasted_iota(jnp.int32, (block, block), 1)
    causal = jnp.where(key_at <= query_at, 0.0, NEG)

    def bias(key_block, query_block):
        value = jnp.where(id_columns[key_block] == id_rows[query_block], 0.0, NEG)
        if key_block == query_block:
            value = value + causal
        return jnp.concatenate([value] * group, axis=1)

    q_total = jnp.zeros((width, rows), f32)
    k_total = jnp.zeros((width, block), f32)
    for p in range(per):
        out_base = p * (group + 2) * block
        dk = [None] * parts
        dv = [None] * parts
        spans = [range(max(0, b - back), b + 1) for b in range(parts)]
        qts = [qt_ref[b * per + p] for b in range(parts)]
        gs = [g_ref[b * per + p] for b in range(parts)]
        first = []
        for b, span in enumerate(spans):
            k = jnp.concatenate([k_ref[j, grp * per + p] for j in span], axis=0)
            v = jnp.concatenate([v_ref[j, grp * per + p] for j in span], axis=0)
            scores = jnp.dot(k, qts[b], preferred_element_type=f32)
            prob_grads = lax.dot_general(v, gs[b], NT, preferred_element_type=f32)
            first.append((scores, prob_grads))
        second = []
        for b, span in enumerate(spans):
            scores, prob_grads = first[b]
            hidden = jnp.concatenate([bias(j, b) for j in span], axis=0)
            expo = jnp.exp2(scores * (SCALE * LOG2E) + hidden)
            inverse = 1.0 / jnp.sum(expo, axis=0, keepdims=True)
            delta = jnp.sum(expo * prob_grads, axis=0, keepdims=True) * inverse
            probs = expo * inverse
            score_grads = (probs * (prob_grads - delta)).astype(bf16)
            second.append((probs.astype(bf16), score_grads))
        third = []
        for b, span in enumerate(spans):
            probs, score_grads = second[b]
            kt = jnp.concatenate([kt_ref[j, grp * per + p] for j in span], axis=1)
            third.append(jnp.dot(kt, score_grads, preferred_element_type=f32))
            dvs = jnp.dot(probs, gs[b], preferred_element_type=f32)
            dks = lax.dot_general(qts[b], score_grads, NT, preferred_element_type=f32)
            for i, j in enumerate(span):
                cut = slice(i * block, (i + 1) * block)
                dk[j] = dks[:, cut] if dk[j] is None else dk[j] + dks[:, cut]
                dv[j] = dvs[cut] if dv[j] is None else dv[j] + dvs[cut]
        for b, dq in enumerate(third):
            at = b * per + p
            dx, share = embed_back(dq, q_gain, *rope(table_ref, b, group), qn_ref[at], qs_ref[at][0:1, :])
            q_total = q_total + share
            res_ref[b, pl.ds(out_base, rows), :] = turned(dx).astype(bf16)
        for b in range(parts):
            dx, share = embed_back(dk[b], k_gain, *rope(table_ref, b, 1), kn_ref[b, grp * per + p], ks_ref[b, grp * per + p][0:1, :])
            k_total = k_total + share
            res_ref[b, pl.ds(out_base + rows, block), :] = turned(dx).astype(bf16)
            res_ref[b, pl.ds(out_base + rows + block, block), :] = dv[b].astype(bf16)
    size = res_ref.shape[1]
    for m in range(parts):
        for i in range(grp):
            outs[m][pl.ds(i * size, size), :] = earlier[i * parts + m][...]
        outs[m][pl.ds(grp * size, size), :] = res_ref[me ^ m]
    q_share = sum(q_total[:, i * block : (i + 1) * block] for i in range(group))
    q_share = jnp.sum(q_share.T, axis=0, keepdims=True)
    k_share = jnp.sum(k_total.T, axis=0, keepdims=True)
    row = lax.broadcasted_iota(jnp.int32, (8, width), 0)
    share_ref[...] = jnp.where(row == 0, q_share, jnp.where(row == 1, k_share, 0.0)) * SCALE


def collect_kernel(axis, parts, groups, heads, kv_heads, *rest):
    msgs = rest[:parts]
    gq_hbm, gk_hbm, gv_hbm, q_f32, k_f32, v_f32, q_out, k_out, v_out, sems = rest[parts:]
    group = heads // kv_heads
    per = kv_heads // parts // groups
    block = q_out.shape[0] // heads
    me = lax.axis_index(axis)
    arrays = ((q_f32, q_out, gq_hbm, heads), (k_f32, k_out, gk_hbm, kv_heads), (v_f32, v_out, gv_hbm, kv_heads))
    tokens = block // PIECES
    stores = []
    for piece in range(PIECES):
        start = piece * tokens
        for m in range(parts):
            at = start
            for grp in range(groups):
                for p in range(per):
                    kv = ((me ^ m) * groups + grp) * per + p
                    places = [(0, kv * group + i) for i in range(group)] + [(1, kv), (2, kv)]
                    for which, head in places:
                        dst, _, _, stride = arrays[which]
                        rows = msgs[m][pl.ds(at, tokens), :].astype(jnp.float32)
                        dst[pl.ds(start * stride + head, tokens, stride=stride), :] = rows
                        at += block
        for src, out, dst, stride in arrays:
            cut = pl.ds(start * stride, tokens * stride)
            out[cut, :] = src[cut, :].astype(jnp.bfloat16)
            copy = pltpu.make_async_copy(out.at[cut], dst.at[cut], sems.at[len(stores)])
            copy.start()
            stores.append(copy)
    for copy in stores:
        copy.wait()


def call_in(kernel, ins, outs, scratch, cost, *args, limit=HEADS_VMEM):
    return pl.pallas_call(
        kernel,
        out_shape=[jax.ShapeDtypeStruct(s, t) for s, t, _ in outs],
        in_specs=[pl.BlockSpec(memory_space=m) for m in ins],
        out_specs=[pl.BlockSpec(memory_space=m) for _, _, m in outs],
        scratch_shapes=scratch,
        compiler_params=pltpu.CompilerParams(vmem_limit_bytes=limit),
        cost_estimate=pl.CostEstimate(flops=cost, bytes_accessed=1 << 20, transcendentals=0),
    )(*args)


def exchange_sum(x, axis, size, *partners):
    got = [lax.ppermute(x, axis, [(i, i ^ m) for i in range(size)]) for m in partners]
    return x + got[0] if len(got) == 1 else (x + got[0]) + (got[1] + got[2])


def by_heads(spans, parts, q_pre, k_pre, values, grad_out, segment_ids, q_gain, k_gain):
    block, heads, width = q_pre.shape[1:]
    kv_heads = k_pre.shape[2]
    group = heads // kv_heads
    groups = min(GROUPS, kv_heads // parts)
    per = kv_heads // parts // groups
    rows = group * block
    longest = parts * block // 2
    back = min(parts - 1, (longest - 2) // block + 1)
    bf16, f32, vmem, hbm = jnp.bfloat16, jnp.float32, pltpu.VMEM, pltpu.HBM
    freqs = ROPE_BASE ** (-(np.arange(width // 2, dtype=np.float64) * 2.0 / width))
    angles = (np.arange(parts * block) / ROPE_FACTOR).reshape(parts, 1, block) * freqs[:, None]
    table = jnp.asarray(np.stack([np.cos(angles), np.sin(angles)], axis=1).astype(np.float32))
    q2, g2 = (x.reshape(block * heads, width) for x in (q_pre, grad_out))
    k2, v2 = (x.reshape(block * kv_heads, width) for x in (k_pre, values))
    owned = kv_heads // parts
    kv_sent = (2 * owned * block, width)
    sent = (per * 2 * rows, width)
    back_sent = (per * (group + 2) * block, width)
    dma = pltpu.SemaphoreType.DMA
    q_shape, k_shape = q2.shape, k2.shape

    xor = lambda m, size: [(i, i ^ m) for i in range(size)]
    send = lambda out: [out[0]] + [lax.ppermute(out[m], "seq", xor(m, parts)) for m in range(1, parts)]
    kv_messages = call_in(
        functools.partial(spread_keys_kernel, "seq", parts, owned),
        [hbm] * 2, [(kv_sent, bf16, vmem)] * parts,
        [vmem(k_shape, bf16), vmem(k_shape, bf16), vmem(k_shape, f32), vmem(k_shape, f32), dma((2,))],
        1 << 20, k2, v2, limit=SPREAD_VMEM,
    )
    kv_arrived = send(kv_messages)
    messages = call_in(
        functools.partial(spread_queries_kernel, "seq", parts, groups, per * group),
        [vmem] * 3, [((sent[0] + 16, width), bf16, vmem)] * (parts * groups),
        [vmem(q_shape, f32), vmem(q_shape, f32)], 1 << 33, q2, g2, segment_ids,
    )
    arrived = [send(messages[grp * parts : (grp + 1) * parts]) for grp in range(groups)]
    gains = jnp.concatenate([q_gain[None], k_gain[None], jnp.zeros((6, width), f32)], axis=0)
    held = (parts, owned)
    keys = call_in(
        functools.partial(keys_kernel, "seq", parts), [vmem] * (parts + 2),
        [((*held, width, block), bf16, vmem), ((*held, block, width), bf16, vmem), ((*held, block, width), bf16, vmem)]
        + [((*held, width, block), f32, vmem), ((*held, 8, block), f32, vmem)],
        [], 1 << 33, *kv_arrived, table, gains,
    )
    results, shares, ids = [], [], []
    for grp in range(groups):
        inputs = [*results, *arrived[grp], *keys, table, gains, *ids]
        id_shape = ((parts, 8, block), f32, vmem)
        made = call_in(
            functools.partial(heads_kernel, "seq", parts, grp, per, group, back),
            [vmem] * len(inputs),
            [(((grp + 1) * back_sent[0], width), bf16, vmem)] * parts + [((8, width), f32, vmem)] + [id_shape] * (grp == 0),
            [vmem((parts * per, width, rows), bf16), vmem((parts * per, rows, width), bf16)]
            + [vmem((parts * per, width, rows), f32), vmem((parts * per, 8, rows), f32), vmem((parts, *back_sent), bf16)],
            1 << 34, *inputs,
        )
        results, share, ids = made[:parts], made[parts], made[parts + 1 :] or ids
        shares.append(share)
    go = lambda m: lax.ppermute(results[m], "seq", xor(m, parts))
    total = functools.reduce(jnp.add, shares)
    first, second, third = go(1), go(2), go(3)
    total = exchange_sum(total, "seq", parts, 1, 2, 3)
    total = exchange_sum(exchange_sum(exchange_sum(total, "dp", spans, 1), "dp", spans, 2), "dp", spans, 4)
    grad_q, grad_k, grad_v = call_in(
        functools.partial(collect_kernel, "seq", parts, groups, heads, kv_heads),
        [vmem] * parts, [(q_shape, bf16, hbm), (k_shape, bf16, hbm), (k_shape, bf16, hbm)],
        [vmem(q_shape, f32), vmem(k_shape, f32), vmem(k_shape, f32)]
        + [vmem(q_shape, bf16), vmem(k_shape, bf16), vmem(k_shape, bf16), dma((3 * PIECES,))],
        1 << 20, results[0], first, second, third,
    )
    return (
        grad_q.reshape(q_pre.shape), grad_k.reshape(k_pre.shape), grad_v.reshape(values.shape), total[0], total[1],
    )


def solution(mesh):
    tokens = P("dp", "seq", None, None)
    spans, parts = mesh.shape["dp"], mesh.shape["seq"]
    body = by_heads if (spans, parts) == (8, 4) else by_tokens
    return jax.shard_map(
        functools.partial(body, spans, parts),
        mesh=mesh,
        in_specs=(tokens, tokens, tokens, tokens, P("dp", "seq"), P(), P()),
        out_specs=(tokens, tokens, tokens, P(), P()),
        check_vma=False,
    )
```

```python
import functools

import jax
import jax.numpy as jnp
import numpy as np
from jax import lax
from jax.experimental import pallas as pl
from jax.experimental.pallas import tpu as pltpu
from jax.sharding import PartitionSpec as P

PRESCALE = 168
EPS = 1e-06
ROPE_BASE = 1000000.0
ROPE_FACTOR = 8.0
GROUPS = 2
PIECES = 4
NEG = -1e30
SCALE = float(PRESCALE) ** (-0.5)
LOG2E = 1.4426950408889634
VMEM_LIMIT = 48 * 1024 * 1024
HEADS_VMEM = 24 * 1024 * 1024
SPREAD_VMEM = 426 * 128 * 1024
NT = (((1,), (1,)), ((), ()))
TN = (((0,), (0,)), ((), ()))


def rope_tables(block, width, blocks):
    half = width // 2
    freqs = ROPE_BASE ** (-(np.arange(half, dtype=np.float64) * 2.0 / width))
    freqs = np.concatenate([freqs, freqs])
    inner = (np.arange(block) / ROPE_FACTOR)[:, None] * freqs[None, :]
    outer = (np.asarray(blocks) * block / ROPE_FACTOR)[:, None] * freqs[None, :]
    f32 = lambda x: jnp.asarray(x.astype(np.float32))
    return f32(np.stack([np.cos(inner), np.sin(inner)])), f32(np.stack([np.cos(outer), np.sin(outer)], axis=1))


def rope_of(inner_ref, outer_ref, row):
    both = outer_ref[row]
    cb, sb = both[0:1, :], both[1:2, :]
    ct, st = inner_ref[0], inner_ref[1]
    cos = ct * cb - st * sb
    sin = st * cb + ct * sb
    lane = lax.broadcasted_iota(jnp.int32, sin.shape, 1)
    return cos, jnp.where(lane < sin.shape[1] // 2, -sin, sin)


def swap_halves(x):
    return pltpu.roll(x, x.shape[1] // 2, 1)


def unrotate(y, cos, sin):
    return y * cos + swap_halves(y * sin)


def pack_kernel(kv_heads, back, axis, k_ref, v_ref, seg_ref, gain_ref, inner_ref, outer_ref, *rest):
    outs, scratch = rest[:-1], rest[-1]
    block = seg_ref.shape[1]
    per = kv_heads // len(outs)
    cos, sin = rope_of(inner_ref, outer_ref, lax.axis_index(axis) + back)
    gain = gain_ref[...]
    scratch[...] = k_ref[...].astype(jnp.float32)
    for h in range(kv_heads):
        x = scratch[pl.ds(h, block, stride=kv_heads), :]
        r = x * lax.rsqrt(jnp.mean(x * x, axis=1, keepdims=True) + EPS) * gain
        y = r * cos + swap_halves(r) * sin
        outs[h // per][pl.ds((h % per) * block, block), :] = y.astype(jnp.bfloat16)
    scratch[...] = v_ref[...].astype(jnp.float32)
    seg = jnp.broadcast_to(seg_ref[...].astype(jnp.float32) + 1.0, (16, block)).astype(jnp.bfloat16)
    for h in range(kv_heads):
        x = scratch[pl.ds(h, block, stride=kv_heads), :]
        outs[h // per][pl.ds((per + h % per) * block, block), :] = x.astype(jnp.bfloat16)
    for out in outs:
        out[pl.ds(2 * per * block, 16), :] = seg


def query_kernel(heads, back, axis, q_ref, g_ref, gain_ref, inner_ref, outer_ref, qo_ref, go_ref, scratch):
    block = q_ref.shape[0] // heads
    cos, sin = rope_of(inner_ref, outer_ref, lax.axis_index(axis) + back)
    gain = gain_ref[...]
    scratch[...] = q_ref[...].astype(jnp.float32)
    for h in range(heads):
        x = scratch[pl.ds(h, block, stride=heads), :]
        r = x * lax.rsqrt(jnp.mean(x * x, axis=1, keepdims=True) + EPS) * gain
        y = r * cos + swap_halves(r) * sin
        qo_ref[pl.ds(h * block, block), :] = y.astype(jnp.bfloat16)
    scratch[...] = g_ref[...].astype(jnp.float32)
    for h in range(heads):
        go_ref[pl.ds(h * block, block), :] = scratch[pl.ds(h, block, stride=heads), :].astype(jnp.bfloat16)


def attend_kernel(per, group, back, q_ref, g_ref, *rest):
    blocks = rest[: back + 1]
    dq_ref, own_ref = rest[back + 1 : back + 3]
    part_refs = rest[back + 3 : 2 * back + 3]
    bias_ref = rest[-1]
    block = own_ref.shape[0] // (2 * per)
    rows = group * block
    ids = blocks[0][pl.ds(2 * per * block, 16), :].astype(jnp.float32)[0:1, :]
    ids = jnp.concatenate([ids] * group, axis=1)
    for d in range(back + 1):
        key_row = blocks[d][pl.ds(2 * per * block, 16), :].astype(jnp.float32)[0:1, :]
        key_ids = jnp.broadcast_to(key_row, (block, block)).T
        key_ids = jnp.concatenate([key_ids] * group, axis=1)
        seen = key_ids == ids
        if d == 0:
            key_at = lax.broadcasted_iota(jnp.int32, (block, rows), 0)
            query_at = lax.broadcasted_iota(jnp.int32, (block, rows), 1) & (block - 1)
            seen = seen & (key_at <= query_at)
        bias_ref[pl.ds(d * block, block), :] = jnp.where(seen, 0.0, NEG)
    for h in range(per):
        q = q_ref[pl.ds(h * rows, rows), :]
        g = g_ref[pl.ds(h * rows, rows), :]
        k = jnp.concatenate([b[pl.ds(h * block, block), :] for b in blocks], axis=0)
        v = jnp.concatenate([b[pl.ds((per + h) * block, block), :] for b in blocks], axis=0)
        scores = lax.dot_general(k, q, NT, preferred_element_type=jnp.float32)
        expo = jnp.exp2(scores * (SCALE * LOG2E) + bias_ref[...])
        prob_grads = lax.dot_general(v, g, NT, preferred_element_type=jnp.float32)
        inverse = 1.0 / jnp.sum(expo, axis=0, keepdims=True)
        delta = jnp.sum(expo * prob_grads, axis=0, keepdims=True) * inverse
        probs = expo * inverse
        score_grads = (probs * (prob_grads - delta)).astype(jnp.bfloat16)
        dv = jnp.dot(probs.astype(jnp.bfloat16), g, preferred_element_type=jnp.float32)
        dk = jnp.dot(score_grads, q, preferred_element_type=jnp.float32) * SCALE
        dq = lax.dot_general(score_grads, k, TN, preferred_element_type=jnp.float32) * SCALE
        dq_ref[pl.ds(h * rows, rows), :] = dq
        own_ref[pl.ds(h * block, block), :] = dk[:block]
        own_ref[pl.ds((per + h) * block, block), :] = dv[:block]
        for d in range(1, back + 1):
            part = part_refs[d - 1]
            part[pl.ds(h * block, block), :] = dk[d * block : (d + 1) * block].astype(jnp.bfloat16)
            part[pl.ds((per + h) * block, block), :] = dv[d * block : (d + 1) * block].astype(jnp.bfloat16)


def query_back_kernel(heads, kv_heads, groups, back, axis, *rest):
    q_ref, qgain_ref, kgain_ref, inner_ref, outer_ref = rest[:5]
    rest = rest[5:]
    dq_refs, own_refs = rest[:groups], rest[groups : 2 * groups]
    msg_refs = rest[2 * groups : (3 + back) * groups]
    part_refs = rest[(3 + back) * groups : (3 + 2 * back) * groups]
    gq_ref, gains_ref, scratch = rest[-3:]
    block = q_ref.shape[0] // heads
    width = q_ref.shape[1]
    per = kv_heads // groups
    here = lax.axis_index(axis) + back
    total = jnp.zeros((block, width), jnp.float32)
    for d in range(back + 1):
        cos, sin = rope_of(inner_ref, outer_ref, here - d)
        for g in range(groups):
            for h in range(per):
                at = pl.ds(h * block, block)
                dk = own_refs[g][at, :] if d == 0 else part_refs[g * back + d - 1][at, :].astype(jnp.float32)
                k = msg_refs[g * (back + 1) + d][at, :].astype(jnp.float32)
                total = total + unrotate(dk, cos, sin) * unrotate(k, cos, sin)
    kgain = jnp.sum(total, axis=0, keepdims=True) / kgain_ref[...]
    cos, sin = rope_of(inner_ref, outer_ref, here)
    scratch[...] = q_ref[...].astype(jnp.float32)
    gain = qgain_ref[...]
    total = jnp.zeros((block, width), jnp.float32)
    each = heads // groups
    for h in range(heads):
        x = scratch[pl.ds(h, block, stride=heads), :]
        scale = lax.rsqrt(jnp.mean(x * x, axis=1, keepdims=True) + EPS)
        normed = x * scale
        dr = unrotate(dq_refs[h // each][pl.ds((h % each) * block, block), :], cos, sin)
        total = total + dr * normed
        dn = dr * gain
        dx = scale * (dn - normed * jnp.mean(dn * normed, axis=1, keepdims=True))
        scratch[pl.ds(h, block, stride=heads), :] = dx
    gq_ref[...] = scratch[...].astype(jnp.bfloat16)
    qgain = jnp.sum(total, axis=0, keepdims=True)
    gains_ref[...] = jnp.concatenate([qgain, kgain, jnp.zeros((6, width), jnp.float32)], axis=0)


def key_back_kernel(kv_heads, groups, back, axis, *rest):
    k_ref, gain_ref, inner_ref, outer_ref = rest[:4]
    own_refs = rest[4 : 4 + groups]
    got_refs = rest[4 + groups : 4 + (1 + back) * groups]
    gk_ref, gv_ref, scratch = rest[-3:]
    block = k_ref.shape[0] // kv_heads
    per = kv_heads // groups
    cos, sin = rope_of(inner_ref, outer_ref, lax.axis_index(axis) + back)
    gain = gain_ref[...]

    def total(g, row):
        at = pl.ds(row * block, block)
        value = own_refs[g][at, :]
        for d in range(back):
            value = value + got_refs[g * back + d][at, :].astype(jnp.float32)
        return value

    scratch[...] = k_ref[...].astype(jnp.float32)
    for h in range(kv_heads):
        x = scratch[pl.ds(h, block, stride=kv_heads), :]
        scale = lax.rsqrt(jnp.mean(x * x, axis=1, keepdims=True) + EPS)
        normed = x * scale
        dn = unrotate(total(h // per, h % per), cos, sin) * gain
        dx = scale * (dn - normed * jnp.mean(dn * normed, axis=1, keepdims=True))
        scratch[pl.ds(h, block, stride=kv_heads), :] = dx
    gk_ref[...] = scratch[...].astype(jnp.bfloat16)
    for h in range(kv_heads):
        scratch[pl.ds(h, block, stride=kv_heads), :] = total(h // per, per + h % per)
    gv_ref[...] = scratch[...].astype(jnp.bfloat16)


def call(kernel, outs, scratch, cost, *args):
    vmem = pl.BlockSpec(memory_space=pltpu.VMEM)
    return pl.pallas_call(
        kernel,
        out_shape=[jax.ShapeDtypeStruct(s, t) for s, t in outs],
        in_specs=[vmem] * len(args),
        out_specs=[vmem] * len(outs),
        scratch_shapes=[pltpu.VMEM(s, jnp.float32) for s in scratch],
        compiler_params=pltpu.CompilerParams(vmem_limit_bytes=VMEM_LIMIT),
        cost_estimate=pl.CostEstimate(flops=cost, bytes_accessed=1 << 20, transcendentals=0),
    )(*args)


def sum_over(x, axis, size):
    if size & (size - 1):
        return lax.psum(x, axis)
    step = 1
    while step < size:
        x = x + lax.ppermute(x, axis, [(i, i ^ step) for i in range(size)])
        step *= 2
    return x


def by_tokens(spans, parts, q_pre, k_pre, values, grad_out, segment_ids, q_gain, k_gain):
    block, heads, width = q_pre.shape[1:]
    kv_heads = k_pre.shape[2]
    group = heads // kv_heads
    groups = GROUPS
    per = kv_heads // groups
    longest = parts * block // 2
    back = min(parts - 1, (longest - 2) // block + 1)
    bf16, f32 = jnp.bfloat16, jnp.float32
    inner, outer = rope_tables(block, width, range(-back, parts))
    q2, g2 = (x.reshape(block * heads, width) for x in (q_pre, grad_out))
    k2, v2 = (x.reshape(block * kv_heads, width) for x in (k_pre, values))
    qg, kg = q_gain.reshape(1, width), k_gain.reshape(1, width)

    message = (2 * per * block + 16, width)
    own = call(
        functools.partial(pack_kernel, kv_heads, back, "seq"),
        [(message, bf16)] * groups, [(block * kv_heads, width)], 1 << 28,
        k2, v2, segment_ids, kg, inner, outer,
    )
    window = [
        [own[g]] + [lax.ppermute(own[g], "seq", [(i, i + d) for i in range(parts - d)]) for d in range(1, back + 1)]
        for g in range(groups)
    ]
    q_rot, g_rot = call(
        functools.partial(query_kernel, heads, back, "seq"),
        [((heads * block, width), bf16)] * 2, [(heads * block, width)], 1 << 29,
        q2, g2, qg, inner, outer,
    )
    dqs, owns, shares, returned = [], [], [], []
    rows = group * block * per
    for g in range(groups):
        dq, kept, *share = call(
            functools.partial(attend_kernel, per, group, back),
            [((rows, width), f32), ((2 * per * block, width), f32)] + [((2 * per * block, width), bf16)] * back,
            [((back + 1) * block, group * block)], 1 << 30,
            lax.slice_in_dim(q_rot, g * rows, (g + 1) * rows), lax.slice_in_dim(g_rot, g * rows, (g + 1) * rows),
            *window[g],
        )
        dqs.append(dq)
        owns.append(kept)
        shares += share
        returned += [
            lax.ppermute(share[d - 1], "seq", [(i + d, i) for i in range(parts - d)]) for d in range(1, back + 1)
        ]
    grad_q, gains = call(
        functools.partial(query_back_kernel, heads, kv_heads, groups, back, "seq"),
        [((heads * block, width), bf16), ((8, width), f32)], [(heads * block, width)], 1 << 29,
        q2, qg, kg, inner, outer, *dqs, *owns, *[m for w in window for m in w], *shares,
    )
    gains = sum_over(sum_over(gains, "seq", parts), "dp", spans)
    grad_k, grad_v = call(
        functools.partial(key_back_kernel, kv_heads, groups, back, "seq"),
        [((kv_heads * block, width), bf16)] * 2, [(kv_heads * block, width)], 1 << 28,
        k2, kg, inner, outer, *owns, *returned,
    )
    return (
        grad_q.reshape(q_pre.shape),
        grad_k.reshape(k_pre.shape),
        grad_v.reshape(values.shape),
        gains[0],
        gains[1],
    )


def head_rows(refs, first, per, block):
    for ref in refs:
        for h in range(per):
            yield ref[pl.ds(first + h, block, stride=ref.shape[0] // block), :].astype(jnp.bfloat16)


def spread_keys_kernel(axis, parts, per, a_hbm, b_hbm, *rest):
    outs = rest[:parts]
    a_in, b_in, a_f32, b_f32, in_sems = rest[parts:]
    block = outs[0].shape[0] // (2 * per)
    me = lax.axis_index(axis)
    loads = [pltpu.make_async_copy(src, dst, in_sems.at[i]) for i, (src, dst) in enumerate(((a_hbm, a_in), (b_hbm, b_in)))]
    for copy in loads:
        copy.start()
    for copy, src, dst in zip(loads, (a_in, b_in), (a_f32, b_f32)):
        copy.wait()
        dst[...] = src[...].astype(jnp.float32)
    for m in range(parts):
        for i, rows in enumerate(head_rows((a_f32, b_f32), (me ^ m) * per, per, block)):
            outs[m][pl.ds(i * block, block), :] = rows


def spread_queries_kernel(axis, parts, groups, per, a_ref, b_ref, seg_ref, *rest):
    outs, a_f32, b_f32 = rest[-2 - parts * groups : -2], rest[-2], rest[-1]
    block = seg_ref.shape[1]
    ids = jnp.broadcast_to(seg_ref[...].astype(jnp.float32), (16, block)).astype(jnp.bfloat16)
    me = lax.axis_index(axis)
    for src, dst in ((a_ref, a_f32), (b_ref, b_f32)):
        dst[...] = src[...].astype(jnp.float32)
    for grp in range(groups):
        for m in range(parts):
            for i, rows in enumerate(head_rows((a_f32, b_f32), ((me ^ m) * groups + grp) * per, per, block)):
                outs[grp * parts + m][pl.ds(i * block, block), :] = rows
            outs[m][pl.ds(2 * per * block, 16), :] = ids


def turned(x):
    return x.astype(jnp.float32).T


def rotated(x, c, s):
    half = x.shape[0] // 2
    a, b = x[:half], x[half:]
    return jnp.concatenate([a * c - b * s, b * c + a * s], axis=0)


def embed(x, gain, c, s):
    scale = lax.rsqrt(jnp.sum(x * x, axis=0, keepdims=True) * (1.0 / x.shape[0]) + EPS)
    normed = x * scale
    return rotated(normed * gain, c, s).astype(jnp.bfloat16), normed, scale


def embed_back(dy, gain, c, s, normed, scale):
    dr = rotated(dy, c, -s)
    share = dr * normed
    dn = dr * gain
    mean = jnp.sum(dn * normed, axis=0, keepdims=True) * (1.0 / dy.shape[0])
    return ((scale * SCALE) * (dn - normed * mean)).astype(jnp.bfloat16), share


def rope(table_ref, b, copies):
    c, s = table_ref[b, 0], table_ref[b, 1]
    return jnp.concatenate([c] * copies, axis=1), jnp.concatenate([s] * copies, axis=1)


def gain_columns(gains_ref, row, copies):
    width = gains_ref.shape[1]
    return jnp.concatenate([jnp.broadcast_to(gains_ref[row : row + 1, :], (width, width)).T] * copies, axis=1)


def keys_kernel(axis, parts, *rest):
    msgs, table_ref, gains_ref = rest[:parts], rest[parts], rest[parts + 1]
    kt_ref, k_ref, v_ref, kn_ref, ks_ref, gain_ref = rest[parts + 2 :]
    block = table_ref.shape[3]
    owned = v_ref.shape[1]
    f32, bf16 = jnp.float32, jnp.bfloat16
    me = lax.axis_index(axis)
    gain = gain_columns(gains_ref, 1, 1)
    gain_ref[0], gain_ref[1] = gain_columns(gains_ref, 0, 1), gain
    for m in range(parts):
        b = me ^ m
        for h in range(owned):
            y, normed, scale = embed(turned(msgs[m][pl.ds(h * block, block), :]), gain, *rope(table_ref, b, 1))
            kt_ref[b, h], kn_ref[b, h], ks_ref[b, h] = y, normed, jnp.broadcast_to(scale, (8, block))
            k_ref[b, h] = turned(y).astype(bf16)
            v_ref[b, h] = msgs[m][pl.ds((owned + h) * block, block), :]


def heads_kernel(axis, parts, grp, per, group, back, *rest):
    earlier, rest = rest[: grp * parts], rest[grp * parts :]
    msgs, rest = rest[:parts], rest[parts:]
    kt_ref, k_ref, v_ref, kn_ref, ks_ref, gain_ref, table_ref = rest[:7]
    rest = rest[7:]
    if grp:
        mask_ref, rest = rest[0], rest[1:]
    outs, share_ref, rest = rest[:parts], rest[parts], rest[parts + 1 :]
    if not grp:
        mask_ref, rest = rest[0], rest[1:]
    qt_ref, g_ref, qn_ref, qs_ref, res_ref, id_ref = rest
    block, width = table_ref.shape[3], gain_ref.shape[1]
    rows = group * block
    f32, bf16 = jnp.float32, jnp.bfloat16
    me = lax.axis_index(axis)
    q_gain, k_gain = jnp.concatenate([gain_ref[0]] * group, axis=1), gain_ref[1]
    for m in range(parts):
        b = me ^ m
        if not grp:
            ids = msgs[m][pl.ds(2 * per * rows, 16), :].astype(f32)[0:1, :]
            id_ref[b] = jnp.broadcast_to(ids, (8, block))
        for p in range(per):
            at = b * per + p
            x = turned(msgs[m][pl.ds(p * rows, rows), :])
            y, normed, scale = embed(x, q_gain, *rope(table_ref, b, group))
            qt_ref[at], qn_ref[at], qs_ref[at] = y, normed, jnp.broadcast_to(scale, (8, rows))
            g_ref[at] = msgs[m][pl.ds((per + p) * rows, rows), :]

    if not grp:
        id_rows = [id_ref[b][0:1, :] for b in range(parts)]
        id_columns = [jnp.broadcast_to(row, (block, block)).T for row in id_rows]
        key_at = lax.broadcasted_iota(jnp.int32, (block, block), 0)
        query_at = lax.broadcasted_iota(jnp.int32, (block, block), 1)
        causal = jnp.where(key_at <= query_at, 0.0, NEG)
        for b in range(parts):
            for j in range(max(0, b - back), b + 1):
                value = jnp.where(id_columns[j] == id_rows[b], 0.0, NEG)
                mask_ref[b * (back + 1) + b - j] = value + causal if j == b else value

    def bias(key_block, query_block):
        return jnp.concatenate([mask_ref[query_block * (back + 1) + query_block - key_block]] * group, axis=1)

    q_total = jnp.zeros((width, rows), f32)
    k_total = jnp.zeros((width, block), f32)
    for p in range(per):
        out_base = p * (group + 2) * block
        dk = [None] * parts
        dv = [None] * parts
        spans = [range(max(0, b - back), b + 1) for b in range(parts)]
        qts = [qt_ref[b * per + p] for b in range(parts)]
        gs = [g_ref[b * per + p] for b in range(parts)]
        first = []
        for b, span in enumerate(spans):
            k = jnp.concatenate([k_ref[j, grp * per + p] for j in span], axis=0)
            v = jnp.concatenate([v_ref[j, grp * per + p] for j in span], axis=0)
            scores = jnp.dot(k, qts[b], preferred_element_type=f32)
            prob_grads = lax.dot_general(v, gs[b], NT, preferred_element_type=f32)
            first.append((scores, prob_grads))
        second = []
        for b, span in enumerate(spans):
            scores, prob_grads = first[b]
            hidden = jnp.concatenate([bias(j, b) for j in span], axis=0)
            expo = jnp.exp2(scores * (SCALE * LOG2E) + hidden)
            inverse = 1.0 / jnp.sum(expo, axis=0, keepdims=True)
            delta = jnp.sum(expo * prob_grads, axis=0, keepdims=True) * inverse
            probs = expo * inverse
            score_grads = (probs * (prob_grads - delta)).astype(bf16)
            second.append((probs.astype(bf16), score_grads))
        third = []
        for b, span in enumerate(spans):
            probs, score_grads = second[b]
            kt = jnp.concatenate([kt_ref[j, grp * per + p] for j in span], axis=1)
            third.append(jnp.dot(kt, score_grads, preferred_element_type=f32))
            dvs = jnp.dot(probs, gs[b], preferred_element_type=f32)
            dks = lax.dot_general(qts[b], score_grads, NT, preferred_element_type=f32)
            for i, j in enumerate(span):
                cut = slice(i * block, (i + 1) * block)
                dk[j] = dks[:, cut] if dk[j] is None else dk[j] + dks[:, cut]
                dv[j] = dvs[cut] if dv[j] is None else dv[j] + dvs[cut]
        for b, dq in enumerate(third):
            at = b * per + p
            dx, share = embed_back(dq, q_gain, *rope(table_ref, b, group), qn_ref[at], qs_ref[at][0:1, :])
            q_total = q_total + share
            res_ref[b, pl.ds(out_base, rows), :] = turned(dx).astype(bf16)
        for b in range(parts):
            dx, share = embed_back(dk[b], k_gain, *rope(table_ref, b, 1), kn_ref[b, grp * per + p], ks_ref[b, grp * per + p][0:1, :])
            k_total = k_total + share
            res_ref[b, pl.ds(out_base + rows, block), :] = turned(dx).astype(bf16)
            res_ref[b, pl.ds(out_base + rows + block, block), :] = dv[b].astype(bf16)
    size = res_ref.shape[1]
    for m in range(parts):
        for i in range(grp):
            outs[m][pl.ds(i * size, size), :] = earlier[i * parts + m][...]
        outs[m][pl.ds(grp * size, size), :] = res_ref[me ^ m]
    q_share = sum(q_total[:, i * block : (i + 1) * block] for i in range(group))
    q_share = jnp.sum(q_share.T, axis=0, keepdims=True)
    k_share = jnp.sum(k_total.T, axis=0, keepdims=True)
    row = lax.broadcasted_iota(jnp.int32, (8, width), 0)
    share_ref[...] = jnp.where(row == 0, q_share, jnp.where(row == 1, k_share, 0.0)) * SCALE


def collect_kernel(axis, parts, groups, heads, kv_heads, *rest):
    msgs = rest[:parts]
    gq_hbm, gk_hbm, gv_hbm, q_f32, k_f32, v_f32, q_out, k_out, v_out, sems = rest[parts:]
    group = heads // kv_heads
    per = kv_heads // parts // groups
    block = q_out.shape[0] // heads
    me = lax.axis_index(axis)
    arrays = ((q_f32, q_out, gq_hbm, heads), (k_f32, k_out, gk_hbm, kv_heads), (v_f32, v_out, gv_hbm, kv_heads))
    tokens = block // PIECES
    stores = []
    for piece in range(PIECES):
        start = piece * tokens
        for m in range(parts):
            at = start
            for grp in range(groups):
                for p in range(per):
                    kv = ((me ^ m) * groups + grp) * per + p
                    places = [(0, kv * group + i) for i in range(group)] + [(1, kv), (2, kv)]
                    for which, head in places:
                        dst, _, _, stride = arrays[which]
                        rows = msgs[m][pl.ds(at, tokens), :].astype(jnp.float32)
                        dst[pl.ds(start * stride + head, tokens, stride=stride), :] = rows
                        at += block
        for src, out, dst, stride in arrays:
            cut = pl.ds(start * stride, tokens * stride)
            out[cut, :] = src[cut, :].astype(jnp.bfloat16)
            copy = pltpu.make_async_copy(out.at[cut], dst.at[cut], sems.at[len(stores)])
            copy.start()
            stores.append(copy)
    for copy in stores:
        copy.wait()


def call_in(kernel, ins, outs, scratch, cost, *args, limit=HEADS_VMEM):
    return pl.pallas_call(
        kernel,
        out_shape=[jax.ShapeDtypeStruct(s, t) for s, t, _ in outs],
        in_specs=[pl.BlockSpec(memory_space=m) for m in ins],
        out_specs=[pl.BlockSpec(memory_space=m) for _, _, m in outs],
        scratch_shapes=scratch,
        compiler_params=pltpu.CompilerParams(vmem_limit_bytes=limit),
        cost_estimate=pl.CostEstimate(flops=cost, bytes_accessed=1 << 20, transcendentals=0),
    )(*args)


def exchange_sum(x, axis, size, *partners):
    got = [lax.ppermute(x, axis, [(i, i ^ m) for i in range(size)]) for m in partners]
    return x + got[0] if len(got) == 1 else (x + got[0]) + (got[1] + got[2])


def by_heads(spans, parts, q_pre, k_pre, values, grad_out, segment_ids, q_gain, k_gain):
    block, heads, width = q_pre.shape[1:]
    kv_heads = k_pre.shape[2]
    group = heads // kv_heads
    groups = min(GROUPS, kv_heads // parts)
    per = kv_heads // parts // groups
    rows = group * block
    longest = parts * block // 2
    back = min(parts - 1, (longest - 2) // block + 1)
    bf16, f32, vmem, hbm = jnp.bfloat16, jnp.float32, pltpu.VMEM, pltpu.HBM
    freqs = ROPE_BASE ** (-(np.arange(width // 2, dtype=np.float64) * 2.0 / width))
    angles = (np.arange(parts * block) / ROPE_FACTOR).reshape(parts, 1, block) * freqs[:, None]
    table = jnp.asarray(np.stack([np.cos(angles), np.sin(angles)], axis=1).astype(np.float32))
    q2, g2 = (x.reshape(block * heads, width) for x in (q_pre, grad_out))
    k2, v2 = (x.reshape(block * kv_heads, width) for x in (k_pre, values))
    owned = kv_heads // parts
    kv_sent = (2 * owned * block, width)
    sent = (per * 2 * rows, width)
    back_sent = (per * (group + 2) * block, width)
    dma = pltpu.SemaphoreType.DMA
    q_shape, k_shape = q2.shape, k2.shape

    xor = lambda m, size: [(i, i ^ m) for i in range(size)]
    send = lambda out: [out[0]] + [lax.ppermute(out[m], "seq", xor(m, parts)) for m in range(1, parts)]
    kv_messages = call_in(
        functools.partial(spread_keys_kernel, "seq", parts, owned),
        [hbm] * 2, [(kv_sent, bf16, vmem)] * parts,
        [vmem(k_shape, bf16), vmem(k_shape, bf16), vmem(k_shape, f32), vmem(k_shape, f32), dma((2,))],
        1 << 20, k2, v2, limit=SPREAD_VMEM,
    )
    kv_arrived = send(kv_messages)
    messages = call_in(
        functools.partial(spread_queries_kernel, "seq", parts, groups, per * group),
        [vmem] * 3, [((sent[0] + 16, width), bf16, vmem)] * (parts * groups),
        [vmem(q_shape, f32), vmem(q_shape, f32)], 1 << 33, q2, g2, segment_ids,
    )
    arrived = [send(messages[grp * parts : (grp + 1) * parts]) for grp in range(groups)]
    gains = jnp.concatenate([q_gain[None], k_gain[None], jnp.zeros((6, width), f32)], axis=0)
    held = (parts, owned)
    keys = call_in(
        functools.partial(keys_kernel, "seq", parts), [vmem] * (parts + 2),
        [((*held, width, block), bf16, vmem), ((*held, block, width), bf16, vmem), ((*held, block, width), bf16, vmem)]
        + [((*held, width, block), f32, vmem), ((*held, 8, block), f32, vmem), ((2, width, block), f32, vmem)],
        [], 1 << 33, *kv_arrived, table, gains,
    )
    results, shares, masks = [], [], []
    for grp in range(groups):
        inputs = [*results, *arrived[grp], *keys, table, *masks]
        mask_shape = ((parts * (back + 1), block, block), f32, vmem)
        made = call_in(
            functools.partial(heads_kernel, "seq", parts, grp, per, group, back),
            [vmem] * len(inputs),
            [(((grp + 1) * back_sent[0], width), bf16, vmem)] * parts + [((8, width), f32, vmem)] + [mask_shape] * (grp == 0),
            [vmem((parts * per, width, rows), bf16), vmem((parts * per, rows, width), bf16)]
            + [vmem((parts * per, width, rows), f32), vmem((parts * per, 8, rows), f32), vmem((parts, *back_sent), bf16)]
            + [vmem((parts, 8, block), f32)],
            1 << 34, *inputs,
        )
        results, share, masks = made[:parts], made[parts], made[parts + 1 :] or masks
        shares.append(share)
    go = lambda m: lax.ppermute(results[m], "seq", xor(m, parts))
    total = functools.reduce(jnp.add, shares)
    first, second, third = go(1), go(2), go(3)
    total = exchange_sum(total, "seq", parts, 1, 2, 3)
    total = exchange_sum(exchange_sum(exchange_sum(total, "dp", spans, 1), "dp", spans, 2), "dp", spans, 4)
    grad_q, grad_k, grad_v = call_in(
        functools.partial(collect_kernel, "seq", parts, groups, heads, kv_heads),
        [vmem] * parts, [(q_shape, bf16, hbm), (k_shape, bf16, hbm), (k_shape, bf16, hbm)],
        [vmem(q_shape, f32), vmem(k_shape, f32), vmem(k_shape, f32)]
        + [vmem(q_shape, bf16), vmem(k_shape, bf16), vmem(k_shape, bf16), dma((3 * PIECES,))],
        1 << 20, results[0], first, second, third,
    )
    return (
        grad_q.reshape(q_pre.shape), grad_k.reshape(k_pre.shape), grad_v.reshape(values.shape), total[0], total[1],
    )


def solution(mesh):
    tokens = P("dp", "seq", None, None)
    spans, parts = mesh.shape["dp"], mesh.shape["seq"]
    body = by_heads if (spans, parts) == (8, 4) else by_tokens
    return jax.shard_map(
        functools.partial(body, spans, parts),
        mesh=mesh,
        in_specs=(tokens, tokens, tokens, tokens, P("dp", "seq"), P(), P()),
        out_specs=(tokens, tokens, tokens, P(), P()),
        check_vma=False,
    )
```

```python
import functools

import jax
import jax.numpy as jnp
import numpy as np
from jax import lax
from jax.experimental import pallas as pl
from jax.experimental.pallas import tpu as pltpu
from jax.sharding import PartitionSpec as P

PRESCALE = 168
EPS = 1e-06
ROPE_BASE = 1000000.0
ROPE_FACTOR = 8.0
GROUPS = 2
PIECES = 4
NEG = -1e30
SCALE = float(PRESCALE) ** (-0.5)
LOG2E = 1.4426950408889634
VMEM_LIMIT = 48 * 1024 * 1024
HEADS_VMEM = 24 * 1024 * 1024
SPREAD_VMEM = 426 * 128 * 1024
NT = (((1,), (1,)), ((), ()))
TN = (((0,), (0,)), ((), ()))


def rope_tables(block, width, blocks):
    half = width // 2
    freqs = ROPE_BASE ** (-(np.arange(half, dtype=np.float64) * 2.0 / width))
    freqs = np.concatenate([freqs, freqs])
    inner = (np.arange(block) / ROPE_FACTOR)[:, None] * freqs[None, :]
    outer = (np.asarray(blocks) * block / ROPE_FACTOR)[:, None] * freqs[None, :]
    f32 = lambda x: jnp.asarray(x.astype(np.float32))
    return f32(np.stack([np.cos(inner), np.sin(inner)])), f32(np.stack([np.cos(outer), np.sin(outer)], axis=1))


def rope_of(inner_ref, outer_ref, row):
    both = outer_ref[row]
    cb, sb = both[0:1, :], both[1:2, :]
    ct, st = inner_ref[0], inner_ref[1]
    cos = ct * cb - st * sb
    sin = st * cb + ct * sb
    lane = lax.broadcasted_iota(jnp.int32, sin.shape, 1)
    return cos, jnp.where(lane < sin.shape[1] // 2, -sin, sin)


def swap_halves(x):
    return pltpu.roll(x, x.shape[1] // 2, 1)


def unrotate(y, cos, sin):
    return y * cos + swap_halves(y * sin)


def pack_kernel(kv_heads, back, axis, k_ref, v_ref, seg_ref, gain_ref, inner_ref, outer_ref, *rest):
    outs, scratch = rest[:-1], rest[-1]
    block = seg_ref.shape[1]
    per = kv_heads // len(outs)
    cos, sin = rope_of(inner_ref, outer_ref, lax.axis_index(axis) + back)
    gain = gain_ref[...]
    scratch[...] = k_ref[...].astype(jnp.float32)
    for h in range(kv_heads):
        x = scratch[pl.ds(h, block, stride=kv_heads), :]
        r = x * lax.rsqrt(jnp.mean(x * x, axis=1, keepdims=True) + EPS) * gain
        y = r * cos + swap_halves(r) * sin
        outs[h // per][pl.ds((h % per) * block, block), :] = y.astype(jnp.bfloat16)
    scratch[...] = v_ref[...].astype(jnp.float32)
    seg = jnp.broadcast_to(seg_ref[...].astype(jnp.float32) + 1.0, (16, block)).astype(jnp.bfloat16)
    for h in range(kv_heads):
        x = scratch[pl.ds(h, block, stride=kv_heads), :]
        outs[h // per][pl.ds((per + h % per) * block, block), :] = x.astype(jnp.bfloat16)
    for out in outs:
        out[pl.ds(2 * per * block, 16), :] = seg


def query_kernel(heads, back, axis, q_ref, g_ref, gain_ref, inner_ref, outer_ref, qo_ref, go_ref, scratch):
    block = q_ref.shape[0] // heads
    cos, sin = rope_of(inner_ref, outer_ref, lax.axis_index(axis) + back)
    gain = gain_ref[...]
    scratch[...] = q_ref[...].astype(jnp.float32)
    for h in range(heads):
        x = scratch[pl.ds(h, block, stride=heads), :]
        r = x * lax.rsqrt(jnp.mean(x * x, axis=1, keepdims=True) + EPS) * gain
        y = r * cos + swap_halves(r) * sin
        qo_ref[pl.ds(h * block, block), :] = y.astype(jnp.bfloat16)
    scratch[...] = g_ref[...].astype(jnp.float32)
    for h in range(heads):
        go_ref[pl.ds(h * block, block), :] = scratch[pl.ds(h, block, stride=heads), :].astype(jnp.bfloat16)


def attend_kernel(per, group, back, q_ref, g_ref, *rest):
    blocks = rest[: back + 1]
    dq_ref, own_ref = rest[back + 1 : back + 3]
    part_refs = rest[back + 3 : 2 * back + 3]
    bias_ref = rest[-1]
    block = own_ref.shape[0] // (2 * per)
    rows = group * block
    ids = blocks[0][pl.ds(2 * per * block, 16), :].astype(jnp.float32)[0:1, :]
    ids = jnp.concatenate([ids] * group, axis=1)
    for d in range(back + 1):
        key_row = blocks[d][pl.ds(2 * per * block, 16), :].astype(jnp.float32)[0:1, :]
        key_ids = jnp.broadcast_to(key_row, (block, block)).T
        key_ids = jnp.concatenate([key_ids] * group, axis=1)
        seen = key_ids == ids
        if d == 0:
            key_at = lax.broadcasted_iota(jnp.int32, (block, rows), 0)
            query_at = lax.broadcasted_iota(jnp.int32, (block, rows), 1) & (block - 1)
            seen = seen & (key_at <= query_at)
        bias_ref[pl.ds(d * block, block), :] = jnp.where(seen, 0.0, NEG)
    for h in range(per):
        q = q_ref[pl.ds(h * rows, rows), :]
        g = g_ref[pl.ds(h * rows, rows), :]
        k = jnp.concatenate([b[pl.ds(h * block, block), :] for b in blocks], axis=0)
        v = jnp.concatenate([b[pl.ds((per + h) * block, block), :] for b in blocks], axis=0)
        scores = lax.dot_general(k, q, NT, preferred_element_type=jnp.float32)
        expo = jnp.exp2(scores * (SCALE * LOG2E) + bias_ref[...])
        prob_grads = lax.dot_general(v, g, NT, preferred_element_type=jnp.float32)
        inverse = 1.0 / jnp.sum(expo, axis=0, keepdims=True)
        delta = jnp.sum(expo * prob_grads, axis=0, keepdims=True) * inverse
        probs = expo * inverse
        score_grads = (probs * (prob_grads - delta)).astype(jnp.bfloat16)
        dv = jnp.dot(probs.astype(jnp.bfloat16), g, preferred_element_type=jnp.float32)
        dk = jnp.dot(score_grads, q, preferred_element_type=jnp.float32) * SCALE
        dq = lax.dot_general(score_grads, k, TN, preferred_element_type=jnp.float32) * SCALE
        dq_ref[pl.ds(h * rows, rows), :] = dq
        own_ref[pl.ds(h * block, block), :] = dk[:block]
        own_ref[pl.ds((per + h) * block, block), :] = dv[:block]
        for d in range(1, back + 1):
            part = part_refs[d - 1]
            part[pl.ds(h * block, block), :] = dk[d * block : (d + 1) * block].astype(jnp.bfloat16)
            part[pl.ds((per + h) * block, block), :] = dv[d * block : (d + 1) * block].astype(jnp.bfloat16)


def query_back_kernel(heads, kv_heads, groups, back, axis, *rest):
    q_ref, qgain_ref, kgain_ref, inner_ref, outer_ref = rest[:5]
    rest = rest[5:]
    dq_refs, own_refs = rest[:groups], rest[groups : 2 * groups]
    msg_refs = rest[2 * groups : (3 + back) * groups]
    part_refs = rest[(3 + back) * groups : (3 + 2 * back) * groups]
    gq_ref, gains_ref, scratch = rest[-3:]
    block = q_ref.shape[0] // heads
    width = q_ref.shape[1]
    per = kv_heads // groups
    here = lax.axis_index(axis) + back
    total = jnp.zeros((block, width), jnp.float32)
    for d in range(back + 1):
        cos, sin = rope_of(inner_ref, outer_ref, here - d)
        for g in range(groups):
            for h in range(per):
                at = pl.ds(h * block, block)
                dk = own_refs[g][at, :] if d == 0 else part_refs[g * back + d - 1][at, :].astype(jnp.float32)
                k = msg_refs[g * (back + 1) + d][at, :].astype(jnp.float32)
                total = total + unrotate(dk, cos, sin) * unrotate(k, cos, sin)
    kgain = jnp.sum(total, axis=0, keepdims=True) / kgain_ref[...]
    cos, sin = rope_of(inner_ref, outer_ref, here)
    scratch[...] = q_ref[...].astype(jnp.float32)
    gain = qgain_ref[...]
    total = jnp.zeros((block, width), jnp.float32)
    each = heads // groups
    for h in range(heads):
        x = scratch[pl.ds(h, block, stride=heads), :]
        scale = lax.rsqrt(jnp.mean(x * x, axis=1, keepdims=True) + EPS)
        normed = x * scale
        dr = unrotate(dq_refs[h // each][pl.ds((h % each) * block, block), :], cos, sin)
        total = total + dr * normed
        dn = dr * gain
        dx = scale * (dn - normed * jnp.mean(dn * normed, axis=1, keepdims=True))
        scratch[pl.ds(h, block, stride=heads), :] = dx
    gq_ref[...] = scratch[...].astype(jnp.bfloat16)
    qgain = jnp.sum(total, axis=0, keepdims=True)
    gains_ref[...] = jnp.concatenate([qgain, kgain, jnp.zeros((6, width), jnp.float32)], axis=0)


def key_back_kernel(kv_heads, groups, back, axis, *rest):
    k_ref, gain_ref, inner_ref, outer_ref = rest[:4]
    own_refs = rest[4 : 4 + groups]
    got_refs = rest[4 + groups : 4 + (1 + back) * groups]
    gk_ref, gv_ref, scratch = rest[-3:]
    block = k_ref.shape[0] // kv_heads
    per = kv_heads // groups
    cos, sin = rope_of(inner_ref, outer_ref, lax.axis_index(axis) + back)
    gain = gain_ref[...]

    def total(g, row):
        at = pl.ds(row * block, block)
        value = own_refs[g][at, :]
        for d in range(back):
            value = value + got_refs[g * back + d][at, :].astype(jnp.float32)
        return value

    scratch[...] = k_ref[...].astype(jnp.float32)
    for h in range(kv_heads):
        x = scratch[pl.ds(h, block, stride=kv_heads), :]
        scale = lax.rsqrt(jnp.mean(x * x, axis=1, keepdims=True) + EPS)
        normed = x * scale
        dn = unrotate(total(h // per, h % per), cos, sin) * gain
        dx = scale * (dn - normed * jnp.mean(dn * normed, axis=1, keepdims=True))
        scratch[pl.ds(h, block, stride=kv_heads), :] = dx
    gk_ref[...] = scratch[...].astype(jnp.bfloat16)
    for h in range(kv_heads):
        scratch[pl.ds(h, block, stride=kv_heads), :] = total(h // per, per + h % per)
    gv_ref[...] = scratch[...].astype(jnp.bfloat16)


def call(kernel, outs, scratch, cost, *args):
    vmem = pl.BlockSpec(memory_space=pltpu.VMEM)
    return pl.pallas_call(
        kernel,
        out_shape=[jax.ShapeDtypeStruct(s, t) for s, t in outs],
        in_specs=[vmem] * len(args),
        out_specs=[vmem] * len(outs),
        scratch_shapes=[pltpu.VMEM(s, jnp.float32) for s in scratch],
        compiler_params=pltpu.CompilerParams(vmem_limit_bytes=VMEM_LIMIT),
        cost_estimate=pl.CostEstimate(flops=cost, bytes_accessed=1 << 20, transcendentals=0),
    )(*args)


def sum_over(x, axis, size):
    if size & (size - 1):
        return lax.psum(x, axis)
    step = 1
    while step < size:
        x = x + lax.ppermute(x, axis, [(i, i ^ step) for i in range(size)])
        step *= 2
    return x


def by_tokens(spans, parts, q_pre, k_pre, values, grad_out, segment_ids, q_gain, k_gain):
    block, heads, width = q_pre.shape[1:]
    kv_heads = k_pre.shape[2]
    group = heads // kv_heads
    groups = GROUPS
    per = kv_heads // groups
    longest = parts * block // 2
    back = min(parts - 1, (longest - 2) // block + 1)
    bf16, f32 = jnp.bfloat16, jnp.float32
    inner, outer = rope_tables(block, width, range(-back, parts))
    q2, g2 = (x.reshape(block * heads, width) for x in (q_pre, grad_out))
    k2, v2 = (x.reshape(block * kv_heads, width) for x in (k_pre, values))
    qg, kg = q_gain.reshape(1, width), k_gain.reshape(1, width)

    message = (2 * per * block + 16, width)
    own = call(
        functools.partial(pack_kernel, kv_heads, back, "seq"),
        [(message, bf16)] * groups, [(block * kv_heads, width)], 1 << 28,
        k2, v2, segment_ids, kg, inner, outer,
    )
    window = [
        [own[g]] + [lax.ppermute(own[g], "seq", [(i, i + d) for i in range(parts - d)]) for d in range(1, back + 1)]
        for g in range(groups)
    ]
    q_rot, g_rot = call(
        functools.partial(query_kernel, heads, back, "seq"),
        [((heads * block, width), bf16)] * 2, [(heads * block, width)], 1 << 29,
        q2, g2, qg, inner, outer,
    )
    dqs, owns, shares, returned = [], [], [], []
    rows = group * block * per
    for g in range(groups):
        dq, kept, *share = call(
            functools.partial(attend_kernel, per, group, back),
            [((rows, width), f32), ((2 * per * block, width), f32)] + [((2 * per * block, width), bf16)] * back,
            [((back + 1) * block, group * block)], 1 << 30,
            lax.slice_in_dim(q_rot, g * rows, (g + 1) * rows), lax.slice_in_dim(g_rot, g * rows, (g + 1) * rows),
            *window[g],
        )
        dqs.append(dq)
        owns.append(kept)
        shares += share
        returned += [
            lax.ppermute(share[d - 1], "seq", [(i + d, i) for i in range(parts - d)]) for d in range(1, back + 1)
        ]
    grad_q, gains = call(
        functools.partial(query_back_kernel, heads, kv_heads, groups, back, "seq"),
        [((heads * block, width), bf16), ((8, width), f32)], [(heads * block, width)], 1 << 29,
        q2, qg, kg, inner, outer, *dqs, *owns, *[m for w in window for m in w], *shares,
    )
    gains = sum_over(sum_over(gains, "seq", parts), "dp", spans)
    grad_k, grad_v = call(
        functools.partial(key_back_kernel, kv_heads, groups, back, "seq"),
        [((kv_heads * block, width), bf16)] * 2, [(kv_heads * block, width)], 1 << 28,
        k2, kg, inner, outer, *owns, *returned,
    )
    return (
        grad_q.reshape(q_pre.shape),
        grad_k.reshape(k_pre.shape),
        grad_v.reshape(values.shape),
        gains[0],
        gains[1],
    )


def head_rows(refs, first, per, block):
    for ref in refs:
        for h in range(per):
            yield ref[pl.ds(first + h, block, stride=ref.shape[0] // block), :].astype(jnp.bfloat16)


def spread_keys_kernel(axis, parts, per, a_hbm, b_hbm, *rest):
    outs = rest[:parts]
    a_in, b_in, a_f32, b_f32, in_sems = rest[parts:]
    block = outs[0].shape[0] // (2 * per)
    me = lax.axis_index(axis)
    loads = [pltpu.make_async_copy(src, dst, in_sems.at[i]) for i, (src, dst) in enumerate(((a_hbm, a_in), (b_hbm, b_in)))]
    for copy in loads:
        copy.start()
    for copy, src, dst in zip(loads, (a_in, b_in), (a_f32, b_f32)):
        copy.wait()
        dst[...] = src[...].astype(jnp.float32)
    for m in range(parts):
        for i, rows in enumerate(head_rows((a_f32, b_f32), (me ^ m) * per, per, block)):
            outs[m][pl.ds(i * block, block), :] = rows


def spread_queries_kernel(axis, parts, groups, per, a_ref, b_ref, seg_ref, *rest):
    outs, a_f32, b_f32 = rest[-2 - parts * groups : -2], rest[-2], rest[-1]
    block = seg_ref.shape[1]
    ids = jnp.broadcast_to(seg_ref[...].astype(jnp.float32), (16, block)).astype(jnp.bfloat16)
    me = lax.axis_index(axis)
    for src, dst in ((a_ref, a_f32), (b_ref, b_f32)):
        dst[...] = src[...].astype(jnp.float32)
    for grp in range(groups):
        for m in range(parts):
            for i, rows in enumerate(head_rows((a_f32, b_f32), ((me ^ m) * groups + grp) * per, per, block)):
                outs[grp * parts + m][pl.ds(i * block, block), :] = rows
            outs[m][pl.ds(2 * per * block, 16), :] = ids


def turned(x):
    return x.astype(jnp.float32).T


def rotated(x, c, s):
    half = x.shape[0] // 2
    a, b = x[:half], x[half:]
    return jnp.concatenate([a * c - b * s, b * c + a * s], axis=0)


def embed(x, gain, c, s):
    scale = lax.rsqrt(jnp.sum(x * x, axis=0, keepdims=True) * (1.0 / x.shape[0]) + EPS)
    normed = x * scale
    return rotated(normed * gain, c, s).astype(jnp.bfloat16), normed, scale


def embed_back(dy, gain, c, s, normed, scale):
    dr = rotated(dy, c, -s)
    share = dr * normed
    dn = dr * gain
    mean = jnp.sum(dn * normed, axis=0, keepdims=True) * (1.0 / dy.shape[0])
    return ((scale * SCALE) * (dn - normed * mean)).astype(jnp.bfloat16), share


def rope(table_ref, b, copies):
    c, s = table_ref[b, 0], table_ref[b, 1]
    return jnp.concatenate([c] * copies, axis=1), jnp.concatenate([s] * copies, axis=1)


def gain_columns(gains_ref, row, copies):
    width = gains_ref.shape[1]
    return jnp.concatenate([jnp.broadcast_to(gains_ref[row : row + 1, :], (width, width)).T] * copies, axis=1)


def keys_kernel(axis, parts, *rest):
    msgs, table_ref, gains_ref = rest[:parts], rest[parts], rest[parts + 1]
    kt_ref, k_ref, v_ref, kn_ref, ks_ref = rest[parts + 2 :]
    block = table_ref.shape[3]
    owned = v_ref.shape[1]
    f32, bf16 = jnp.float32, jnp.bfloat16
    me = lax.axis_index(axis)
    gain = gain_columns(gains_ref, 1, 1)
    for m in range(parts):
        b = me ^ m
        for h in range(owned):
            y, normed, scale = embed(turned(msgs[m][pl.ds(h * block, block), :]), gain, *rope(table_ref, b, 1))
            kt_ref[b, h], kn_ref[b, h], ks_ref[b, h] = y, normed, jnp.broadcast_to(scale, (8, block))
            k_ref[b, h] = turned(y).astype(bf16)
            v_ref[b, h] = msgs[m][pl.ds((owned + h) * block, block), :]


def heads_kernel(axis, parts, grp, per, group, back, *rest):
    earlier, rest = rest[: grp * parts], rest[grp * parts :]
    msgs, rest = rest[:parts], rest[parts:]
    kt_ref, k_ref, v_ref, kn_ref, ks_ref, table_ref, gains_ref = rest[:7]
    rest = rest[7:]
    if grp:
        id_ref, rest = rest[0], rest[1:]
    outs, share_ref, rest = rest[:parts], rest[parts], rest[parts + 1 :]
    if not grp:
        id_ref, rest = rest[0], rest[1:]
    qt_ref, g_ref, qn_ref, qs_ref, res_ref = rest
    block, width = table_ref.shape[3], gains_ref.shape[1]
    rows = group * block
    f32, bf16 = jnp.float32, jnp.bfloat16
    me = lax.axis_index(axis)
    q_gain, k_gain = gain_columns(gains_ref, 0, group), gain_columns(gains_ref, 1, 1)
    for m in range(parts):
        b = me ^ m
        if not grp:
            ids = msgs[m][pl.ds(2 * per * rows, 16), :].astype(f32)[0:1, :]
            id_ref[b] = jnp.broadcast_to(ids, (8, block))
        for p in range(per):
            at = b * per + p
            x = turned(msgs[m][pl.ds(p * rows, rows), :])
            y, normed, scale = embed(x, q_gain, *rope(table_ref, b, group))
            qt_ref[at], qn_ref[at], qs_ref[at] = y, normed, jnp.broadcast_to(scale, (8, rows))
            g_ref[at] = msgs[m][pl.ds((per + p) * rows, rows), :]

    id_rows = [id_ref[b][0:1, :] for b in range(parts)]
    id_columns = [jnp.broadcast_to(row, (block, block)).T for row in id_rows]
    key_at = lax.broadcasted_iota(jnp.int32, (block, block), 0)
    query_at = lax.broadcasted_iota(jnp.int32, (block, block), 1)
    causal = jnp.where(key_at <= query_at, 0.0, NEG)

    def bias(key_block, query_block):
        value = jnp.where(id_columns[key_block] == id_rows[query_block], 0.0, NEG)
        if key_block == query_block:
            value = value + causal
        return jnp.concatenate([value] * group, axis=1)

    q_total = jnp.zeros((width, rows), f32)
    k_total = jnp.zeros((width, block), f32)
    for p in range(per):
        out_base = p * (group + 2) * block
        dk = [None] * parts
        dv = [None] * parts
        spans = [range(max(0, b - back), b + 1) for b in range(parts)]
        qts = [qt_ref[b * per + p] for b in range(parts)]
        gs = [g_ref[b * per + p] for b in range(parts)]
        first = []
        for b, span in enumerate(spans):
            k = jnp.concatenate([k_ref[j, grp * per + p] for j in span], axis=0)
            v = jnp.concatenate([v_ref[j, grp * per + p] for j in span], axis=0)
            scores = jnp.dot(k, qts[b], preferred_element_type=f32)
            prob_grads = lax.dot_general(v, gs[b], NT, preferred_element_type=f32)
            first.append((scores, prob_grads))
        second = []
        for b, span in enumerate(spans):
            scores, prob_grads = first[b]
            hidden = jnp.concatenate([bias(j, b) for j in span], axis=0)
            expo = jnp.exp2(scores * (SCALE * LOG2E) + hidden)
            inverse = 1.0 / jnp.sum(expo, axis=0, keepdims=True)
            delta = jnp.sum(expo * prob_grads, axis=0, keepdims=True) * inverse
            probs = expo * inverse
            score_grads = (probs * (prob_grads - delta)).astype(bf16)
            second.append((probs.astype(bf16), score_grads))
        third = []
        for b, span in enumerate(spans):
            probs, score_grads = second[b]
            kt = jnp.concatenate([kt_ref[j, grp * per + p] for j in span], axis=1)
            third.append(jnp.dot(kt, score_grads, preferred_element_type=f32))
            dvs = jnp.dot(probs, gs[b], preferred_element_type=f32)
            dks = lax.dot_general(qts[b], score_grads, NT, preferred_element_type=f32)
            for i, j in enumerate(span):
                cut = slice(i * block, (i + 1) * block)
                dk[j] = dks[:, cut] if dk[j] is None else dk[j] + dks[:, cut]
                dv[j] = dvs[cut] if dv[j] is None else dv[j] + dvs[cut]
        for b, dq in enumerate(third):
            at = b * per + p
            dx, share = embed_back(dq, q_gain, *rope(table_ref, b, group), qn_ref[at], qs_ref[at][0:1, :])
            q_total = q_total + share
            res_ref[b, pl.ds(out_base, rows), :] = turned(dx).astype(bf16)
        for b in range(parts):
            dx, share = embed_back(dk[b], k_gain, *rope(table_ref, b, 1), kn_ref[b, grp * per + p], ks_ref[b, grp * per + p][0:1, :])
            k_total = k_total + share
            res_ref[b, pl.ds(out_base + rows, block), :] = turned(dx).astype(bf16)
            res_ref[b, pl.ds(out_base + rows + block, block), :] = dv[b].astype(bf16)
    size = res_ref.shape[1]
    for m in range(parts):
        for i in range(grp):
            outs[m][pl.ds(i * size, size), :] = earlier[i * parts + m][...]
        outs[m][pl.ds(grp * size, size), :] = res_ref[me ^ m]
    q_share = sum(q_total[:, i * block : (i + 1) * block] for i in range(group))
    q_share = jnp.sum(q_share.T, axis=0, keepdims=True)
    k_share = jnp.sum(k_total.T, axis=0, keepdims=True)
    row = lax.broadcasted_iota(jnp.int32, (8, width), 0)
    share_ref[...] = jnp.where(row == 0, q_share, jnp.where(row == 1, k_share, 0.0)) * SCALE


def collect_kernel(axis, parts, groups, heads, kv_heads, *rest):
    msgs = rest[:parts]
    gq_hbm, gk_hbm, gv_hbm, q_f32, k_f32, v_f32, q_out, k_out, v_out, sems = rest[parts:]
    group = heads // kv_heads
    per = kv_heads // parts // groups
    block = q_out.shape[0] // heads
    me = lax.axis_index(axis)
    arrays = ((q_f32, q_out, gq_hbm, heads), (k_f32, k_out, gk_hbm, kv_heads), (v_f32, v_out, gv_hbm, kv_heads))
    tokens = block // PIECES
    stores = []
    for piece in range(PIECES):
        start = piece * tokens
        for m in range(parts):
            at = start
            for grp in range(groups):
                for p in range(per):
                    kv = ((me ^ m) * groups + grp) * per + p
                    places = [(0, kv * group + i) for i in range(group)] + [(1, kv), (2, kv)]
                    for which, head in places:
                        dst, _, _, stride = arrays[which]
                        rows = msgs[m][pl.ds(at, tokens), :].astype(jnp.float32)
                        dst[pl.ds(start * stride + head, tokens, stride=stride), :] = rows
                        at += block
        for src, out, dst, stride in arrays:
            cut = pl.ds(start * stride, tokens * stride)
            out[cut, :] = src[cut, :].astype(jnp.bfloat16)
            copy = pltpu.make_async_copy(out.at[cut], dst.at[cut], sems.at[len(stores)])
            copy.start()
            stores.append(copy)
    for copy in stores:
        copy.wait()


def call_in(kernel, ins, outs, scratch, cost, *args, limit=HEADS_VMEM):
    return pl.pallas_call(
        kernel,
        out_shape=[jax.ShapeDtypeStruct(s, t) for s, t, _ in outs],
        in_specs=[pl.BlockSpec(memory_space=m) for m in ins],
        out_specs=[pl.BlockSpec(memory_space=m) for _, _, m in outs],
        scratch_shapes=scratch,
        compiler_params=pltpu.CompilerParams(vmem_limit_bytes=limit),
        cost_estimate=pl.CostEstimate(flops=cost, bytes_accessed=1 << 20, transcendentals=0),
    )(*args)


def exchange_sum(x, axis, size, *partners):
    got = [lax.ppermute(x, axis, [(i, i ^ m) for i in range(size)]) for m in partners]
    return x + got[0] if len(got) == 1 else (x + got[0]) + (got[1] + got[2])


def by_heads(spans, parts, q_pre, k_pre, values, grad_out, segment_ids, q_gain, k_gain):
    block, heads, width = q_pre.shape[1:]
    kv_heads = k_pre.shape[2]
    group = heads // kv_heads
    groups = min(GROUPS, kv_heads // parts)
    per = kv_heads // parts // groups
    rows = group * block
    longest = parts * block // 2
    back = min(parts - 1, (longest - 2) // block + 1)
    bf16, f32, vmem, hbm = jnp.bfloat16, jnp.float32, pltpu.VMEM, pltpu.HBM
    freqs = ROPE_BASE ** (-(np.arange(width // 2, dtype=np.float64) * 2.0 / width))
    angles = (np.arange(parts * block) / ROPE_FACTOR).reshape(parts, 1, block) * freqs[:, None]
    table = jnp.asarray(np.stack([np.cos(angles), np.sin(angles)], axis=1).astype(np.float32))
    q2, g2 = (x.reshape(block * heads, width) for x in (q_pre, grad_out))
    k2, v2 = (x.reshape(block * kv_heads, width) for x in (k_pre, values))
    owned = kv_heads // parts
    kv_sent = (2 * owned * block, width)
    sent = (per * 2 * rows, width)
    back_sent = (per * (group + 2) * block, width)
    dma = pltpu.SemaphoreType.DMA
    q_shape, k_shape = q2.shape, k2.shape

    xor = lambda m, size: [(i, i ^ m) for i in range(size)]
    send = lambda out: [out[0]] + [lax.ppermute(out[m], "seq", xor(m, parts)) for m in range(1, parts)]
    kv_messages = call_in(
        functools.partial(spread_keys_kernel, "seq", parts, owned),
        [hbm] * 2, [(kv_sent, bf16, vmem)] * parts,
        [vmem(k_shape, bf16), vmem(k_shape, bf16), vmem(k_shape, f32), vmem(k_shape, f32), dma((2,))],
        1 << 20, k2, v2, limit=SPREAD_VMEM,
    )
    kv_arrived = send(kv_messages)
    messages = call_in(
        functools.partial(spread_queries_kernel, "seq", parts, groups, per * group),
        [vmem] * 3, [((sent[0] + 16, width), bf16, vmem)] * (parts * groups),
        [vmem(q_shape, f32), vmem(q_shape, f32)], 1 << 33, q2, g2, segment_ids,
    )
    arrived = [send(messages[grp * parts : (grp + 1) * parts]) for grp in range(groups)]
    gains = jnp.concatenate([q_gain[None], k_gain[None], jnp.zeros((6, width), f32)], axis=0)
    held = (parts, owned)
    keys = call_in(
        functools.partial(keys_kernel, "seq", parts), [vmem] * (parts + 2),
        [((*held, width, block), bf16, vmem), ((*held, block, width), bf16, vmem), ((*held, block, width), bf16, vmem)]
        + [((*held, width, block), f32, vmem), ((*held, 8, block), f32, vmem)],
        [], 1 << 33, *kv_arrived, table, gains,
    )
    results, shares, ids = [], [], []
    for grp in range(groups):
        inputs = [*results, *arrived[grp], *keys, table, gains, *ids]
        id_shape = ((parts, 8, block), f32, vmem)
        made = call_in(
            functools.partial(heads_kernel, "seq", parts, grp, per, group, back),
            [vmem] * len(inputs),
            [(((grp + 1) * back_sent[0], width), bf16, vmem)] * parts + [((8, width), f32, vmem)] + [id_shape] * (grp == 0),
            [vmem((parts * per, width, rows), bf16), vmem((parts * per, rows, width), bf16)]
            + [vmem((parts * per, width, rows), f32), vmem((parts * per, 8, rows), f32), vmem((parts, *back_sent), bf16)],
            1 << 34, *inputs,
        )
        results, share, ids = made[:parts], made[parts], made[parts + 1 :] or ids
        shares.append(share)
    go = lambda m: lax.ppermute(results[m], "seq", xor(m, parts))
    total = functools.reduce(jnp.add, shares)
    third, first, second = go(3), go(1), go(2)
    total = exchange_sum(total, "seq", parts, 1, 2, 3)
    total = exchange_sum(exchange_sum(exchange_sum(total, "dp", spans, 1), "dp", spans, 4), "dp", spans, 2)
    grad_q, grad_k, grad_v = call_in(
        functools.partial(collect_kernel, "seq", parts, groups, heads, kv_heads),
        [vmem] * parts, [(q_shape, bf16, hbm), (k_shape, bf16, hbm), (k_shape, bf16, hbm)],
        [vmem(q_shape, f32), vmem(k_shape, f32), vmem(k_shape, f32)]
        + [vmem(q_shape, bf16), vmem(k_shape, bf16), vmem(k_shape, bf16), dma((3 * PIECES,))],
        1 << 20, results[0], first, second, third,
    )
    return (
        grad_q.reshape(q_pre.shape), grad_k.reshape(k_pre.shape), grad_v.reshape(values.shape), total[0], total[1],
    )


def solution(mesh):
    tokens = P("dp", "seq", None, None)
    spans, parts = mesh.shape["dp"], mesh.shape["seq"]
    body = by_heads if (spans, parts) == (8, 4) else by_tokens
    return jax.shard_map(
        functools.partial(body, spans, parts),
        mesh=mesh,
        in_specs=(tokens, tokens, tokens, tokens, P("dp", "seq"), P(), P()),
        out_specs=(tokens, tokens, tokens, P(), P()),
        check_vma=False,
    )
```
